32 devices in a mesh: feat: 4 (over x, core), rows: 8 (over z, y).
Axes of the slice: x: 2, y: 2, z: 4, core: 2. Of those that a mesh axis runs over, the one named last changes fastest.
Arguments:
- features: bfloat16 [16, 2, 1024, 100], P('rows', None, None, 'feat'), may hold values from -6 to 6
- feature_masks: int32 [16, 100], P(None, 'feat'), may hold values from 0 to 1, as said below
- table_map: int32 [16], P('rows'), may hold values from 0 to 15, each once
- owners: int32 [24], replicated, may hold values from 0 to 7, as said below
- out_grad: bfloat16 [16, 2, 1024, 512], P('rows', None, 'feat'), may hold values from -6 to 6
- weight_slots: float32 [32, 256, 512], P('rows')
- moment1_slots: float32 [32, 256, 512], P('rows')
- moment2_slots: float32 [32, 256, 512], P('rows')
- emb_weight: float32 [100, 512], P('feat'), may hold values from -0.625 to 0.625
- emb_moment1: float32 [100, 512], P('feat')
- emb_moment2: float32 [100, 512], P('feat')
- small_weight: float32 [10, 512], replicated
- small_moment1: float32 [10, 512], replicated
- small_moment2: float32 [10, 512], replicated
Outputs:
- layer_out: bfloat16 [16, 2, 1024, 512], P('rows', None, 'feat')
- grad_inputs: bfloat16 [16, 2, 1024, 100], P('rows', None, None, 'feat')
- grad_slots: float32 [32, 256, 512], P('rows')
- moment1_out: float32 [32, 256, 512], P('rows')
- moment2_out: float32 [32, 256, 512], P('rows')
- weight_out: float32 [32, 256, 512], P('rows')
- weight_copies: bfloat16 [32, 256, 512], P('rows')
- emb_grad: float32 [100, 512], P('feat')
- emb_moment1_out: float32 [100, 512], P('feat')
- emb_moment2_out: float32 [100, 512], P('feat')
- emb_weight_out: float32 [100, 512], P('feat')
- emb_copy: bfloat16 [100, 512], P('feat')
- small_grad: float32 [10, 512], replicated
- small_moment1_out: float32 [10, 512], replicated
- small_moment2_out: float32 [10, 512], replicated
- small_weight_out: float32 [10, 512], replicated
The draws below stay inside these ranges and needn't reach their ends.
Inputs may be any that keep to these rules, and one draw needn't show every extreme that they name: `feature_masks`: each row is 1 on the first k features and 0 on the rest, k from 2 to 100; some table has all 100. `table_map`: A permutation of the table numbers. `owners`: no index owns more than 4 blocks, and some own exactly 4.
All inputs are finite; a program needn't handle non-finite values.
Results may differ from the reference program's by a relative error of at most 0.015.
Values may be sent and summed in bfloat16 or wider, within the bound.
A program may use at most 192 MiB of HBM per device.

```python
import math
import jax
import jax.numpy as jnp
from jax import lax

D = 512
HEADS = 4
HEAD_DIM = 128
FF = 2048
F = 100
HALF = 1024
NMAT = 12
CAP = 4
SMALL = 10
STEP = 10
BLOCKS = 2
UNITS = 24
TABLES = 16
SLOTS = 32
TOKENS = 32768


def owner_list(key):
    scores = jax.random.permutation(jax.random.fold_in(key, 101), SLOTS).astype(jnp.int32)
    chosen = jax.random.randint(jax.random.fold_in(key, 102), (), 0, SLOTS // CAP)
    slot_iota = jnp.arange(SLOTS, dtype=jnp.int32)
    scores = jnp.where(slot_iota // CAP == chosen, scores - SLOTS, scores)
    order = jnp.argsort(scores, stable=True).astype(jnp.int32)
    taken = order[:UNITS] // CAP
    shuffle = jax.random.permutation(jax.random.fold_in(key, 103), UNITS).astype(jnp.int32)
    return taken[shuffle].astype(jnp.int32)


def slot_matrix(key):
    owners = owner_list(key)
    positions = jnp.arange(UNITS, dtype=jnp.int32)
    same_owner = owners[:, None] == owners[None, :]
    earlier = positions[None, :] < positions[:, None]
    owner_rank = jnp.sum((same_owner & earlier).astype(jnp.int32), axis=1)
    slot_ids = owners * CAP + owner_rank
    hits = (slot_ids[None, :] == jnp.arange(SLOTS, dtype=jnp.int32)[:, None]).astype(jnp.int32)
    which = jnp.sum(hits * (positions[None, :] + 1), axis=1)
    return jnp.where(which > 0, (which - 1) // BLOCKS + 1, 0)


def signed_draw(key, shape, scale):
    return scale * jax.random.normal(key, shape, jnp.float32)


def positive_draw(key, shape, lowest):
    return lowest * jnp.exp(jax.random.uniform(key, shape, jnp.float32, 0.0, math.log(4.0)))


def matrix_grad():
    return 0.4 * math.sqrt(TOKENS)


def draw_owners(key, part):
    shared = owner_list(key)
    return shared


def draw_feature_masks(key, part):
    key = jax.random.fold_in(key, 11)
    counts = jax.random.randint(key, (TABLES,), 2, F + 1)
    chosen = jax.random.randint(jax.random.fold_in(key, 1), (), 0, TABLES)
    counts = jnp.where(jnp.arange(TABLES) == chosen, F, counts)
    return (jnp.arange(F)[None, :] < counts[:, None]).astype(jnp.int32)


def draw_weight_slots(key, part):
    which = slot_matrix(key)
    key = jax.random.fold_in(key, 21)
    factors = jnp.array([1.0, 1.3, 1.3, 1.0, 6.0, 1.0, 1.0, 1.0, 1.0, 0.5, 0.5, 0.5, 0.5], jnp.float32)
    scales = factors[which] / math.sqrt(D)
    base = jax.random.normal(key, (SLOTS, D // BLOCKS, D), jnp.float32)
    return base * scales[:, None, None]


def draw_moment1_slots(key, part):
    key = jax.random.fold_in(key, 22)
    return signed_draw(key, (SLOTS, D // BLOCKS, D), 0.111 * matrix_grad())


def draw_moment2_slots(key, part):
    key = jax.random.fold_in(key, 23)
    return positive_draw(key, (SLOTS, D // BLOCKS, D), 0.001 * matrix_grad() ** 2)


def draw_emb_moment1(key, part):
    key = jax.random.fold_in(key, 31)
    return signed_draw(key, (F, D), 0.111 * 0.7 * math.sqrt(TOKENS))


def draw_emb_moment2(key, part):
    key = jax.random.fold_in(key, 32)
    return positive_draw(key, (F, D), 0.001 * 0.49 * TOKENS)


def draw_small_weight(key, part):
    key = jax.random.fold_in(key, 41)
    base = jax.random.normal(key, (SMALL, D), jnp.float32)
    rows_index = jnp.arange(SMALL)[:, None]
    gains = (rows_index == 1) | (rows_index == 3)
    return jnp.where(gains, 1.0 + 0.15 * base, 0.3 * base)


def draw_small_moment1(key, part):
    key = jax.random.fold_in(key, 42)
    return signed_draw(key, (SMALL, D), 0.111 * math.sqrt(TOKENS))


def draw_small_moment2(key, part):
    key = jax.random.fold_in(key, 43)
    return positive_draw(key, (SMALL, D), 0.001 * TOKENS)


def steps_of(stream_key, dims, cuts, least, top_value):
    def one(dim, shards_of):
        draws = jax.random.uniform(jax.random.fold_in(jax.random.fold_in(stream_key, 6), dim), (shards_of,), jnp.float32, least / len(cuts), top_value / len(cuts))
        return jnp.repeat(jnp.exp(draws), dims[dim] // shards_of).reshape((-1,) + (1,) * (len(dims) - dim - 1))

    factor_of = one(*cuts[0])
    for cut in cuts[1:]:
        factor_of = factor_of * one(*cut)
    return factor_of


def scatter_about(stream_key, extent, deviation, limit, cuts=(), kind=jnp.bfloat16):
    values = jax.random.normal(stream_key, extent, jnp.float32) * deviation
    if len(cuts) > 0:
        values = steps_of(stream_key, extent, cuts, -0.22, 0.18) * values
    return jnp.clip(values, min=-limit, max=limit).astype(kind)


def setup_inputs(seed: int = 0) -> dict:
    key_of = jax.random.split(jax.random.key(seed), 15)
    features = scatter_about(key_of[0], (TABLES, 2, HALF, F), 1.0, 6.0, ((0, 8), (3, 4)))
    feature_masks = draw_feature_masks(jax.random.fold_in(key_of[14], 71), 0)
    table_map = jax.random.permutation(key_of[2], TABLES).astype(jnp.int32)
    owners = draw_owners(jax.random.fold_in(key_of[14], 71), 0)
    out_grad = scatter_about(key_of[4], (TABLES, 2, HALF, D), 1.0, 6.0, ((0, 8), (2, 4)))
    weight_slots = draw_weight_slots(jax.random.fold_in(key_of[14], 71), 0)
    moment1_slots = draw_moment1_slots(jax.random.fold_in(key_of[14], 71), 0)
    moment2_slots = draw_moment2_slots(jax.random.fold_in(key_of[14], 71), 0)
    emb_weight = scatter_about(key_of[8], (F, D), F ** -0.5, 0.625, ((0, 4),), jnp.float32)
    emb_moment1 = draw_emb_moment1(jax.random.fold_in(key_of[14], 71), 0)
    emb_moment2 = draw_emb_moment2(jax.random.fold_in(key_of[14], 71), 0)
    small_weight = draw_small_weight(jax.random.fold_in(key_of[14], 71), 0)
    small_moment1 = draw_small_moment1(jax.random.fold_in(key_of[14], 71), 0)
    small_moment2 = draw_small_moment2(jax.random.fold_in(key_of[14], 71), 0)
    return dict(features=features, feature_masks=feature_masks, table_map=table_map, owners=owners, out_grad=out_grad, weight_slots=weight_slots, moment1_slots=moment1_slots, moment2_slots=moment2_slots, emb_weight=emb_weight, emb_moment1=emb_moment1, emb_moment2=emb_moment2, small_weight=small_weight, small_moment1=small_moment1, small_moment2=small_moment2)


@jax.custom_vjp
def low(v):
    return lax.optimization_barrier(v.astype(jnp.bfloat16)).astype(jnp.float32)

@jax.custom_vjp
def low_back(v):
    return v

def low_keep(v):
    return (low(v), None)

def low_pass(kept, grad):
    return (grad,)

def back_keep(v):
    return (v, None)

def back_low(kept, grad):
    return (low(grad),)
low.defvjp(low_keep, low_pass)
low_back.defvjp(back_keep, back_low)
HIGH = lax.Precision.HIGHEST
LN_EPS = 1e-05
BETA_FIRST = 0.9
BETA_SECOND = 0.999
ADAM_EPS = 1e-08
DECAY = 0.01
RATE_MATRIX = 0.1
RATE_EMBED = 0.3
RATE_SMALL = 0.6

def copy_low(values):
    return lax.optimization_barrier(values.astype(jnp.bfloat16)).astype(jnp.float32)

def layer_norm(values, gain, shift):
    center = values - lax.optimization_barrier(jnp.mean(values, axis=-1, keepdims=True))
    spread = lax.optimization_barrier(jnp.mean(center * center, axis=-1, keepdims=True))
    return center * lax.rsqrt(spread + LN_EPS) * gain + shift

def matmul(left, right):
    return jnp.dot(left, right, precision=HIGH)

def adamw(weight, grad, first, second, rate):
    first_new = BETA_FIRST * first + (1.0 - BETA_FIRST) * grad
    second_new = BETA_SECOND * second + (1.0 - BETA_SECOND) * grad * grad
    first_hat = first_new / (1.0 - BETA_FIRST ** STEP)
    second_hat = second_new / (1.0 - BETA_SECOND ** STEP)
    weight_new = weight - rate * (first_hat / (jnp.sqrt(second_hat) + ADAM_EPS) + DECAY * weight)
    return (first_new, second_new, weight_new)

def table_forward(params, rows_in, mask_row):
    matrices, emb_w, small = params
    flat = (rows_in * mask_row[None, None, :]).reshape(2 * HALF, F)
    hidden0 = low_back(matmul(flat, emb_w)) + small[0]
    act1 = low(layer_norm(hidden0, small[1], small[2]))
    query = low_back(low(matmul(act1, matrices[0])))
    support = act1[:HALF]
    keys = low_back(low(matmul(support, matrices[1])))
    values = low_back(low(matmul(support, matrices[2])))
    q_heads = query.reshape(2 * HALF, HEADS, HEAD_DIM)
    k_heads = keys.reshape(HALF, HEADS, HEAD_DIM)
    v_heads = values.reshape(HALF, HEADS, HEAD_DIM)
    scores = jnp.einsum('qhd,khd->hqk', q_heads, k_heads, precision=HIGH) * HEAD_DIM ** (-0.5)
    scores = low_back(scores)
    probs = low(jax.nn.softmax(scores, axis=-1))
    mixed = jnp.einsum('hqk,khd->qhd', probs, v_heads, precision=HIGH).reshape(2 * HALF, D)
    mixed = low_back(low(mixed))
    resid1 = hidden0 + low_back(matmul(mixed, matrices[3]))
    act2 = low(layer_norm(resid1, small[3], small[4]))
    w_up = matrices[4:8].transpose(1, 0, 2).reshape(D, FF)
    w_down = matrices[8:12].reshape(FF, D)
    pre_gelu = low_back(matmul(act2, w_up) + small[6:10].reshape(FF))
    gelu_out = low(jax.nn.gelu(pre_gelu, approximate=False))
    result = resid1 + low_back(matmul(gelu_out, w_down)) + small[5]
    return result.reshape(2, HALF, D)

def reference(features, feature_masks, table_map, owners, out_grad, weight_slots, moment1_slots, moment2_slots, emb_weight, emb_moment1, emb_moment2, small_weight, small_moment1, small_moment2):
    unit_count = owners.shape[0]
    block_rows = weight_slots.shape[1]
    positions = jnp.arange(unit_count, dtype=jnp.int32)
    same_owner = owners[:, None] == owners[None, :]
    earlier = positions[None, :] < positions[:, None]
    owner_rank = lax.optimization_barrier(jnp.sum((same_owner & earlier).astype(jnp.int32), axis=1))
    slot_ids = (owners * CAP + owner_rank).astype(jnp.int32)
    master_blocks = weight_slots[slot_ids]
    masters = master_blocks.reshape(NMAT, D, D)
    params = (copy_low(masters), copy_low(emb_weight), small_weight)
    mask_rows = feature_masks.astype(jnp.float32)[table_map]

    def one_table(total, position):
        rows_in = features[position].astype(jnp.float32)
        mask_row = mask_rows[position]

        def forward(weights, inputs):
            return table_forward(weights, inputs, mask_row)
        result, pull = jax.vjp(forward, params, rows_in)
        grads, grad_in = pull(out_grad[position].astype(jnp.float32))
        total = jax.tree.map(jnp.add, total, grads)
        return (total, (result.astype(jnp.bfloat16), grad_in.astype(jnp.bfloat16)))
    zeros = jax.tree.map(jnp.zeros_like, params)
    total, (layer_out, grad_inputs) = lax.scan(one_table, zeros, jnp.arange(TABLES, dtype=jnp.int32))
    matrix_grads, emb_grad, small_grad = total
    block_grads = matrix_grads.reshape(unit_count, block_rows, D)
    first, second, weight_new = adamw(master_blocks, block_grads, moment1_slots[slot_ids], moment2_slots[slot_ids], RATE_MATRIX)
    emb_first, emb_second, emb_new = adamw(emb_weight, emb_grad, emb_moment1, emb_moment2, RATE_EMBED)
    small_first, small_second, small_new = adamw(small_weight, small_grad, small_moment1, small_moment2, RATE_SMALL)

    def place(values):
        return jnp.zeros((SLOTS, block_rows, D), values.dtype).at[slot_ids].set(values)
    weight_out = place(weight_new)
    return (layer_out, grad_inputs, place(block_grads), place(first), place(second), weight_out, weight_out.astype(jnp.bfloat16), emb_grad, emb_first, emb_second, emb_new, emb_new.astype(jnp.bfloat16), small_grad, small_first, small_second, small_new)
```

```python
import functools
import jax
import jax.numpy as jnp
from jax import lax
from jax.sharding import PartitionSpec as P
from jax.experimental import pallas as pl
from jax.experimental.pallas import tpu as pltpu

MESH = pl.DeviceIdType.MESH

def gather_kernel(R, slots_ref, G_ref, own, lsem, hs, hr, xs, xr, cs, cr, c2s, c2r):
    f = lax.axis_index("feat")
    r = lax.axis_index("rows")
    x = f // 2
    c = f % 2
    n = R.bit_length() - 1
    S, BR, W = own.shape
    BH, CH = BR // 2, W // 2
    core_id = (f ^ 1, r)
    x_id = (f ^ 2, r)
    row_id = [(f, r ^ (1 << (n - 1 - j))) for j in range(n)]
    bar = pltpu.get_barrier_semaphore()
    peers = [core_id, x_id] + row_id
    for d in peers:
        pl.semaphore_signal(bar, inc=1, device_id=d, device_id_type=MESH)
    own[...] = slots_ref[...].astype(jnp.bfloat16)
    pl.semaphore_wait(bar, len(peers))
    local = pltpu.make_async_copy(own, G_ref.at[0], lsem)
    local.start()
    subs = [(j, g) for j in range(n) for g in range(-1, j)]
    index = {jg: i for i, jg in enumerate(subs)}

    def span(g):
        return (0, 1) if g < 0 else (1 << g, 1 << g)

    def region(s, half_row, half_col):
        rows = pl.ds(pl.multiple_of(half_row * BH, BH), BH)
        cols = pl.ds(0, W) if s == 0 else pl.ds(pl.multiple_of(half_col * CH, CH), CH)
        return rows, cols

    def hyper(s, j, g):
        rows, cols = region(s, c, x)
        start, size = span(g)
        src = own.at[pl.ds(s, 1), rows, cols] if g < 0 else G_ref.at[pl.ds(start, size), s, rows, cols]
        k = index[(j, g)]
        return pltpu.make_async_remote_copy(
            src_ref=src,
            dst_ref=G_ref.at[pl.ds((1 << j) + start, size), s, rows, cols],
            send_sem=hs.at[s, k], recv_sem=hr.at[s, k], device_id=row_id[j], device_id_type=MESH)

    def forward(s, j, g, half_col, sems, semr, dev):
        rows, cols = region(s, c, half_col)
        start, size = span(g)
        k = index[(j, g)]
        ref = G_ref.at[pl.ds((1 << j) + start, size), s, rows, cols]
        return pltpu.make_async_remote_copy(src_ref=ref, dst_ref=ref, send_sem=sems.at[s, k], recv_sem=semr.at[s, k], device_id=dev, device_id_type=MESH)

    order = [1, 2, 3, 0]
    for s in order:
        for j in range(n):
            hyper(s, j, -1).start()
    def x_arrive(j):
        for s in order:
            if s == 0:
                continue
            for g in range(-1, j):
                forward(s, j, g, x, xs, xr, x_id).wait_recv()
                forward(s, j, g, 1 - x, c2s, c2r, core_id).start()
    for j in range(n):
        for s in order:
            for g in range(-1, j):
                hyper(s, j, g).wait_recv()
                if s > 0:
                    forward(s, j, g, x, xs, xr, x_id).start()
                forward(s, j, g, x, cs, cr, core_id).start()
            for j2 in range(j + 1, n):
                hyper(s, j2, j).start()
        if j > 0:
            x_arrive(j - 1)
    x_arrive(n - 1)
    local.wait()
    for s in order:
        for (j, g) in subs:
            hyper(s, j, g).wait_send()
            forward(s, j, g, x, cs, cr, core_id).wait()
            if s > 0:
                forward(s, j, g, x, xs, xr, x_id).wait_send()
                forward(s, j, g, 1 - x, c2s, c2r, core_id).wait()

def gather_weights(R, slots):
    S, BR, W = slots.shape
    n = R.bit_length() - 1
    M = n * (n + 1) // 2
    sem = pltpu.SemaphoreType.DMA((S, M))
    return pl.pallas_call(
        functools.partial(gather_kernel, R),
        out_shape=jax.ShapeDtypeStruct((R, S, BR, W), jnp.bfloat16),
        in_specs=[pl.BlockSpec(memory_space=pltpu.VMEM)],
        out_specs=pl.BlockSpec(memory_space=pl.ANY),
        scratch_shapes=[pltpu.VMEM((S, BR, W), jnp.bfloat16), pltpu.SemaphoreType.DMA] + [sem] * 8,
        compiler_params=pltpu.CompilerParams(collective_id=0, has_side_effects=True, vmem_limit_bytes=56 * 2**20),
        name="gather_weights",
    )(slots)

HEADS = 4
HEAD_DIM = 128
STEP = 10


HIGH = lax.Precision.HIGHEST
LN_EPS = 1e-05
BETA_FIRST = 0.9
BETA_SECOND = 0.999
ADAM_EPS = 1e-08
DECAY = 0.01
RATE_MATRIX = 0.1
RATE_EMBED = 0.3
RATE_SMALL = 0.6


def layer_norm(values, gain, shift):
    center = values - jnp.mean(values, axis=-1, keepdims=True)
    spread = jnp.mean(center * center, axis=-1, keepdims=True)
    return center * lax.rsqrt(spread + LN_EPS) * gain + shift


def exact_gelu(values):
    return jax.nn.gelu(values, approximate=False)


def adamw(weight, grad, first, second, rate):
    first_new = BETA_FIRST * first + (1.0 - BETA_FIRST) * grad
    second_new = BETA_SECOND * second + (1.0 - BETA_SECOND) * grad * grad
    first_hat = first_new / (1.0 - BETA_FIRST**STEP)
    second_hat = second_new / (1.0 - BETA_SECOND**STEP)
    weight_new = weight - rate * (first_hat / (jnp.sqrt(second_hat) + ADAM_EPS) + DECAY * weight)
    return (first_new, second_new, weight_new)


def split_heads(matrix):
    return matrix.reshape(matrix.shape[0], HEADS, HEAD_DIM)


def attend_forward(operands):
    query, keys, values = operands
    scale = HEAD_DIM ** (-0.5)
    scores = (
        jnp.einsum(
            "qhd,khd->hqk",
            split_heads(query),
            split_heads(keys),
            preferred_element_type=jnp.float32,
        )
        * scale
    )
    highest = jnp.max(scores, axis=-1, keepdims=True)
    weights = jnp.exp(scores - highest)
    totals = jnp.sum(weights, axis=-1, keepdims=True)
    probs = (weights / totals).astype(jnp.bfloat16)
    mixed = jnp.einsum(
        "hqk,khd->qhd", probs, split_heads(values), preferred_element_type=jnp.float32
    )
    return (
        mixed.reshape(query.shape[0], -1).astype(jnp.bfloat16),
        (highest + jnp.log(totals))[..., 0],
    )


def attend_backward(operands):
    query, keys, values, grad_mixed, log_totals = operands
    scale = HEAD_DIM ** (-0.5)
    q_heads = split_heads(query)
    k_heads = split_heads(keys)
    g_heads = split_heads(grad_mixed)
    scores = (
        jnp.einsum("qhd,khd->hqk", q_heads, k_heads, preferred_element_type=jnp.float32) * scale
    )
    probs = jnp.exp(scores - log_totals[..., None])
    grad_probs = jnp.einsum(
        "qhd,khd->hqk", g_heads, split_heads(values), preferred_element_type=jnp.float32
    )
    inner = jnp.sum(probs * grad_probs, axis=-1, keepdims=True)
    grad_scores = (probs * (grad_probs - inner)).astype(jnp.bfloat16)
    grad_query = (
        jnp.einsum("hqk,khd->qhd", grad_scores, k_heads, preferred_element_type=jnp.float32) * scale
    )
    grad_keys = (
        jnp.einsum("hqk,qhd->khd", grad_scores, q_heads, preferred_element_type=jnp.float32) * scale
    )
    grad_values = jnp.einsum(
        "hqk,qhd->khd", probs.astype(jnp.bfloat16), g_heads, preferred_element_type=jnp.float32
    )
    return (
        grad_query.reshape(query.shape[0], -1).astype(jnp.bfloat16),
        grad_keys.reshape(keys.shape[0], -1),
        grad_values.reshape(keys.shape[0], -1),
    )


def body(
    features,
    feature_masks,
    table_map,
    owners,
    out_grad,
    weight_slots,
    moment1_slots,
    moment2_slots,
    emb_weight,
    emb_moment1,
    emb_moment2,
    small_weight,
    small_moment1,
    small_moment2,
):
    unit_count = owners.shape[0]
    capacity = weight_slots.shape[0]
    block_rows = weight_slots.shape[1]
    width = weight_slots.shape[2]
    my_row = lax.axis_index("rows")
    same_owner = owners[:, None] == owners[None, :]
    earlier = lax.broadcasted_iota(jnp.int32, (unit_count, unit_count), 1) < lax.broadcasted_iota(
        jnp.int32, (unit_count, unit_count), 0
    )
    owner_rank = jnp.sum((same_owner & earlier).astype(jnp.int32), axis=1)
    slot_iota = lax.broadcasted_iota(jnp.int32, (capacity, unit_count), 0)
    selector = ((owners[None, :] == my_row) & (owner_rank[None, :] == slot_iota)).astype(
        jnp.float32
    )
    row_count = lax.axis_size("rows")
    piece = gather_weights(row_count, weight_slots)
    distance = owners ^ my_row
    place = jnp.zeros_like(distance)
    bits = row_count.bit_length() - 1
    for bit in range(bits):
        place = place | (((distance >> bit) & 1) << (bits - 1 - bit))
    flat_ids = place * capacity + owner_rank
    pieces = piece.reshape(row_count * capacity, block_rows, width)
    matrices = jnp.take(pieces, flat_ids, axis=0).reshape(-1, width, width)
    w_query = matrices[0]
    w_key = matrices[1]
    w_value = matrices[2]
    w_out = matrices[3]
    w_up = matrices[4:8].transpose(1, 0, 2).reshape(width, 4 * width)
    w_down = matrices[8:12].reshape(4 * width, width)
    local_tables = features.shape[0]
    table_iota = lax.broadcasted_iota(jnp.int32, (local_tables, feature_masks.shape[0]), 1)
    picker = (table_map[:, None] == table_iota).astype(jnp.float32)
    mask_local = jnp.dot(picker, feature_masks.astype(jnp.float32), precision=HIGH)
    masked = features * mask_local[:, None, None, :].astype(jnp.bfloat16)
    emb_low = emb_weight.astype(jnp.bfloat16)
    rows_features = lax.all_to_all(masked, "feat", split_axis=2, concat_axis=3, tiled=True)
    emb_whole = lax.all_gather(emb_low, "feat", axis=0, tiled=True)
    hidden0 = (
        jnp.einsum("tshf,fd->tshd", rows_features, emb_whole, preferred_element_type=jnp.float32)
        + small_weight[0]
    )
    row_shape = hidden0.shape
    quarter_rows = row_shape[2]
    rows_total = row_shape[0] * row_shape[1] * row_shape[2]
    flat0 = hidden0.reshape(rows_total, width)
    normed1, norm1_pull = jax.vjp(layer_norm, flat0, small_weight[1], small_weight[2])
    act1 = normed1.astype(jnp.bfloat16)
    query = jnp.dot(act1, w_query, preferred_element_type=jnp.float32).astype(jnp.bfloat16)
    support = act1.reshape(local_tables, 2, quarter_rows, width)[:, 0]
    keys_local = jnp.einsum(
        "tjd,de->tje", support, w_key, preferred_element_type=jnp.float32
    ).astype(jnp.bfloat16)
    values_local = jnp.einsum(
        "tjd,de->tje", support, w_value, preferred_element_type=jnp.float32
    ).astype(jnp.bfloat16)
    keys_all, values_all = (
        lax.all_gather(keys_local, "feat", axis=1, tiled=True),
        lax.all_gather(values_local, "feat", axis=1, tiled=True),
    )
    query_tables = query.reshape(local_tables, 2 * quarter_rows, width)
    mixed, log_totals = lax.map(attend_forward, (query_tables, keys_all, values_all))
    mixed_flat = mixed.reshape(rows_total, width)
    resid1 = flat0 + jnp.dot(mixed_flat, w_out, preferred_element_type=jnp.float32)
    normed2, norm2_pull = jax.vjp(layer_norm, resid1, small_weight[3], small_weight[4])
    act2 = normed2.astype(jnp.bfloat16)
    pre_gelu = jnp.dot(act2, w_up, preferred_element_type=jnp.float32) + small_weight[6:10].reshape(
        4 * width
    )
    gelu_out, gelu_pull = jax.vjp(exact_gelu, pre_gelu)
    gelu_low = gelu_out.astype(jnp.bfloat16)
    layer_out = (
        resid1 + jnp.dot(gelu_low, w_down, preferred_element_type=jnp.float32) + small_weight[5]
    ).astype(jnp.bfloat16)
    grad_out = out_grad.reshape(rows_total, width)
    grad_down = jnp.einsum("rf,rd->fd", gelu_low, grad_out, preferred_element_type=jnp.float32)
    bias_down = jnp.sum(grad_out, axis=0, dtype=jnp.float32)
    grad_gelu = jnp.einsum("rd,fd->rf", grad_out, w_down, preferred_element_type=jnp.float32)
    grad_pre = gelu_pull(grad_gelu)[0].astype(jnp.bfloat16)
    grad_up = jnp.einsum("rd,rf->df", act2, grad_pre, preferred_element_type=jnp.float32)
    bias_up = jnp.sum(grad_pre, axis=0, dtype=jnp.float32)
    grad_act2 = jnp.einsum("rf,df->rd", grad_pre, w_up, preferred_element_type=jnp.float32)
    back_resid, gain2_grad, shift2_grad = norm2_pull(grad_act2)
    grad_resid1 = grad_out.astype(jnp.float32) + back_resid
    grad_branch = grad_resid1.astype(jnp.bfloat16)
    grad_wout = jnp.einsum("rd,re->de", mixed_flat, grad_branch, preferred_element_type=jnp.float32)
    grad_mixed = jnp.einsum(
        "re,de->rd", grad_branch, w_out, preferred_element_type=jnp.float32
    ).astype(jnp.bfloat16)
    grad_query, key_terms, value_terms = lax.map(
        attend_backward,
        (
            query_tables,
            keys_all,
            values_all,
            grad_mixed.reshape(local_tables, 2 * quarter_rows, width),
            log_totals,
        ),
    )
    key_sums, value_sums = (
        lax.psum_scatter(
            key_terms.astype(jnp.bfloat16), "feat", scatter_dimension=1, tiled=True
        ).astype(jnp.float32),
        lax.psum_scatter(
            value_terms.astype(jnp.bfloat16), "feat", scatter_dimension=1, tiled=True
        ).astype(jnp.float32),
    )
    grad_keys = key_sums.astype(jnp.bfloat16)
    grad_values = value_sums.astype(jnp.bfloat16)
    grad_query = grad_query.reshape(rows_total, width)
    grad_wq = jnp.einsum("rd,re->de", act1, grad_query, preferred_element_type=jnp.float32)
    grad_wk = jnp.einsum("tjd,tje->de", support, grad_keys, preferred_element_type=jnp.float32)
    grad_wv = jnp.einsum("tjd,tje->de", support, grad_values, preferred_element_type=jnp.float32)
    grad_act1 = jnp.einsum(
        "re,de->rd", grad_query, w_query, preferred_element_type=jnp.float32
    ).reshape(local_tables, 2, quarter_rows, width)
    support_back = jnp.einsum(
        "tje,de->tjd", grad_keys, w_key, preferred_element_type=jnp.float32
    ) + jnp.einsum("tje,de->tjd", grad_values, w_value, preferred_element_type=jnp.float32)
    grad_act1 = grad_act1.at[:, 0].add(support_back)
    back_hidden, gain1_grad, shift1_grad = norm1_pull(grad_act1.reshape(rows_total, width))
    grad_hidden = grad_resid1 + back_hidden
    bias_embed = jnp.sum(grad_hidden, axis=0)
    grad_embed = grad_hidden.astype(jnp.bfloat16).reshape(row_shape)
    whole_terms = jnp.einsum(
        "tshf,tshd->fd", rows_features, grad_embed, preferred_element_type=jnp.float32
    )
    emb_terms = lax.psum_scatter(
        whole_terms.astype(jnp.bfloat16), "feat", scatter_dimension=0, tiled=True
    ).astype(jnp.float32)
    row_inputs = jnp.einsum(
        "tshd,fd->tshf", grad_embed, emb_whole, preferred_element_type=jnp.float32
    ).astype(jnp.bfloat16)
    returned = lax.all_to_all(row_inputs, "feat", split_axis=3, concat_axis=2, tiled=True)
    grad_inputs = returned * mask_local[:, None, None, :].astype(jnp.bfloat16)
    grad_stack = jnp.concatenate(
        [
            jnp.stack([grad_wq, grad_wk, grad_wv, grad_wout]),
            grad_up.reshape(width, 4, width).transpose(1, 0, 2),
            grad_down.reshape(4, width, width),
        ],
        axis=0,
    )
    small_terms = jnp.concatenate(
        [
            jnp.stack([bias_embed, gain1_grad, shift1_grad, gain2_grad, shift2_grad, bias_down]),
            bias_up.reshape(4, width),
        ],
        axis=0,
    )
    layer_sum, small_grad = lax.psum((grad_stack, small_terms), ("feat", "rows"))
    embed_sum = lax.psum(emb_terms, "rows")
    unit_grads = layer_sum.reshape(unit_count, block_rows, width)
    slot_grads = jnp.einsum("ci,ixy->cxy", selector, unit_grads, precision=HIGH)
    first_slots, second_slots, weight_new = adamw(
        weight_slots, slot_grads, moment1_slots, moment2_slots, RATE_MATRIX
    )
    small_first, small_second, small_new = adamw(
        small_weight, small_grad, small_moment1, small_moment2, RATE_SMALL
    )
    occupied = jnp.sum(selector, axis=1)[:, None, None]
    weight_new = weight_new * occupied
    emb_first, emb_second, emb_new = adamw(
        emb_weight, embed_sum, emb_moment1, emb_moment2, RATE_EMBED
    )
    return (
        layer_out.reshape(row_shape),
        grad_inputs,
        slot_grads * occupied,
        first_slots * occupied,
        second_slots * occupied,
        weight_new,
        weight_new.astype(jnp.bfloat16),
        embed_sum,
        emb_first,
        emb_second,
        emb_new,
        emb_new.astype(jnp.bfloat16),
        small_grad,
        small_first,
        small_second,
        small_new,
    )


def solution(mesh):
    in_specs = (
        P("rows", None, None, "feat"),
        P(None, "feat"),
        P("rows"),
        P(),
        P("rows", None, "feat", None),
        P("rows", None, None),
        P("rows", None, None),
        P("rows", None, None),
        P("feat", None),
        P("feat", None),
        P("feat", None),
        P(),
        P(),
        P(),
    )
    out_specs = (
        P("rows", None, "feat", None),
        P("rows", None, None, "feat"),
        P("rows", None, None),
        P("rows", None, None),
        P("rows", None, None),
        P("rows", None, None),
        P("rows", None, None),
        P("feat", None),
        P("feat", None),
        P("feat", None),
        P("feat", None),
        P("feat", None),
        P(),
        P(),
        P(),
        P(),
    )
    return jax.shard_map(body, mesh=mesh, in_specs=in_specs, out_specs=out_specs, check_vma=False)
```

```python
import functools
import math

import jax
import jax.numpy as jnp
from jax import lax
from jax.experimental import pallas as pl
from jax.experimental.pallas import tpu as pltpu
from jax.sharding import PartitionSpec as P

MESH = pl.DeviceIdType.MESH
bf16, f32 = jnp.bfloat16, jnp.float32
NN = (((1,), (0,)), ((), ()))
NT = (((1,), (1,)), ((), ()))
TN = (((0,), (0,)), ((), ()))
LOG2E = math.log2(math.e)
HEADS = 4
HEAD_DIM = 128
STEP = 10
LN_EPS = 1e-05
BETA_FIRST = 0.9
BETA_SECOND = 0.999
ADAM_EPS = 1e-08
DECAY = 0.01
RATE_MATRIX = 0.1
RATE_EMBED = 0.3
RATE_SMALL = 0.6
D = 512
HALF = 1024
QUART = 256
PADF = 32
VMEM_BYTES = 60 * 2**20


def dot(a, b, dims=NN):
    return lax.dot_general(a, b, dims, preferred_element_type=f32)


def vmem():
    return pl.BlockSpec(memory_space=pltpu.VMEM)


def anyspace():
    return pl.BlockSpec(memory_space=pl.ANY)


def smem():
    return pl.BlockSpec(memory_space=pltpu.SMEM)


def remote(src, dst, send, recv, dev):
    return pltpu.make_async_remote_copy(
        src_ref=src, dst_ref=dst, send_sem=send, recv_sem=recv, device_id=dev, device_id_type=MESH
    )


def greet(peers):
    bar = pltpu.get_barrier_semaphore()
    for d in peers:
        pl.semaphore_signal(bar, inc=1, device_id=d, device_id_type=MESH)
    return bar


GROUPS = ((1, 3, True), (0, 1, False))


def gather_kernel(
    R, slots_ref, feat_ref, mask_ref, tmap_ref, emb_ref, small_ref,
    G_ref, XT_ref, h0_ref, a1s_ref, a1q_ref, n1s_ref, n1q_ref, rs_ref, rq_ref,
    own, XTo, XTa, tmpq, lsem, fs, fr, hs, hr, xs, xr, cs, cr, c2s, c2r,
):
    f = lax.axis_index("feat")
    r = lax.axis_index("rows")
    x = f // 2
    c = f % 2
    n = R.bit_length() - 1
    S, BR, W = own.shape
    BH, CH = BR // 2, W // 2
    core_id = (f ^ 1, r)
    x_id = (f ^ 2, r)
    row_id = [(f, r ^ (1 << (n - 1 - j))) for j in range(n)]
    peers = [core_id, x_id] + row_id
    bar = greet(peers)
    own[...] = slots_ref[...].astype(bf16)
    pl.semaphore_wait(bar, len(peers))
    local = pltpu.make_async_copy(own, G_ref.at[0], lsem)
    local.start()
    subs = [(j, g) for j in range(n) for g in range(-1, j)]
    index = {jg: i for i, jg in enumerate(subs)}

    def span(g):
        return (0, 1) if g < 0 else (1 << g, 1 << g)

    def region(s, half_col):
        rows = pl.ds(pl.multiple_of(c * BH, BH), BH)
        cols = pl.ds(pl.multiple_of(half_col * CH, CH), CH) if GROUPS[s][2] else pl.ds(0, W)
        return pl.ds(GROUPS[s][0], GROUPS[s][1]), rows, cols

    def hyper(s, j, g):
        where = region(s, x)
        start, size = span(g)
        k = index[(j, g)]
        if g < 0:
            src, dst = own.at[where], G_ref.at[(1 << j, *where)]
        else:
            src = G_ref.at[(pl.ds(start, size), *where)]
            dst = G_ref.at[(pl.ds((1 << j) + start, size), *where)]
        return remote(src, dst, hs.at[s, k], hr.at[s, k], row_id[j])

    def forward(s, j, g, half_col, sems, semr, dev):
        start, size = span(g)
        k = index[(j, g)]
        ref = G_ref.at[(pl.ds((1 << j) + start, size), *region(s, half_col))]
        return remote(ref, ref, sems.at[s, k], semr.at[s, k], dev)

    order = range(len(GROUPS))
    for s in order:
        for j in range(n):
            hyper(s, j, -1).start()

    T = mask_ref.shape[0]
    nf = feat_ref.shape[3]
    row_iota = lax.broadcasted_iota(jnp.int32, (T, nf), 0)
    for t in range(2):
        line = jnp.sum(jnp.where(row_iota == tmap_ref[t], mask_ref[...], 0), axis=0, keepdims=True)
        diag = jnp.where(
            lax.broadcasted_iota(jnp.int32, (PADF, nf), 0) == lax.broadcasted_iota(jnp.int32, (PADF, nf), 1),
            jnp.broadcast_to(line, (PADF, nf)), 0,
        ).astype(f32).astype(bf16)
        XTo[:, pl.ds(t * HALF, HALF)] = dot(diag, feat_ref[t, 0], NT).astype(bf16)
        query = dot(diag, feat_ref[t, 1], NT).astype(bf16)
        for k in range(4):
            XTo[:, pl.ds(2 * HALF + D + k * 512 + t * QUART, QUART)] = query[:, k * QUART:(k + 1) * QUART]
    XTo[:, pl.ds(2 * HALF, D)] = jnp.zeros((PADF, D), bf16)
    XTo[pl.ds(0, nf), pl.ds(2 * HALF, D)] = emb_ref[...].astype(bf16)
    wide = 2 * HALF + D
    shared = pl.ds(0, wide)

    def rows_of(dev):
        return pl.ds(pl.multiple_of(dev * PADF, PADF), PADF)

    def chunk_of(dev):
        return pl.ds(pl.multiple_of(wide + dev * 512, 512), 512)

    tail = pl.ds(wide, 512)
    feats = [
        remote(XTo.at[:, shared], XTa.at[rows_of(f), shared], fs.at[0], fr.at[0], core_id),
        remote(XTo.at[:, chunk_of(f ^ 1)], XTa.at[rows_of(f), tail], fs.at[1], fr.at[1], core_id),
        remote(XTo.at[:, shared], XTa.at[rows_of(f), shared], fs.at[2], fr.at[2], x_id),
        remote(XTo.at[:, chunk_of(f ^ 2)], XTa.at[rows_of(f), tail], fs.at[3], fr.at[3], x_id),
        remote(XTo.at[:, chunk_of(f ^ 3)], tmpq, fs.at[4], fr.at[4], x_id),
        remote(XTa.at[rows_of(f ^ 2), shared], XTa.at[rows_of(f ^ 2), shared], fs.at[5], fr.at[5], core_id),
        remote(tmpq, XTa.at[rows_of(f ^ 2), tail], fs.at[6], fr.at[6], core_id),
    ]
    for copy in feats[:5]:
        copy.start()
    XTa[rows_of(f), shared] = XTo[:, shared]
    XTa[rows_of(f), tail] = XTo[:, chunk_of(f)]

    def x_arrive(j):
        for s in order:
            if GROUPS[s][2]:
                for g in range(-1, j):
                    forward(s, j, g, x, xs, xr, x_id).wait_recv()
                    forward(s, j, g, 1 - x, c2s, c2r, core_id).start()

    def hyper_arrive(j):
        for s in order:
            for g in range(-1, j):
                hyper(s, j, g).wait_recv()
                if GROUPS[s][2]:
                    forward(s, j, g, x, xs, xr, x_id).start()
                forward(s, j, g, x, cs, cr, core_id).start()
            for j2 in range(j + 1, n):
                hyper(s, j2, j).start()

    hyper_arrive(0)
    feats[2].wait_recv()
    feats[4].wait_recv()
    feats[5].start()
    feats[6].start()
    for j in range(1, n - 1):
        hyper_arrive(j)
        x_arrive(j - 1)
    for k in (0, 1, 3, 5, 6):
        feats[k].wait_recv()

    shift0 = small_ref[0:1]
    gain = small_ref[1:2]
    shift = small_ref[2:3]
    E = XTa[:, pl.ds(2 * HALF, D)]

    def norm(cols):
        h = dot(XTa[:, cols], E, TN) + shift0
        mean = jnp.mean(h, axis=-1, keepdims=True)
        cen = h - mean
        rstd = lax.rsqrt(jnp.mean(cen * cen, axis=-1, keepdims=True) + LN_EPS)
        nrm = cen * rstd
        return h, nrm, rstd, (nrm * gain + shift).astype(bf16)

    @pl.loop(0, 8)
    def _(i):
        rows = pl.ds(pl.multiple_of(i * QUART, QUART), QUART)
        h, nrm, rstd, act = norm(rows)
        n1s_ref[rows] = nrm.astype(bf16)
        a1s_ref[rows] = act
        rs_ref[rows] = jnp.broadcast_to(rstd, (QUART, 128))

        @pl.when(i % 4 == f)
        def _():
            h0_ref[pl.ds(pl.multiple_of((i // 4) * 512, 512), QUART)] = h

    @pl.loop(0, 2)
    def _(t):
        rows = pl.ds(pl.multiple_of(t * QUART, QUART), QUART)
        h, nrm, rstd, act = norm(pl.ds(pl.multiple_of(wide + t * QUART, QUART), QUART))
        n1q_ref[rows] = nrm.astype(bf16)
        a1q_ref[rows] = act
        rq_ref[rows] = jnp.broadcast_to(rstd, (QUART, 128))
        h0_ref[pl.ds(pl.multiple_of(t * 512 + QUART, QUART), QUART)] = h

    XT_ref[...] = XTa[...]
    hyper_arrive(n - 1)
    if n > 1:
        x_arrive(n - 2)
    x_arrive(n - 1)
    local.wait()
    for copy in feats:
        copy.wait_send()
    for s in order:
        for j, g in subs:
            hyper(s, j, g).wait_send()
            forward(s, j, g, x, cs, cr, core_id).wait()
            if GROUPS[s][2]:
                forward(s, j, g, x, xs, xr, x_id).wait_send()
                forward(s, j, g, 1 - x, c2s, c2r, core_id).wait()


def gather_call(R, slots, features, masks, tmap, emb, small):
    S, BR, W = slots.shape
    n = R.bit_length() - 1
    M = n * (n + 1) // 2
    sem = pltpu.SemaphoreType.DMA((len(GROUPS), M))
    sd = jax.ShapeDtypeStruct
    cols = 2 * HALF + D + 512
    return pl.pallas_call(
        functools.partial(gather_kernel, R),
        out_shape=(
            sd((R, S, BR, W), bf16), sd((4 * PADF, cols), bf16), sd((1024, D), f32),
            sd((2048, D), bf16), sd((512, D), bf16), sd((2048, D), bf16), sd((512, D), bf16),
            sd((2048, 128), f32), sd((512, 128), f32),
        ),
        in_specs=[vmem(), vmem(), vmem(), smem(), vmem(), vmem()],
        out_specs=(anyspace(),) + (vmem(),) * 8,
        scratch_shapes=[
            pltpu.VMEM((S, BR, W), bf16), pltpu.VMEM((PADF, 2 * HALF + D + 2048), bf16),
            pltpu.VMEM((4 * PADF, cols), bf16), pltpu.VMEM((PADF, 512), bf16),
            pltpu.SemaphoreType.DMA, pltpu.SemaphoreType.DMA((7,)), pltpu.SemaphoreType.DMA((7,)),
        ] + [sem] * 8,
        compiler_params=pltpu.CompilerParams(collective_id=0, has_side_effects=True, vmem_limit_bytes=VMEM_BYTES),
        name="gather_weights",
    )(slots, features, masks, tmap, emb, small)


def gelu_pair(u):
    t = 1.0 / (1.0 + (0.3275911 * math.sqrt(0.5)) * jnp.abs(u))
    ex = jnp.exp2((-0.5 * LOG2E) * (u * u))
    poly = t * (0.127414796 + t * (-0.142248368 + t * (0.7107068705 + t * (-0.7265760135 + t * 0.5307027145))))
    e = poly * ex
    phi = jnp.where(u >= 0, 1.0 - e, e)
    return u * phi, phi + u * ex * (1.0 / math.sqrt(2 * math.pi))


def forward_kernel(
    BR, pos, G, h0o, a1s, a1q, dY, small,
    out, gF, dy1, sg, ET, linv, OT, qo, ko, kTo, vo, Wout,
    W, q_s, k_s, kT_s, v_s, vT_s, ET_s, OT_s, O_s, a2_s, G_s, dU_s, gF_s, wsem, osem,
):
    U = W.shape[0] // BR
    R = U // 3
    f = lax.axis_index("feat")
    per = D // BR
    BH = BR // 2

    def wcopy(u):
        return pltpu.make_async_copy(G.at[pos[u]], W.at[pl.ds(u * BR, BR)], wsem.at[u])

    for u in range(U):
        wcopy(u).start()

    def wwait(i):
        for u in range(i * per, (i + 1) * per):
            wcopy(u).wait()

    def mat(i):
        return W[pl.ds(i * D, D)]

    scale = (HEAD_DIM**-0.5) * LOG2E
    outs = []

    def ship(src, dst):
        copy = pltpu.make_async_copy(src, dst, osem.at[len(outs)])
        copy.start()
        outs.append(copy)

    wwait(0)
    for t in range(2):
        sup = pl.multiple_of(t * HALF + f * QUART, QUART)
        q_s[pl.ds(t * 512, QUART)] = (dot(a1s[pl.ds(sup, QUART)], mat(0)) * scale).astype(bf16)
        q_s[pl.ds(t * 512 + QUART, QUART)] = (dot(a1q[pl.ds(t * QUART, QUART)], mat(0)) * scale).astype(bf16)
    wwait(1)
    wwait(2)

    @pl.loop(0, 4)
    def _(i):
        rows = pl.ds(pl.multiple_of(i * 512, 512), 512)
        a = a1s[rows]
        k = dot(a, mat(1)).astype(bf16)
        k_s[rows] = k
        kT_s[:, rows] = k.T
        v = dot(a, mat(2)).astype(bf16)
        v_s[rows] = v
        vT_s[:, rows] = v.T

    @pl.loop(0, 8)
    def _(i):
        t = i // HEADS
        h = i % HEADS
        ks = pl.ds(pl.multiple_of(t * HALF, HALF), HALF)
        qs = pl.ds(pl.multiple_of(t * 512, 512), 512)
        hs = pl.ds(pl.multiple_of(h * HEAD_DIM, HEAD_DIM), HEAD_DIM)
        st = dot(k_s[ks, hs], q_s[qs, hs], NT)
        top = jnp.max(st, axis=0, keepdims=True)
        e = jnp.exp2(st - top)
        inv = 1.0 / jnp.sum(e, axis=0, keepdims=True)
        eb = e.astype(bf16)
        ET_s[i] = eb
        linv[pl.ds(i, 1)] = inv
        ot = (dot(vT_s[hs, ks], eb) * inv).astype(bf16)
        OT_s[hs, qs] = ot
        O_s[qs, hs] = ot.T

    wwait(3)
    ship(q_s, qo)
    ship(k_s, ko)
    ship(kT_s, kTo)
    ship(v_s, vo)
    ship(ET_s, ET)
    ship(OT_s, OT)
    ship(W.at[pl.ds(0, 4 * D)], Wout)
    for i in range(4, 12):
        wwait(i)
    gain = small[3:4]
    shift = small[4:5]
    sg[...] = jnp.zeros_like(sg)
    RB = 256

    @pl.loop(0, 1024 // RB)
    def _(i):
        rows = pl.ds(pl.multiple_of(i * RB, RB), RB)
        y1 = h0o[rows] + dot(O_s[rows], mat(3))
        mean = jnp.mean(y1, axis=-1, keepdims=True)
        cen = y1 - mean
        rstd = lax.rsqrt(jnp.mean(cen * cen, axis=-1, keepdims=True) + LN_EPS)
        n2 = cen * rstd
        a2 = (n2 * gain + shift).astype(bf16)
        a2_s[rows] = a2
        dy = dY[rows]
        acc = y1 + small[5:6]
        da2 = jnp.zeros((RB, D), f32)
        for j in range(4):
            cols = pl.ds(j * 512, 512)
            wu = mat(4 + j)
            wd = mat(8 + j)
            u = dot(a2, wu) + small[6 + j:7 + j]
            gl, gp = gelu_pair(u)
            gb = gl.astype(bf16)
            G_s[rows, cols] = gb
            acc = acc + dot(gb, wd)
            du = (dot(dy, wd, NT) * gp).astype(bf16)
            dU_s[rows, cols] = du
            sg[6 + j:7 + j] += jnp.sum(du.astype(f32), axis=0, keepdims=True)
            da2 = da2 + dot(du, wu, NT)
        out[rows] = acc.astype(bf16)
        dyf = dy.astype(f32)
        sg[3:4] += jnp.sum(da2 * n2, axis=0, keepdims=True)
        sg[4:5] += jnp.sum(da2, axis=0, keepdims=True)
        sg[5:6] += jnp.sum(dyf, axis=0, keepdims=True)
        cc = da2 * gain
        m1 = jnp.mean(cc, axis=-1, keepdims=True)
        m2 = jnp.mean(cc * n2, axis=-1, keepdims=True)
        dy1[rows] = dyf + rstd * (cc - m1 - n2 * m2)

    def put(chunk, j, val):
        for m in range(2):
            for c in range(2):
                k = 2 * m + c
                gF_s[chunk * 2 + m, c, pl.ds(j * per, per)] = val[:, k * 128:(k + 1) * 128].reshape(per, 2, BH, 128)

    for j in range(4):
        put(1, j, dot(G_s[:, pl.ds(j * 512, 512)], dY[...], TN).astype(bf16))
    for j in range(4):
        put(0, j, dot(a2_s[...], dU_s[:, pl.ds(j * 512, 512)], TN).astype(bf16))
    ship(gF_s, gF)
    for copy in outs:
        copy.wait()


def forward_call(pos, G, h0o, a1s, a1q, dY, small):
    BR = G.shape[1]
    U = pos.shape[0]
    R = U // 3
    sd = jax.ShapeDtypeStruct
    gshape = (4, 2, R, 2, BR // 2, 128)
    V = pltpu.VMEM
    return pl.pallas_call(
        functools.partial(forward_kernel, BR),
        out_shape=(
            sd((1024, D), bf16), sd(gshape, bf16), sd((1024, D), f32), sd((16, D), f32),
            sd((8, HALF, 512), bf16), sd((8, 512), f32), sd((D, 1024), bf16), sd((1024, D), bf16),
            sd((2048, D), bf16), sd((D, 2048), bf16), sd((2048, D), bf16), sd((2048, D), bf16),
        ),
        in_specs=[smem(), anyspace()] + [vmem()] * 5,
        out_specs=(vmem(), anyspace(), vmem(), vmem(), anyspace(), vmem()) + (anyspace(),) * 6,
        scratch_shapes=[
            V((U * BR, D), bf16), V((1024, D), bf16), V((2048, D), bf16), V((D, 2048), bf16), V((2048, D), bf16),
            V((D, 2048), bf16), V((8, HALF, 512), bf16), V((D, 1024), bf16), V((1024, D), bf16), V((1024, D), bf16),
            V((1024, 2048), bf16), V((1024, 2048), bf16), V(gshape, bf16),
            pltpu.SemaphoreType.DMA((U,)), pltpu.SemaphoreType.DMA((8,)),
        ],
        compiler_params=pltpu.CompilerParams(vmem_limit_bytes=VMEM_BYTES),
        name="forward",
    )(pos, G, h0o, a1s, a1q, dY, small)


CHUNKS = ((2, 2), (0, 2), (4, 1), (5, 1))


def backward_kernel(
    R, gF, su, occ, dy1, W4, ET, linv, OT, qs, ks, kT, vs, a1s, a1q, n1s, n1q, rs, rq, XT, small, sgF,
    FIN, SM, EM, GI,
    ETb, dZ, dOT, Dp, dq, dk, dv, sg, eg, GT,
    gA, ownF, RC, S1, RX, S2, RH, AGB, SEL, PK, RK, GC, XS, XR,
    esem, osem, ss, sr, fs, fr, ps, pr, gs, gr,
):
    f = lax.axis_index("feat")
    r = lax.axis_index("rows")
    x = f // 2
    c = f % 2
    n = R.bit_length() - 1
    BH = gA.shape[4]
    per = D // (2 * BH)
    core_id = (f ^ 1, r)
    x_id = (f ^ 2, r)
    row_id = [(f, r ^ (1 << j)) for j in range(n)]
    peers = [core_id, x_id] + row_id
    bar = greet(peers)

    def ecopy(i):
        return pltpu.make_async_copy(ET.at[i], ETb.at[i], esem.at[i])

    order = [t * HEADS + h for h in range(HEADS) for t in range(2)]
    ownc = pltpu.make_async_copy(gF.at[:, c], ownF, osem)
    ownc.start()
    for i in order:
        ecopy(i).start()
    pl.semaphore_wait(bar, len(peers))

    bits = [(r >> j) & 1 for j in range(n)]
    base = [0]
    for j in range(n):
        base.append(base[j] + bits[j] * (R >> (j + 1)))

    def groups(k):
        return pl.ds(CHUNKS[k][0], CHUNKS[k][1])

    def core_copy(k):
        g0, ng = CHUNKS[k]
        src = gF.at[groups(k), 1 - c] if g0 < 4 else gA.at[pl.ds(g0 - 4, ng), 1 - c]
        return remote(src, RC.at[groups(k)], ss.at[k, 0], sr.at[k, 0], core_id)

    def x_copy(k):
        return remote(S1.at[1 - x, groups(k)], RX.at[groups(k)], ss.at[k, 1], sr.at[k, 1], x_id)

    def rs_copy(k, j):
        half = R >> (j + 1)
        away = base[j] + (1 - bits[j]) * half
        off = R - (R >> j)
        return remote(
            S2.at[groups(k), pl.ds(away, half)], RH.at[groups(k), pl.ds(off, half)],
            ss.at[k, 2 + j], sr.at[k, 2 + j], row_id[j],
        )

    def ag_copy(k, j):
        size = R >> (j + 1)
        ref = AGB.at[groups(k), pl.ds(base[j + 1], size)]
        return remote(ref, ref, ss.at[k, 2 + n + j], sr.at[k, 2 + n + j], row_id[j])

    def step(k, stage):
        g0, ng = CHUNKS[k]
        gl = range(g0, g0 + ng)
        if stage == 0:
            core_copy(k).wait_recv()
            for g in gl:
                for p in range(R):
                    for h in range(2):
                        mine = ownF[g, p, h] if g < 4 else gA[g - 4, c, p, h]
                        S1[h, g, p] = (mine.astype(f32) + RC[g, p, h].astype(f32)).astype(bf16)
            x_copy(k).start()
        elif stage == 1:
            x_copy(k).wait_recv()
            for g in gl:
                S2[g] = (S1[x, g].astype(f32) + RX[g].astype(f32)).astype(bf16)
            rs_copy(k, 0).start()
        elif stage < 2 + n:
            j = stage - 2
            half = R >> (j + 1)
            off = R - (R >> j)
            rs_copy(k, j).wait_recv()
            keep = pl.ds(base[j + 1], half)
            for g in gl:
                total = (S2[g, keep].astype(f32) + RH[g, pl.ds(off, half)].astype(f32)).astype(bf16)
                if j < n - 1:
                    S2[g, keep] = total
                else:
                    AGB[g, keep] = total
            if j < n - 1:
                rs_copy(k, j + 1).start()
            else:
                ag_copy(k, n - 1).start()
        else:
            j = 2 * n + 1 - stage
            ag_copy(k, j).wait_recv()
            if j > 0:
                ag_copy(k, j - 1).start()

    core_copy(0).start()
    core_copy(1).start()

    scale = HEAD_DIM**-0.5
    for i in range(2):
        dZ[pl.ds(i * 512, 512)] = dy1[pl.ds(i * 512, 512)].astype(bf16)

    def put(m, i, val):
        for cc in range(2):
            gA[m, cc, pl.ds(i * per, per)] = val[:, cc * 128:(cc + 1) * 128].reshape(per, 2, BH, 128)

    go = dot(OT[...], dZ[...]).astype(bf16)
    put(0, 3, go[:, :256])
    put(1, 3, go[:, 256:])
    for t in range(2):
        cols = pl.ds(t * 512, 512)
        for h in range(HEADS):
            rows = pl.ds(h * HEAD_DIM, HEAD_DIM)
            d = dot(W4[pl.ds(3 * D + h * HEAD_DIM, HEAD_DIM)], dZ[cols], NT) * linv[pl.ds(t * HEADS + h, 1)]
            Dp[pl.ds(t * HEADS + h, 1)] = jnp.sum(d * OT[rows, cols].astype(f32), axis=0, keepdims=True)
            dOT[rows, cols] = d.astype(bf16)
    ownc.wait()
    step(0, 0)
    step(1, 0)

    def heads(h):
        hs = pl.ds(h * HEAD_DIM, HEAD_DIM)
        for t in range(2):
            ecopy(t * HEADS + h).wait()

        @pl.loop(0, 2)
        def _(t):
            i = t * HEADS + h
            ksl = pl.ds(pl.multiple_of(t * HALF, HALF), HALF)
            qsl = pl.ds(pl.multiple_of(t * 512, 512), 512)
            do = dOT[hs, qsl]
            dp = dot(vs[ksl, hs], do)
            e = ETb[i]
            ds = (e.astype(f32) * (dp - Dp[pl.ds(i, 1)])).astype(bf16)
            dv[ksl, hs] = dot(e, do, NT).astype(bf16)
            dk[ksl, hs] = (dot(ds, qs[qsl, hs]) * (1.0 / LOG2E)).astype(bf16)
            dqT = (dot(kT[hs, ksl], ds) * scale).astype(bf16)
            dq[qsl, hs] = dqT.T

    def weight_grads(m):
        cols = pl.ds(m * 256, 256)
        acc = jnp.zeros((D, 256), f32)
        for t in range(2):
            sup = pl.multiple_of(t * HALF + f * QUART, QUART)
            acc += dot(a1s[pl.ds(sup, QUART)], dq[pl.ds(t * 512, QUART), cols], TN)
            acc += dot(a1q[pl.ds(t * QUART, QUART)], dq[pl.ds(t * 512 + QUART, QUART), cols], TN)
        put(m, 0, acc.astype(bf16))
        put(m, 1, dot(a1s[...], dk[:, cols], TN).astype(bf16))
        put(m, 2, dot(a1s[...], dv[:, cols], TN).astype(bf16))

    heads(0)
    heads(1)
    weight_grads(0)
    core_copy(2).start()
    heads(2)
    step(2, 0)
    step(0, 1)
    heads(3)
    weight_grads(1)
    core_copy(3).start()
    step(0, 2)

    sg[...] = sgF[...]
    eg[...] = jnp.zeros_like(eg)
    gain = small[1:2]
    emb_cols = pl.ds(2 * HALF, D)

    def back(da, nrm, rstd, extra, cols, out_cols):
        sg[1:2] += jnp.sum(da * nrm, axis=0, keepdims=True)
        sg[2:3] += jnp.sum(da, axis=0, keepdims=True)
        cc = da * gain
        m1 = jnp.mean(cc, axis=-1, keepdims=True)
        m2 = jnp.mean(cc * nrm, axis=-1, keepdims=True)
        wide = jnp.concatenate([rstd] * 4, axis=1)
        dh = wide * (cc - m1 - nrm * m2)
        if extra is not None:
            dh = dh + extra
        sg[0:1] += jnp.sum(dh, axis=0, keepdims=True)
        de = dh.astype(bf16)
        part = dot(XT[:, cols], de)
        back_in = dot(XT[:, emb_cols], de, NT).astype(bf16)
        for k in range(4):
            eg[k] += part[k * PADF:(k + 1) * PADF]
            GT[k % 2, k // 2, :, out_cols] = back_in[k * PADF:(k + 1) * PADF]

    def below(t):
        q0 = t * 512
        wq, wk, wv = W4[pl.ds(0, D)], W4[pl.ds(D, D)], W4[pl.ds(2 * D, D)]
        da = dot(dq[pl.ds(q0 + QUART, QUART)], wq, NT)
        p0 = pl.ds(t * QUART, QUART)
        back(
            da, n1q[p0].astype(f32), rq[p0], dy1[pl.ds(q0 + QUART, QUART)],
            pl.ds(2 * HALF + D + t * QUART, QUART), pl.ds(2 * HALF + t * QUART, QUART),
        )
        for b in range(4):
            rows = pl.ds(pl.multiple_of(t * HALF + ((f + b) % 4) * QUART, QUART), QUART)
            da = dot(dk[rows], wk, NT) + dot(dv[rows], wv, NT)
            extra = None
            if b == 0:
                da = da + dot(dq[pl.ds(q0, QUART)], wq, NT)
                extra = dy1[pl.ds(q0, QUART)]
            back(da, n1s[rows].astype(f32), rs[rows], extra, rows, rows)

    below(0)
    step(3, 0)
    step(1, 1)
    step(0, 3)
    below(1)

    small_rows = pl.ds(0, 16)
    PK[0, small_rows] = sg[...]
    for k in range(2):
        PK[0, pl.ds(16 + k * PADF, PADF)] = eg[2 * k + 1 - c]
    def pk_copy(i, rows):
        dev = core_id if i == 0 else x_id if i == 1 else row_id[i - 2]
        return remote(PK.at[i, pl.ds(0, rows)], RK.at[i, pl.ds(0, rows)], ps.at[i], pr.at[i], dev)

    def pk_step(i):
        pk_copy(i, 80 if i == 0 else 48).wait_recv()
        if i == 0:
            PK[1, small_rows] = PK[0, small_rows] + RK[0, small_rows]
            own = [eg[2 * k + c] + RK[0, pl.ds(16 + k * PADF, PADF)] for k in range(2)]
            keep = jnp.where(x == 0, own[0], own[1])
            PK[1, pl.ds(16, PADF)] = jnp.where(x == 0, own[1], own[0])
            PK[1, pl.ds(48, PADF)] = keep
            pk_copy(1, 48).start()
        else:
            old = PK[1, pl.ds(48, PADF)] if i == 1 else PK[i, pl.ds(16, PADF)]
            a = PK[i, small_rows] + RK[i, small_rows]
            b = old + RK[i, pl.ds(16, PADF)]
            if i < n + 1:
                PK[i + 1, small_rows] = a
                PK[i + 1, pl.ds(16, PADF)] = b
                pk_copy(i + 1, 48).start()
            else:
                SM[...] = a
                EM[...] = b

    pk_copy(0, 80).start()
    gt1 = remote(GT.at[1 - c], GC, gs.at[0], gr.at[0], core_id)
    gt1.start()
    sup = pl.ds(0, 2 * HALF)
    que = pl.ds(2 * HALF, 512)

    def que_of(k, first=2 * HALF):
        return pl.ds(pl.multiple_of(first + k * 512, 512), 512)

    gt2 = remote(XS, XR, gs.at[1], gr.at[1], x_id)
    step(0, 4)
    step(2, 1)
    pk_step(0)
    gt1.wait_recv()
    XS[:, sup] = (GT[c, 1 - x, :, sup].astype(f32) + GC[1 - x, :, sup].astype(f32)).astype(bf16)
    XS[:, que_of(c)] = GT[c, 1 - x, :, que]
    XS[:, que_of(1 - c)] = GC[1 - x, :, que]
    gt2.start()
    step(3, 1)
    step(1, 2)
    pk_step(1)
    for st in range(3, 2 + 2 * n):
        step(1, st)
        step(2, st - 1)
        step(3, st - 1)
        if st + 2 < 2 + 2 * n:
            step(0, st + 2)
        if st - 1 < 2 + n:
            pk_step(st - 1)
    step(2, 1 + 2 * n)
    step(3, 1 + 2 * n)
    gt2.wait_recv()
    GI[:, sup] = (
        GT[c, x, :, sup].astype(f32) + GC[x, :, sup].astype(f32) + XR[:, sup].astype(f32)
    ).astype(bf16)
    GI[:, que_of(f)] = GT[c, x, :, que]
    GI[:, que_of(f ^ 1)] = GC[x, :, que]
    for k in range(2):
        GI[:, que_of(2 * (1 - x) + k)] = XR[:, que_of(k)]

    for s in range(4):
        u = su[s]
        g = lax.rem(2 * lax.div(u, R) + 4, 6)
        p = lax.rem(u, R)
        keep = occ[s]
        for m in range(2):
            SEL[s, m] = (AGB[g + m, p].astype(f32) * keep).astype(bf16)
    fin = [
        remote(SEL, FIN.at[f], fs.at[0], fr.at[0], core_id),
        remote(SEL, FIN.at[f], fs.at[1], fr.at[1], x_id),
        remote(FIN.at[f ^ 2], FIN.at[f ^ 2], fs.at[2], fr.at[2], core_id),
    ]
    mine = pltpu.make_async_copy(SEL, FIN.at[f], osem)
    fin[1].start()
    fin[0].start()
    mine.start()
    fin[1].wait_recv()
    fin[2].start()
    mine.wait()
    fin[0].wait()
    fin[1].wait_send()
    fin[2].wait()
    for k in range(4):
        core_copy(k).wait_send()
        x_copy(k).wait_send()
        for j in range(n):
            rs_copy(k, j).wait_send()
            ag_copy(k, j).wait_send()
    for i in range(n + 2):
        pk_copy(i, 80 if i == 0 else 48).wait_send()
    gt1.wait_send()
    gt2.wait_send()


def backward_call(R, gF, su, occ, dy1, W4, ET, linv, OT, q, k, kT, v, a1s, a1q, n1s, n1q, rs, rq, XT, small, sg):
    BH = gF.shape[4]
    n = R.bit_length() - 1
    sd = jax.ShapeDtypeStruct
    V = pltpu.VMEM
    dma = pltpu.SemaphoreType.DMA
    blk = (R, BH, 128)
    return pl.pallas_call(
        functools.partial(backward_kernel, R),
        out_shape=(sd((4, 4, 2, BH, 128), bf16), sd((16, D), f32), sd((PADF, D), f32), sd((PADF, 4096), bf16)),
        in_specs=[anyspace(), smem(), smem(), vmem(), vmem(), anyspace()] + [vmem()] * 15,
        out_specs=(anyspace(), vmem(), vmem(), vmem()),
        scratch_shapes=[
            V((8, HALF, 512), bf16), V((1024, D), bf16), V((D, 1024), bf16), V((8, 512), f32),
            V((1024, D), bf16), V((2048, D), bf16), V((2048, D), bf16), V((16, D), f32), V((4, PADF, D), f32),
            V((2, 2, PADF, 2560), bf16),
            V((2, 2, R, 2, BH, 128), bf16), V((4, R, 2, BH, 128), bf16), V((6, R, 2, BH, 128), bf16),
            V((2, 6) + blk, bf16), V((6,) + blk, bf16), V((6,) + blk, bf16), V((6,) + blk, bf16), V((6,) + blk, bf16),
            V((4, 2, BH, 128), bf16), V((n + 2, 80, D), f32), V((n + 2, 80, D), f32),
            V((2, PADF, 2560), bf16), V((PADF, 3072), bf16), V((PADF, 3072), bf16),
            dma((8,)), dma, dma((4, 2 + 2 * n)), dma((4, 2 + 2 * n)), dma((3,)), dma((3,)),
            dma((n + 2,)), dma((n + 2,)), dma((2,)), dma((2,)),
        ],
        compiler_params=pltpu.CompilerParams(collective_id=1, has_side_effects=True, vmem_limit_bytes=VMEM_BYTES),
        name="backward",
    )(gF, su, occ, dy1, W4, ET, linv, OT, q, k, kT, v, a1s, a1q, n1s, n1q, rs, rq, XT, small, sg)


def adamw(weight, grad, first, second, rate):
    first_new = BETA_FIRST * first + (1.0 - BETA_FIRST) * grad
    second_new = BETA_SECOND * second + (1.0 - BETA_SECOND) * grad * grad
    first_hat = first_new / (1.0 - BETA_FIRST**STEP)
    second_hat = second_new / (1.0 - BETA_SECOND**STEP)
    weight_new = weight - rate * (first_hat / (jnp.sqrt(second_hat) + ADAM_EPS) + DECAY * weight)
    return (first_new, second_new, weight_new)


def update_kernel(
    occ, tmap, FIN, w, m, v, SM, sw, sm, sv, EM, ew, em, ev, GI, masks,
    g_o, m_o, v_o, w_o, wc_o, eg_o, em_o, ev_o, ew_o, ec_o, sg_o, sm_o, sv_o, sw_o, gi_o,
):
    s = pl.program_id(0)
    keep = occ[s]
    BH = FIN.shape[3]
    for f in range(4):
        rows = pl.ds((f // 2) * BH, BH)
        for k in range(2):
            cols = pl.ds(k * 256 + (f % 2) * 128, 128)
            g = FIN[f, 0, k].astype(f32)
            a, b, d = adamw(w[0, rows, cols], g, m[0, rows, cols], v[0, rows, cols], RATE_MATRIX)
            g_o[0, rows, cols] = g * keep
            m_o[0, rows, cols] = a * keep
            v_o[0, rows, cols] = b * keep
            d = d * keep
            w_o[0, rows, cols] = d
            wc_o[0, rows, cols] = d.astype(bf16)

    @pl.when(s == 0)
    def _():
        g = SM[0:10]
        a, b, d = adamw(sw[...], g, sm[...], sv[...], RATE_SMALL)
        sg_o[...] = g
        sm_o[...] = a
        sv_o[...] = b
        sw_o[...] = d
        nf = ew.shape[0]
        g = EM[pl.ds(0, nf)]
        a, b, d = adamw(ew[...], g, em[...], ev[...], RATE_EMBED)
        eg_o[...] = g
        em_o[...] = a
        ev_o[...] = b
        ew_o[...] = d
        ec_o[...] = d.astype(bf16)

    nf = gi_o.shape[3]
    T = masks.shape[0]
    row_iota = lax.broadcasted_iota(jnp.int32, (T, nf), 0)
    t = s // 2
    line = jnp.sum(jnp.where(row_iota == tmap[t], masks[...], 0), axis=0, keepdims=True)
    eye = jnp.where(
        lax.broadcasted_iota(jnp.int32, (PADF, nf), 0) == lax.broadcasted_iota(jnp.int32, (PADF, nf), 1),
        jnp.broadcast_to(line, (PADF, nf)), 0,
    ).astype(f32).astype(bf16)

    @pl.when(s % 2 == 0)
    def _():
        cols = pl.ds(pl.multiple_of(t * HALF, HALF), HALF)
        gi_o[0, 0] = dot(GI[:, cols], eye, TN).astype(bf16)

    @pl.when(s % 2 == 1)
    def _():
        for k in range(4):
            cols = pl.ds(pl.multiple_of(2 * HALF + k * 512 + t * QUART, QUART), QUART)
            gi_o[0, 0, pl.ds(k * QUART, QUART)] = dot(GI[:, cols], eye, TN).astype(bf16)


def update_call(occ, tmap, FIN, w, m, v, SM, sw, sm, sv, EM, ew, em, ev, GI, masks):
    S, BR, W = w.shape
    nf = ew.shape[0]
    sd = jax.ShapeDtypeStruct
    blk = pl.BlockSpec((1, BR, W), lambda s: (s, 0, 0))
    whole = lambda a: pl.BlockSpec(a.shape, lambda s: (0,) * len(a.shape))
    ins = [smem(), smem(), pl.BlockSpec((4, 1, 2, BR // 2, 128), lambda s: (0, s, 0, 0, 0)), blk, blk, blk]
    ins += [whole(a) for a in (SM, sw, sm, sv, EM, ew, em, ev, GI, masks)]
    big = sd((S, BR, W), f32)
    small = sd((10, D), f32)
    e = sd((nf, D), f32)
    outs = [big, big, big, big, sd((S, BR, W), bf16), e, e, e, e, sd((nf, D), bf16), small, small, small, small, sd((2, 2, HALF, nf), bf16)]
    specs = [blk] * 5 + [whole(a) for a in outs[5:14]] + [pl.BlockSpec((1, 1, HALF, nf), lambda s: (s // 2, s % 2, 0, 0))]
    return pl.pallas_call(
        update_kernel, out_shape=tuple(outs), grid=(S,), in_specs=ins, out_specs=tuple(specs),
        compiler_params=pltpu.CompilerParams(vmem_limit_bytes=VMEM_BYTES), name="update",
    )(occ, tmap, FIN, w, m, v, SM, sw, sm, sv, EM, ew, em, ev, GI, masks)


def body(
    features, feature_masks, table_map, owners, out_grad, weight_slots, moment1_slots, moment2_slots,
    emb_weight, emb_moment1, emb_moment2, small_weight, small_moment1, small_moment2,
):
    unit_count = owners.shape[0]
    capacity, block_rows, width = weight_slots.shape
    R = lax.axis_size("rows")
    bits = R.bit_length() - 1
    my_row = lax.axis_index("rows")
    units = jnp.arange(unit_count, dtype=jnp.int32)
    same_owner = owners[:, None] == owners[None, :]
    owner_rank = jnp.sum((same_owner & (units[None, :] < units[:, None])).astype(jnp.int32), axis=1)
    distance = owners ^ my_row
    place = jnp.zeros_like(distance)
    for bit in range(bits):
        place = place | (((distance >> bit) & 1) << (bits - 1 - bit))
    pos = place * capacity + owner_rank
    slot_iota = jnp.arange(capacity, dtype=jnp.int32)
    hit = (owners[None, :] == my_row) & (owner_rank[None, :] == slot_iota[:, None])
    slot_unit = jnp.sum(jnp.where(hit, units[None, :], 0), axis=1)
    occupied = jnp.sum(hit.astype(f32), axis=1)

    G, XT, h0o, a1s, a1q, n1s, n1q, rs, rq = gather_call(
        R, weight_slots, features, feature_masks, table_map, emb_weight, small_weight
    )
    G = G.reshape(R * capacity, block_rows, width)
    dY = out_grad.reshape(1024, width)
    out, gF, dy1, sg, ET, linv, OT, q, k, kT, v, W4 = forward_call(pos, G, h0o, a1s, a1q, dY, small_weight)
    FIN, SM, EM, GI = backward_call(
        R, gF, slot_unit, occupied, dy1, W4, ET, linv, OT, q, k, kT, v, a1s, a1q, n1s, n1q, rs, rq, XT, small_weight, sg
    )
    (
        g_slots, m_slots, v_slots, w_slots, w_copy, e_grad, e_m, e_v, e_w, e_copy, s_grad, s_m, s_v, s_w, grad_inputs,
    ) = update_call(
        occupied, table_map, FIN, weight_slots, moment1_slots, moment2_slots, SM, small_weight, small_moment1,
        small_moment2, EM, emb_weight, emb_moment1, emb_moment2, GI, feature_masks,
    )
    return (
        out.reshape(out_grad.shape), grad_inputs, g_slots, m_slots, v_slots, w_slots, w_copy,
        e_grad, e_m, e_v, e_w, e_copy, s_grad, s_m, s_v, s_w,
    )


def solution(mesh):
    rows3 = P("rows", None, None)
    feat2 = P("feat", None)
    in_specs = (
        P("rows", None, None, "feat"), P(None, "feat"), P("rows"), P(), P("rows", None, "feat", None),
        rows3, rows3, rows3, feat2, feat2, feat2, P(), P(), P(),
    )
    out_specs = (
        P("rows", None, "feat", None), P("rows", None, None, "feat"), rows3, rows3, rows3, rows3, rows3,
        feat2, feat2, feat2, feat2, feat2, P(), P(), P(), P(),
    )
    return jax.shard_map(body, mesh=mesh, in_specs=in_specs, out_specs=out_specs, check_vma=False)
```

```python
import functools
import math

import jax
import jax.numpy as jnp
from jax import lax
from jax.experimental import pallas as pl
from jax.experimental.pallas import tpu as pltpu
from jax.sharding import PartitionSpec as P

MESH = pl.DeviceIdType.MESH
bf16, f32 = jnp.bfloat16, jnp.float32
NN = (((1,), (0,)), ((), ()))
NT = (((1,), (1,)), ((), ()))
TN = (((0,), (0,)), ((), ()))
LOG2E = math.log2(math.e)
HEADS = 4
HEAD_DIM = 128
STEP = 10
LN_EPS = 1e-05
BETA_FIRST = 0.9
BETA_SECOND = 0.999
ADAM_EPS = 1e-08
DECAY = 0.01
RATE_MATRIX = 0.1
RATE_EMBED = 0.3
RATE_SMALL = 0.6
D = 512
HALF = 1024
QUART = 256
PADF = 32
VMEM_BYTES = 60 * 2**20


def dot(a, b, dims=NN):
    return lax.dot_general(a, b, dims, preferred_element_type=f32)


def vmem():
    return pl.BlockSpec(memory_space=pltpu.VMEM)


def anyspace():
    return pl.BlockSpec(memory_space=pl.ANY)


def smem():
    return pl.BlockSpec(memory_space=pltpu.SMEM)


def remote(src, dst, send, recv, dev):
    return pltpu.make_async_remote_copy(
        src_ref=src, dst_ref=dst, send_sem=send, recv_sem=recv, device_id=dev, device_id_type=MESH
    )


def greet(peers):
    bar = pltpu.get_barrier_semaphore()
    for d in peers:
        pl.semaphore_signal(bar, inc=1, device_id=d, device_id_type=MESH)
    return bar


def mask_column(masks, table):
    which = lax.broadcasted_iota(jnp.int32, masks.shape, 1) == table
    return jnp.sum(jnp.where(which, masks[...], 0), axis=1, keepdims=True).astype(f32)


GROUPS = ((1, 3, True), (0, 1, False))


def gather_kernel(
    R, slots_ref, feat_ref, mask_ref, tmap_ref, emb_ref, small_ref,
    G_ref, XT_ref, h0_ref, a1s_ref, a1q_ref, n1s_ref, n1q_ref, rs_ref, rq_ref,
    own, XTo, XTa, tmpq, lsem, fs, fr, hs, hr, xs, xr, cs, cr, c2s, c2r,
):
    f = lax.axis_index("feat")
    r = lax.axis_index("rows")
    x = f // 2
    c = f % 2
    n = R.bit_length() - 1
    S, BR, W = own.shape
    BH, CH = BR // 2, W // 2
    core_id = (f ^ 1, r)
    x_id = (f ^ 2, r)
    row_id = [(f, r ^ (1 << (n - 1 - j))) for j in range(n)]
    peers = [core_id, x_id] + row_id
    bar = greet(peers)
    own[...] = slots_ref[...].astype(bf16)
    pl.semaphore_wait(bar, len(peers))
    local = pltpu.make_async_copy(own, G_ref.at[0], lsem)
    local.start()
    subs = [(j, g) for j in range(n) for g in range(-1, j)]
    index = {jg: i for i, jg in enumerate(subs)}

    def span(g):
        return (0, 1) if g < 0 else (1 << g, 1 << g)

    def region(s, half_col):
        rows = pl.ds(pl.multiple_of(c * BH, BH), BH)
        cols = pl.ds(pl.multiple_of(half_col * CH, CH), CH) if GROUPS[s][2] else pl.ds(0, W)
        return pl.ds(GROUPS[s][0], GROUPS[s][1]), rows, cols

    def hyper(s, j, g):
        where = region(s, x)
        start, size = span(g)
        k = index[(j, g)]
        if g < 0:
            src, dst = own.at[where], G_ref.at[(1 << j, *where)]
        else:
            src = G_ref.at[(pl.ds(start, size), *where)]
            dst = G_ref.at[(pl.ds((1 << j) + start, size), *where)]
        return remote(src, dst, hs.at[s, k], hr.at[s, k], row_id[j])

    def forward(s, j, g, half_col, sems, semr, dev):
        start, size = span(g)
        k = index[(j, g)]
        ref = G_ref.at[(pl.ds((1 << j) + start, size), *region(s, half_col))]
        return remote(ref, ref, sems.at[s, k], semr.at[s, k], dev)

    order = range(len(GROUPS))
    for s in order:
        for j in range(n):
            hyper(s, j, -1).start()

    nf = feat_ref.shape[1]
    XTo[...] = jnp.zeros_like(XTo)
    for t in range(2):
        keep = mask_column(mask_ref, tmap_ref[t])
        XTo[pl.ds(0, nf), pl.ds(t * HALF, HALF)] = (feat_ref[t, :, 0, :].astype(f32) * keep).astype(bf16)
        query = (feat_ref[t, :, 1, :].astype(f32) * keep).astype(bf16)
        for k in range(4):
            XTo[pl.ds(0, nf), pl.ds(2 * HALF + D + k * 512 + t * QUART, QUART)] = query[:, k * QUART:(k + 1) * QUART]
    XTo[pl.ds(0, nf), pl.ds(2 * HALF, D)] = emb_ref[...].astype(bf16)
    wide = 2 * HALF + D
    shared = pl.ds(0, wide)

    def rows_of(dev):
        return pl.ds(pl.multiple_of(dev * PADF, PADF), PADF)

    def chunk_of(dev):
        return pl.ds(pl.multiple_of(wide + dev * 512, 512), 512)

    tail = pl.ds(wide, 512)
    feats = [
        remote(XTo.at[:, shared], XTa.at[rows_of(f), shared], fs.at[0], fr.at[0], core_id),
        remote(XTo.at[:, chunk_of(f ^ 1)], XTa.at[rows_of(f), tail], fs.at[1], fr.at[1], core_id),
        remote(XTo.at[:, shared], XTa.at[rows_of(f), shared], fs.at[2], fr.at[2], x_id),
        remote(XTo.at[:, chunk_of(f ^ 2)], XTa.at[rows_of(f), tail], fs.at[3], fr.at[3], x_id),
        remote(XTo.at[:, chunk_of(f ^ 3)], tmpq, fs.at[4], fr.at[4], x_id),
        remote(XTa.at[rows_of(f ^ 2), shared], XTa.at[rows_of(f ^ 2), shared], fs.at[5], fr.at[5], core_id),
        remote(tmpq, XTa.at[rows_of(f ^ 2), tail], fs.at[6], fr.at[6], core_id),
    ]
    for copy in feats[:5]:
        copy.start()
    XTa[rows_of(f), shared] = XTo[:, shared]
    XTa[rows_of(f), tail] = XTo[:, chunk_of(f)]

    def x_arrive(j):
        for s in order:
            if GROUPS[s][2]:
                for g in range(-1, j):
                    forward(s, j, g, x, xs, xr, x_id).wait_recv()
                    forward(s, j, g, 1 - x, c2s, c2r, core_id).start()

    def hyper_arrive(j):
        for s in order:
            for g in range(-1, j):
                hyper(s, j, g).wait_recv()
                if GROUPS[s][2]:
                    forward(s, j, g, x, xs, xr, x_id).start()
                forward(s, j, g, x, cs, cr, core_id).start()
            for j2 in range(j + 1, n):
                hyper(s, j2, j).start()

    hyper_arrive(0)
    feats[2].wait_recv()
    feats[4].wait_recv()
    feats[5].start()
    feats[6].start()
    for j in range(1, n - 1):
        hyper_arrive(j)
        x_arrive(j - 1)
    for k in (0, 1, 3, 5, 6):
        feats[k].wait_recv()

    shift0 = small_ref[0:1]
    gain = small_ref[1:2]
    shift = small_ref[2:3]
    E = XTa[:, pl.ds(2 * HALF, D)]

    def norm(cols):
        h = dot(XTa[:, cols], E, TN) + shift0
        mean = jnp.mean(h, axis=-1, keepdims=True)
        cen = h - mean
        rstd = lax.rsqrt(jnp.mean(cen * cen, axis=-1, keepdims=True) + LN_EPS)
        nrm = cen * rstd
        return h, nrm, rstd, (nrm * gain + shift).astype(bf16)

    @pl.loop(0, 8)
    def _(i):
        rows = pl.ds(pl.multiple_of(i * QUART, QUART), QUART)
        h, nrm, rstd, act = norm(rows)
        n1s_ref[rows] = nrm.astype(bf16)
        a1s_ref[rows] = act
        rs_ref[rows] = jnp.broadcast_to(rstd, (QUART, 128))

        @pl.when(i % 4 == f)
        def _():
            h0_ref[pl.ds(pl.multiple_of((i // 4) * 512, 512), QUART)] = h

    @pl.loop(0, 2)
    def _(t):
        rows = pl.ds(pl.multiple_of(t * QUART, QUART), QUART)
        h, nrm, rstd, act = norm(pl.ds(pl.multiple_of(wide + t * QUART, QUART), QUART))
        n1q_ref[rows] = nrm.astype(bf16)
        a1q_ref[rows] = act
        rq_ref[rows] = jnp.broadcast_to(rstd, (QUART, 128))
        h0_ref[pl.ds(pl.multiple_of(t * 512 + QUART, QUART), QUART)] = h

    XT_ref[...] = XTa[...]
    hyper_arrive(n - 1)
    if n > 1:
        x_arrive(n - 2)
    x_arrive(n - 1)
    local.wait()
    for copy in feats:
        copy.wait_send()
    for s in order:
        for j, g in subs:
            hyper(s, j, g).wait_send()
            forward(s, j, g, x, cs, cr, core_id).wait()
            if GROUPS[s][2]:
                forward(s, j, g, x, xs, xr, x_id).wait_send()
                forward(s, j, g, 1 - x, c2s, c2r, core_id).wait()


def gather_call(R, slots, features, masks, tmap, emb, small):
    S, BR, W = slots.shape
    n = R.bit_length() - 1
    M = n * (n + 1) // 2
    sem = pltpu.SemaphoreType.DMA((len(GROUPS), M))
    sd = jax.ShapeDtypeStruct
    cols = 2 * HALF + D + 512
    return pl.pallas_call(
        functools.partial(gather_kernel, R),
        out_shape=(
            sd((R, S, BR, W), bf16), sd((4 * PADF, cols), bf16), sd((1024, D), f32),
            sd((2048, D), bf16), sd((512, D), bf16), sd((2048, D), bf16), sd((512, D), bf16),
            sd((2048, 128), f32), sd((512, 128), f32),
        ),
        in_specs=[vmem(), vmem(), vmem(), smem(), vmem(), vmem()],
        out_specs=(anyspace(),) + (vmem(),) * 8,
        scratch_shapes=[
            pltpu.VMEM((S, BR, W), bf16), pltpu.VMEM((PADF, 2 * HALF + D + 2048), bf16),
            pltpu.VMEM((4 * PADF, cols), bf16), pltpu.VMEM((PADF, 512), bf16),
            pltpu.SemaphoreType.DMA, pltpu.SemaphoreType.DMA((7,)), pltpu.SemaphoreType.DMA((7,)),
        ] + [sem] * 8,
        compiler_params=pltpu.CompilerParams(collective_id=0, has_side_effects=True, vmem_limit_bytes=VMEM_BYTES),
        name="gather_weights",
    )(slots, features, masks, tmap, emb, small)


def gelu_pair(u):
    t = 1.0 / (1.0 + (0.3275911 * math.sqrt(0.5)) * jnp.abs(u))
    ex = jnp.exp2((-0.5 * LOG2E) * (u * u))
    poly = t * (0.127414796 + t * (-0.142248368 + t * (0.7107068705 + t * (-0.7265760135 + t * 0.5307027145))))
    e = poly * ex
    phi = jnp.where(u >= 0, 1.0 - e, e)
    return u * phi, phi + u * ex * (1.0 / math.sqrt(2 * math.pi))


def forward_kernel(
    BR, pos, G, a1s, a1q,
    Wo, linv, qo, kTo, vo, ET, OT, Oo,
    W, q_s, k_s, kT_s, v_s, vT_s, ET_s, OT_s, O_s, wsem, osem,
):
    U = pos.shape[0]
    R = U // 3
    per = D // BR
    f = lax.axis_index("feat")

    def wcopy(u):
        return pltpu.make_async_copy(G.at[pos[u]], W.at[pl.ds(u * BR, BR)], wsem.at[u])

    for u in range(U):
        wcopy(u).start()

    def wwait(i):
        for u in range(i * per, (i + 1) * per):
            wcopy(u).wait()

    def mat(i):
        return W[pl.ds(i * D, D)]

    scale = (HEAD_DIM**-0.5) * LOG2E
    outs = []

    def ship(src, dst):
        copy = pltpu.make_async_copy(src, dst, osem.at[len(outs)])
        copy.start()
        outs.append(copy)

    wwait(0)
    for t in range(2):
        sup = pl.multiple_of(t * HALF + f * QUART, QUART)
        q_s[pl.ds(t * 512, QUART)] = (dot(a1s[pl.ds(sup, QUART)], mat(0)) * scale).astype(bf16)
        q_s[pl.ds(t * 512 + QUART, QUART)] = (dot(a1q[pl.ds(t * QUART, QUART)], mat(0)) * scale).astype(bf16)
    wwait(1)
    wwait(2)

    @pl.loop(0, 4)
    def _(i):
        rows = pl.ds(pl.multiple_of(i * 512, 512), 512)
        a = a1s[rows]
        k = dot(a, mat(1)).astype(bf16)
        k_s[rows] = k
        kT_s[:, rows] = k.T
        v = dot(a, mat(2)).astype(bf16)
        v_s[rows] = v
        vT_s[:, rows] = v.T

    ship(q_s, qo)
    ship(kT_s, kTo)
    ship(v_s, vo)
    for i in range(3, 12):
        wwait(i)
    ship(W, Wo)

    @pl.loop(0, 8)
    def _(i):
        t = i // HEADS
        h = i % HEADS
        ks = pl.ds(pl.multiple_of(t * HALF, HALF), HALF)
        qs = pl.ds(pl.multiple_of(t * 512, 512), 512)
        hs = pl.ds(pl.multiple_of(h * HEAD_DIM, HEAD_DIM), HEAD_DIM)
        st = dot(k_s[ks, hs], q_s[qs, hs], NT)
        top = jnp.max(st, axis=0, keepdims=True)
        e = jnp.exp2(st - top)
        inv = 1.0 / jnp.sum(e, axis=0, keepdims=True)
        eb = e.astype(bf16)
        ET_s[i] = eb
        pltpu.make_async_copy(ET_s.at[i], ET.at[i], osem.at[6 + i]).start()
        linv[pl.ds(i, 1)] = inv
        ot = (dot(vT_s[hs, ks], eb) * inv).astype(bf16)
        OT_s[hs, qs] = ot
        O_s[qs, hs] = ot.T

    ship(O_s, Oo)
    ship(OT_s, OT)
    for copy in outs:
        copy.wait()
    for i in range(8):
        pltpu.make_async_copy(ET_s.at[i], ET.at[i], osem.at[6 + i]).wait()


def forward_call(pos, G, a1s, a1q):
    BR = G.shape[1]
    U = pos.shape[0]
    sd = jax.ShapeDtypeStruct
    V = pltpu.VMEM
    return pl.pallas_call(
        functools.partial(forward_kernel, BR),
        out_shape=(
            sd((12 * D, D), bf16), sd((8, 512), f32), sd((1024, D), bf16), sd((D, 2048), bf16), sd((2048, D), bf16),
            sd((8, HALF, 512), bf16), sd((D, 1024), bf16), sd((1024, D), bf16),
        ),
        in_specs=[smem(), anyspace(), vmem(), vmem()],
        out_specs=(anyspace(), vmem()) + (anyspace(),) * 6,
        scratch_shapes=[
            V((12 * D, D), bf16), V((1024, D), bf16), V((2048, D), bf16), V((D, 2048), bf16), V((2048, D), bf16),
            V((D, 2048), bf16), V((8, HALF, 512), bf16), V((D, 1024), bf16), V((1024, D), bf16),
            pltpu.SemaphoreType.DMA((U,)), pltpu.SemaphoreType.DMA((14,)),
        ],
        compiler_params=pltpu.CompilerParams(vmem_limit_bytes=VMEM_BYTES),
        name="forward",
    )(pos, G, a1s, a1q)


CHUNKS = ((2, 2), (0, 2), (4, 1), (5, 1))


def main_kernel(
    R, su, occ, linv, small, Wh, Oh, h0h, dYh, ETh, OTh, qh, kTh, vh, a1sh, a1qh, n1sh, n1qh, rsh, rqh, XTh,
    out, FIN, SM, EM, GI,
    W, O_s, y_s, dY, ETb, OT, qs, kT, vs, a1s, a1q, n1s, n1q, rs, rq, XT,
    a2_s, G_s, dU_s, Dp, sg, eg, GT, S, RC, RX, RH, AGB, AGL, SEL, PK, RK, GC, XS, XR,
    lsem, esem, osem, ss, sr, fs, fr, ps, pr, gs, gr,
):
    f = lax.axis_index("feat")
    r = lax.axis_index("rows")
    x = f // 2
    c = f % 2
    n = R.bit_length() - 1
    BH = S.shape[4]
    per = D // (2 * BH)
    core_id = (f ^ 1, r)
    x_id = (f ^ 2, r)
    row_id = [(f, r ^ (1 << j)) for j in range(n)]
    peers = [core_id, x_id] + row_id
    bar = greet(peers)

    loads = {}

    def load(name, src, dst):
        loads[name] = pltpu.make_async_copy(src, dst, lsem.at[len(loads)])
        loads[name].start()

    def rows_w(i):
        return pl.ds(i * D, D)

    load("O", Oh, O_s)
    load("h0", h0h, y_s)
    for i in (3, 4, 8, 5, 9, 6, 10, 7, 11):
        load(i, Wh.at[rows_w(i)], W.at[rows_w(i)])
    load("dY", dYh, dY)
    load("OT", OTh, OT)
    load("v", vh, vs)
    load("q", qh, qs)
    load("kT", kTh, kT)

    def ecopy(h, t):
        k = (h % 2) * 2 + t
        return pltpu.make_async_copy(ETh.at[t * HEADS + h], ETb.at[k], esem.at[k])

    for h in range(2):
        for t in range(2):
            ecopy(h, t).start()
    load("a1s", a1sh, a1s)
    load("a1q", a1qh, a1q)
    load("n1s", n1sh, n1s)
    load("n1q", n1qh, n1q)
    load("rs", rsh, rs)
    load("rq", rqh, rq)
    load("XT", XTh, XT)
    for i in range(3):
        load(i, Wh.at[rows_w(i)], W.at[rows_w(i)])
    pl.semaphore_wait(bar, len(peers))

    bits = [(r >> j) & 1 for j in range(n)]
    base = [0]
    for j in range(n):
        base.append(base[j] + bits[j] * (R >> (j + 1)))

    def groups(k):
        return pl.ds(CHUNKS[k][0], CHUNKS[k][1])

    def core_copy(k):
        return remote(S.at[1 - c, :, groups(k)], RC.at[:, groups(k)], ss.at[k, 0], sr.at[k, 0], core_id)

    def x_copy(k):
        return remote(S.at[c, 1 - x, groups(k)], RX.at[groups(k)], ss.at[k, 1], sr.at[k, 1], x_id)

    def rs_copy(k, j):
        half = R >> (j + 1)
        away = base[j] + (1 - bits[j]) * half
        off = R - (R >> j)
        return remote(
            S.at[c, x, groups(k), pl.ds(away, half)], RH.at[groups(k), pl.ds(off, half)],
            ss.at[k, 2 + j], sr.at[k, 2 + j], row_id[j],
        )

    def ag_copy(k, j):
        span = pl.ds(base[j + 1], R >> (j + 1))
        ref = AGB.at[groups(k), span] if k < 3 else AGL.at[span]
        return remote(ref, ref, ss.at[k, 2 + n + j], sr.at[k, 2 + n + j], row_id[j])

    def add(a, b):
        return (a.astype(f32) + b.astype(f32)).astype(bf16)

    def step(k, stage):
        g0, ng = CHUNKS[k]
        gl = range(g0, g0 + ng)
        if stage == 0:
            core_copy(k).wait_recv()
            for g in gl:
                S[c, 1 - x, g] = add(S[c, 1 - x, g], RC[1 - x, g])
            x_copy(k).start()
            for g in gl:
                S[c, x, g] = add(S[c, x, g], RC[x, g])
        elif stage == 1:
            x_copy(k).wait_recv()
            for g in gl:
                S[c, x, g] = add(S[c, x, g], RX[g])
            rs_copy(k, 0).start()
        elif stage < 2 + n:
            j = stage - 2
            half = R >> (j + 1)
            off = R - (R >> j)
            rs_copy(k, j).wait_recv()
            keep = pl.ds(base[j + 1], half)
            for g in gl:
                total = add(S[c, x, g, keep], RH[g, pl.ds(off, half)])
                if j < n - 1:
                    S[c, x, g, keep] = total
                elif k < 3:
                    AGB[g, keep] = total
                else:
                    AGL[keep] = total
            if j < n - 1:
                rs_copy(k, j + 1).start()
            else:
                ag_copy(k, n - 1).start()
        else:
            j = 2 * n + 1 - stage
            ag_copy(k, j).wait_recv()
            if j > 0:
                ag_copy(k, j - 1).start()

    last = 2 + 2 * n
    done = [0] * len(CHUNKS)

    def tick(k):
        if done[k] < last:
            step(k, done[k])
            done[k] += 1

    def put(g0, i, val):
        for k in range(val.shape[1] // 128):
            piece = val[:, k * 128:(k + 1) * 128].reshape(per, 2, BH, 128)
            for h in range(2):
                S[k % 2, h, g0 + k // 2, pl.ds(i * per, per)] = piece[:, h]

    gain2 = small[3:4]
    shift2 = small[4:5]
    RB = 256

    def norm2(y1):
        cen = y1 - jnp.mean(y1, axis=-1, keepdims=True)
        rstd = lax.rsqrt(jnp.mean(cen * cen, axis=-1, keepdims=True) + LN_EPS)
        return cen * rstd, rstd

    loads["O"].wait()
    loads["h0"].wait()
    loads[3].wait()

    @pl.loop(0, 1024 // RB)
    def _(i):
        rows = pl.ds(pl.multiple_of(i * RB, RB), RB)
        y1 = y_s[rows] + dot(O_s[rows], W[rows_w(3)])
        y_s[rows] = y1
        n2, _ = norm2(y1)
        a2 = (n2 * gain2 + shift2).astype(bf16)
        a2_s[rows] = a2
        acc = y1 + small[5:6]
        for j in range(4):
            @pl.when(i == 0)
            def _():
                loads[4 + j].wait()
                loads[8 + j].wait()
            gl, gp = gelu_pair(dot(a2, W[rows_w(4 + j)]) + small[6 + j:7 + j])
            gb = gl.astype(bf16)
            G_s[j, rows] = gb
            dU_s[j, rows] = gp.astype(bf16)
            acc = acc + dot(gb, W[rows_w(8 + j)])
        O_s[rows] = acc.astype(bf16)

    ship_out = pltpu.make_async_copy(O_s, out, osem.at[0])
    ship_out.start()
    loads["dY"].wait()
    for j in range(4):
        put(2, j, dot(G_s[j], dY[...], TN).astype(bf16))
    core_copy(0).start()

    sg[...] = jnp.zeros_like(sg)

    def backward_rows(first, count):
        @pl.loop(first, first + count)
        def _(i):
            rows = pl.ds(pl.multiple_of(i * RB, RB), RB)
            dy = dY[rows]
            da2 = jnp.zeros((RB, D), f32)
            for j in range(4):
                du = (dot(dy, W[rows_w(8 + j)], NT) * dU_s[j, rows].astype(f32)).astype(bf16)
                dU_s[j, rows] = du
                sg[6 + j:7 + j] += jnp.sum(du.astype(f32), axis=0, keepdims=True)
                da2 = da2 + dot(du, W[rows_w(4 + j)], NT)
            n2, rstd = norm2(y_s[rows])
            dyf = dy.astype(f32)
            sg[3:4] += jnp.sum(da2 * n2, axis=0, keepdims=True)
            sg[4:5] += jnp.sum(da2, axis=0, keepdims=True)
            sg[5:6] += jnp.sum(dyf, axis=0, keepdims=True)
            cc = da2 * gain2
            m1 = jnp.mean(cc, axis=-1, keepdims=True)
            m2 = jnp.mean(cc * n2, axis=-1, keepdims=True)
            y_s[rows] = dyf + rstd * (cc - m1 - n2 * m2)

    backward_rows(0, 2)
    tick(0)
    backward_rows(2, 2)
    for j in range(4):
        put(0, j, dot(a2_s[...], dU_s[j], TN).astype(bf16))
    core_copy(1).start()

    scale = HEAD_DIM**-0.5
    for i in range(2):
        dU_s[1, pl.ds(i * 512, 512)] = y_s[pl.ds(i * 512, 512)].astype(bf16)
    for name in ("OT", "v", "q", "kT", "a1s", "a1q"):
        loads[name].wait()
    put(4, 3, dot(OT[...], dU_s[1]).astype(bf16))
    for t in range(2):
        cols = pl.ds(t * 512, 512)
        for h in range(HEADS):
            rows = pl.ds(h * HEAD_DIM, HEAD_DIM)
            d = dot(W[pl.ds(3 * D + h * HEAD_DIM, HEAD_DIM)], dU_s[1, cols], NT) * linv[pl.ds(t * HEADS + h, 1)]
            Dp[pl.ds(t * HEADS + h, 1)] = jnp.sum(d * OT[rows, cols].astype(f32), axis=0, keepdims=True)
            dU_s[2, pl.ds(t * 512 + h * HEAD_DIM, HEAD_DIM)] = d.astype(bf16)
    tick(1)

    def heads(h):
        hs = pl.ds(h * HEAD_DIM, HEAD_DIM)
        for t in range(2):
            ecopy(h, t).wait()

        @pl.loop(0, 2)
        def _(t):
            i = t * HEADS + h
            ksl = pl.ds(pl.multiple_of(t * HALF, HALF), HALF)
            qsl = pl.ds(pl.multiple_of(t * 512, 512), 512)
            do = dU_s[2, pl.ds(pl.multiple_of(t * 512 + h * HEAD_DIM, HEAD_DIM), HEAD_DIM)]
            dp = dot(vs[ksl, hs], do)
            e = ETb[(h % 2) * 2 + t]
            ds = (e.astype(f32) * (dp - Dp[pl.ds(i, 1)])).astype(bf16)
            G_s[2 + t, :, hs] = dot(e, do, NT).astype(bf16)
            G_s[t, :, hs] = (dot(ds, qs[qsl, hs]) * (1.0 / LOG2E)).astype(bf16)
            dqT = (dot(kT[hs, ksl], ds) * scale).astype(bf16)
            dU_s[0, qsl, hs] = dqT.T

        if h + 2 < HEADS:
            for t in range(2):
                ecopy(h + 2, t).start()

    def weight_grads(m):
        cols = pl.ds(m * 256, 256)
        acc = jnp.zeros((D, 256), f32)
        for t in range(2):
            sup = pl.multiple_of(t * HALF + f * QUART, QUART)
            acc += dot(a1s[pl.ds(sup, QUART)], dU_s[0, pl.ds(t * 512, QUART), cols], TN)
            acc += dot(a1q[pl.ds(t * QUART, QUART)], dU_s[0, pl.ds(t * 512 + QUART, QUART), cols], TN)
        put(4 + m, 0, acc.astype(bf16))
        for k in range(2):
            total = dot(a1s[pl.ds(0, HALF)], G_s[2 * k, :, cols], TN) + dot(a1s[pl.ds(HALF, HALF)], G_s[2 * k + 1, :, cols], TN)
            put(4 + m, 1 + k, total.astype(bf16))

    heads(0)
    tick(0)
    heads(1)
    weight_grads(0)
    core_copy(2).start()
    tick(0)
    heads(2)
    tick(2)
    tick(0)
    tick(1)
    heads(3)
    weight_grads(1)
    core_copy(3).start()
    tick(0)
    tick(1)

    eg[...] = jnp.zeros_like(eg)
    gain1 = small[1:2]
    emb_cols = pl.ds(2 * HALF, D)
    for name in ("n1s", "n1q", "rs", "rq", "XT", 0, 1, 2):
        loads[name].wait()

    def back(da, nrm, rstd, extra, cols, out_cols):
        sg[1:2] += jnp.sum(da * nrm, axis=0, keepdims=True)
        sg[2:3] += jnp.sum(da, axis=0, keepdims=True)
        cc = da * gain1
        m1 = jnp.mean(cc, axis=-1, keepdims=True)
        m2 = jnp.mean(cc * nrm, axis=-1, keepdims=True)
        wide = jnp.concatenate([rstd] * 4, axis=1)
        dh = wide * (cc - m1 - nrm * m2)
        if extra is not None:
            dh = dh + extra
        sg[0:1] += jnp.sum(dh, axis=0, keepdims=True)
        de = dh.astype(bf16)
        part = dot(XT[:, cols], de)
        back_in = dot(XT[:, emb_cols], de, NT).astype(bf16)
        for k in range(4):
            eg[k] += part[k * PADF:(k + 1) * PADF]
            GT[k % 2, k // 2, :, out_cols] = back_in[k * PADF:(k + 1) * PADF]

    def below(t):
        q0 = t * 512
        wq, wk, wv = W[rows_w(0)], W[rows_w(1)], W[rows_w(2)]
        da = dot(dU_s[0, pl.ds(q0 + QUART, QUART)], wq, NT)
        p0 = pl.ds(t * QUART, QUART)
        back(
            da, n1q[p0].astype(f32), rq[p0], y_s[pl.ds(q0 + QUART, QUART)],
            pl.ds(2 * HALF + D + t * QUART, QUART), pl.ds(2 * HALF + t * QUART, QUART),
        )
        for b in range(4):
            at = pl.ds(pl.multiple_of(((f + b) % 4) * QUART, QUART), QUART)
            rows = pl.ds(pl.multiple_of(t * HALF + ((f + b) % 4) * QUART, QUART), QUART)
            da = dot(G_s[t, at], wk, NT) + dot(G_s[2 + t, at], wv, NT)
            extra = None
            if b == 0:
                da = da + dot(dU_s[0, pl.ds(q0, QUART)], wq, NT)
                extra = y_s[pl.ds(q0, QUART)]
            back(da, n1s[rows].astype(f32), rs[rows], extra, rows, rows)

    below(0)
    tick(3)
    tick(2)
    tick(0)
    tick(1)
    below(1)

    small_rows = pl.ds(0, 16)
    PK[0, small_rows] = sg[...]
    for k in range(2):
        PK[0, pl.ds(16 + k * PADF, PADF)] = eg[2 * k + 1 - c]

    def pk_copy(i):
        rows = pl.ds(0, 80 if i == 0 else 48)
        dev = core_id if i == 0 else x_id if i == 1 else row_id[i - 2]
        return remote(PK.at[i, rows], RK.at[i, rows], ps.at[i], pr.at[i], dev)

    def pk_step(i):
        pk_copy(i).wait_recv()
        if i == 0:
            PK[1, small_rows] = PK[0, small_rows] + RK[0, small_rows]
            own = [eg[2 * k + c] + RK[0, pl.ds(16 + k * PADF, PADF)] for k in range(2)]
            PK[1, pl.ds(16, PADF)] = jnp.where(x == 0, own[1], own[0])
            PK[1, pl.ds(48, PADF)] = jnp.where(x == 0, own[0], own[1])
            pk_copy(1).start()
        else:
            old = PK[1, pl.ds(48, PADF)] if i == 1 else PK[i, pl.ds(16, PADF)]
            a = PK[i, small_rows] + RK[i, small_rows]
            b = old + RK[i, pl.ds(16, PADF)]
            if i < n + 1:
                PK[i + 1, small_rows] = a
                PK[i + 1, pl.ds(16, PADF)] = b
                pk_copy(i + 1).start()
            else:
                SM[...] = a
                EM[...] = b

    pk_copy(0).start()
    gt1 = remote(GT.at[1 - c], GC, gs.at[0], gr.at[0], core_id)
    gt1.start()
    sup = pl.ds(0, 2 * HALF)
    que = pl.ds(2 * HALF, 512)

    def que_of(k):
        return pl.ds(pl.multiple_of(2 * HALF + k * 512, 512), 512)

    gt2 = remote(XS, XR, gs.at[1], gr.at[1], x_id)
    tick(0)
    tick(2)
    pk_step(0)
    gt1.wait_recv()
    XS[:, sup] = add(GT[c, 1 - x, :, sup], GC[1 - x, :, sup])
    XS[:, que_of(c)] = GT[c, 1 - x, :, que]
    XS[:, que_of(1 - c)] = GC[1 - x, :, que]
    gt2.start()
    tick(1)
    tick(3)
    next_pk = 1

    def select(m):
        for s in range(4):
            p = lax.rem(su[s], R)
            if m == 0:
                g = lax.rem(2 * lax.div(su[s], R) + 4, 6)
                value = AGB[g, p].astype(f32) * occ[s]
            else:
                g = 2 * lax.max(lax.div(su[s], R) - 1, 0) + 1
                value = AGB[g, p].astype(f32) * occ[4 + s] + AGL[p].astype(f32) * occ[8 + s]
            SEL[m, s] = value.astype(bf16)

    def fin(m, k):
        if k == 3:
            return pltpu.make_async_copy(SEL.at[m], FIN.at[m, f], osem.at[1 + m])
        src, at = (FIN.at[m, f ^ 2], f ^ 2) if k == 2 else (SEL.at[m], f)
        return remote(src, FIN.at[m, at], fs.at[m, k], fr.at[m, k], x_id if k == 1 else core_id)

    def send_fin(m):
        select(m)
        for k in (1, 0, 3):
            fin(m, k).start()

    sent = False
    while min(done) < last:
        for k in (0, 1, 2, 3):
            tick(k)
        if next_pk < n + 2:
            pk_step(next_pk)
            next_pk += 1
        if not sent and min(done[:3]) == last:
            send_fin(0)
            sent = True
    send_fin(1)
    for i in range(next_pk, n + 2):
        pk_step(i)
    gt2.wait_recv()
    GI[:, sup] = (
        GT[c, x, :, sup].astype(f32) + GC[x, :, sup].astype(f32) + XR[:, sup].astype(f32)
    ).astype(bf16)
    GI[:, que_of(f)] = GT[c, x, :, que]
    GI[:, que_of(f ^ 1)] = GC[x, :, que]
    for k in range(2):
        GI[:, que_of(2 * (1 - x) + k)] = XR[:, pl.ds(2 * HALF + k * 512, 512)]
    for m in range(2):
        fin(m, 1).wait_recv()
        fin(m, 2).start()
    for m in range(2):
        fin(m, 0).wait()
        fin(m, 1).wait_send()
        fin(m, 2).wait()
        fin(m, 3).wait()
    for k in range(4):
        core_copy(k).wait_send()
        x_copy(k).wait_send()
        for j in range(n):
            rs_copy(k, j).wait_send()
            ag_copy(k, j).wait_send()
    for i in range(n + 2):
        pk_copy(i).wait_send()
    gt1.wait_send()
    gt2.wait_send()
    ship_out.wait()


def main_call(R, su, occ, linv, small, W, O, h0, dY, ET, OT, q, kT, v, a1s, a1q, n1s, n1q, rs, rq, XT):
    BH = 12 * D // (3 * R) // 2
    n = R.bit_length() - 1
    sd = jax.ShapeDtypeStruct
    V = pltpu.VMEM
    dma = pltpu.SemaphoreType.DMA
    blk = (R, BH, 128)
    like = lambda a: V(a.shape, a.dtype)
    return pl.pallas_call(
        functools.partial(main_kernel, R),
        out_shape=(sd((1024, D), bf16), sd((2, 4, 4, BH, 128), bf16), sd((16, D), f32), sd((PADF, D), f32), sd((PADF, 4096), bf16)),
        in_specs=[smem(), smem(), vmem(), vmem()] + [anyspace()] * 16,
        out_specs=(anyspace(), anyspace(), vmem(), vmem(), vmem()),
        scratch_shapes=[
            like(W), like(O), like(h0), like(dY), V((4, HALF, 512), bf16), like(OT), like(q), like(kT), like(v),
            like(a1s), like(a1q), like(n1s), like(n1q), like(rs), like(rq), like(XT),
            V((1024, D), bf16), V((4, 1024, 512), bf16), V((4, 1024, 512), bf16), V((8, 512), f32), V((16, D), f32),
            V((4, PADF, D), f32), V((2, 2, PADF, 2560), bf16),
            V((2, 2, 6) + blk, bf16), V((2, 6) + blk, bf16), V((6,) + blk, bf16), V((6,) + blk, bf16), V((5,) + blk, bf16), V(blk, bf16),
            V((2, 4, BH, 128), bf16), V((n + 2, 80, D), f32), V((n + 2, 80, D), f32),
            V((2, PADF, 2560), bf16), V((PADF, 3072), bf16), V((PADF, 3072), bf16),
            dma((26,)), dma((4,)), dma((3,)), dma((4, 2 + 2 * n)), dma((4, 2 + 2 * n)), dma((2, 3)), dma((2, 3)),
            dma((n + 2,)), dma((n + 2,)), dma((2,)), dma((2,)),
        ],
        compiler_params=pltpu.CompilerParams(collective_id=1, has_side_effects=True, vmem_limit_bytes=VMEM_BYTES),
        name="main",
    )(su, occ, linv, small, W, O, h0, dY, ET, OT, q, kT, v, a1s, a1q, n1s, n1q, rs, rq, XT)


def adamw(weight, grad, first, second, rate):
    first_new = BETA_FIRST * first + (1.0 - BETA_FIRST) * grad
    second_new = BETA_SECOND * second + (1.0 - BETA_SECOND) * grad * grad
    first_hat = first_new / (1.0 - BETA_FIRST**STEP)
    second_hat = second_new / (1.0 - BETA_SECOND**STEP)
    weight_new = weight - rate * (first_hat / (jnp.sqrt(second_hat) + ADAM_EPS) + DECAY * weight)
    return (first_new, second_new, weight_new)


def update_kernel(
    occ, tmap, FIN, w, m, v, SM, sw, sm, sv, EM, ew, em, ev, GI, masks, lo,
    g_o, m_o, v_o, w_o, wc_o, eg_o, em_o, ev_o, ew_o, ec_o, sg_o, sm_o, sv_o, sw_o, gi_o, lo_o,
):
    s = pl.program_id(0)
    keep = occ[s]
    BH = FIN.shape[3]
    for f in range(4):
        rows = pl.ds((f // 2) * BH, BH)
        for k in range(2):
            cols = pl.ds(k * 256 + (f % 2) * 128, 128)
            g = FIN[k, f, 0].astype(f32)
            a, b, d = adamw(w[0, rows, cols], g, m[0, rows, cols], v[0, rows, cols], RATE_MATRIX)
            g_o[0, rows, cols] = g * keep
            m_o[0, rows, cols] = a * keep
            v_o[0, rows, cols] = b * keep
            d = d * keep
            w_o[0, rows, cols] = d
            wc_o[0, rows, cols] = d.astype(bf16)

    @pl.when(s == 0)
    def _():
        g = SM[0:10]
        a, b, d = adamw(sw[...], g, sm[...], sv[...], RATE_SMALL)
        sg_o[...] = g
        sm_o[...] = a
        sv_o[...] = b
        sw_o[...] = d
        nf = ew.shape[0]
        g = EM[pl.ds(0, nf)]
        a, b, d = adamw(ew[...], g, em[...], ev[...], RATE_EMBED)
        eg_o[...] = g
        em_o[...] = a
        ev_o[...] = b
        ew_o[...] = d
        ec_o[...] = d.astype(bf16)

    nf = gi_o.shape[1]
    t = s // 2
    keep_in = mask_column(masks, tmap[t])

    @pl.when(s % 2 == 0)
    def _():
        cols = pl.ds(pl.multiple_of(t * HALF, HALF), HALF)
        gi_o[t, :, 0, :] = (GI[pl.ds(0, nf), cols].astype(f32) * keep_in).astype(bf16)

    @pl.when(s % 2 == 1)
    def _():
        for k in range(4):
            cols = pl.ds(pl.multiple_of(2 * HALF + k * 512 + t * QUART, QUART), QUART)
            gi_o[t, :, 1, pl.ds(k * QUART, QUART)] = (GI[pl.ds(0, nf), cols].astype(f32) * keep_in).astype(bf16)

    lo_o[...] = lo[...]


def update_call(occ, tmap, FIN, w, m, v, SM, sw, sm, sv, EM, ew, em, ev, GI, masks, lo):
    S, BR, W = w.shape
    nf = ew.shape[0]
    sd = jax.ShapeDtypeStruct
    blk = pl.BlockSpec((1, BR, W), lambda s: (s, 0, 0))
    whole = lambda a: pl.BlockSpec(a.shape, lambda s: (0,) * len(a.shape))
    ins = [smem(), smem(), pl.BlockSpec((2, 4, 1, BR // 2, 128), lambda s: (0, 0, s, 0, 0)), blk, blk, blk]
    ins += [whole(a) for a in (SM, sw, sm, sv, EM, ew, em, ev, GI, masks)] + [pl.BlockSpec((1024 // S, D), lambda s: (s, 0))]
    big = sd((S, BR, W), f32)
    small = sd((10, D), f32)
    e = sd((nf, D), f32)
    outs = [big, big, big, big, sd((S, BR, W), bf16), e, e, e, e, sd((nf, D), bf16), small, small, small, small, sd((2, nf, 2, HALF), bf16), sd(lo.shape, lo.dtype)]
    specs = [blk] * 5 + [whole(a) for a in outs[5:14]] + [whole(outs[14]), pl.BlockSpec((1024 // S, D), lambda s: (s, 0))]
    return pl.pallas_call(
        update_kernel, out_shape=tuple(outs), grid=(S,), in_specs=ins, out_specs=tuple(specs),
        compiler_params=pltpu.CompilerParams(vmem_limit_bytes=VMEM_BYTES), name="update",
    )(occ, tmap, FIN, w, m, v, SM, sw, sm, sv, EM, ew, em, ev, GI, masks, lo)


def body(
    features, feature_masks, table_map, owners, out_grad, weight_slots, moment1_slots, moment2_slots,
    emb_weight, emb_moment1, emb_moment2, small_weight, small_moment1, small_moment2,
):
    unit_count = owners.shape[0]
    capacity, block_rows, width = weight_slots.shape
    R = lax.axis_size("rows")
    bits = R.bit_length() - 1
    my_row = lax.axis_index("rows")
    units = jnp.arange(unit_count, dtype=jnp.int32)
    same_owner = owners[:, None] == owners[None, :]
    owner_rank = jnp.sum((same_owner & (units[None, :] < units[:, None])).astype(jnp.int32), axis=1)
    distance = owners ^ my_row
    place = jnp.zeros_like(distance)
    for bit in range(bits):
        place = place | (((distance >> bit) & 1) << (bits - 1 - bit))
    pos = place * capacity + owner_rank
    slot_iota = jnp.arange(capacity, dtype=jnp.int32)
    hit = (owners[None, :] == my_row) & (owner_rank[None, :] == slot_iota[:, None])
    slot_unit = jnp.sum(jnp.where(hit, units[None, :], 0), axis=1)
    occupied = jnp.sum(hit.astype(f32), axis=1)

    masks = feature_masks.T
    late = occupied * (slot_unit < R).astype(f32)
    kinds = jnp.concatenate([occupied, occupied - late, late])
    G, XT, h0o, a1s, a1q, n1s, n1q, rs, rq = gather_call(
        R, weight_slots, features.transpose(0, 3, 1, 2), masks, table_map, emb_weight, small_weight
    )
    G = G.reshape(R * capacity, block_rows, width)
    dY = out_grad.reshape(1024, width)
    W, linv, q, kT, v, ET, OT, O = forward_call(pos, G, a1s, a1q)
    out, FIN, SM, EM, GI = main_call(
        R, slot_unit, kinds, linv, small_weight, W, O, h0o, dY, ET, OT, q, kT, v, a1s, a1q, n1s, n1q, rs, rq, XT
    )
    (
        g_slots, m_slots, v_slots, w_slots, w_copy, e_grad, e_m, e_v, e_w, e_copy, s_grad, s_m, s_v, s_w, grad_inputs, out,
    ) = update_call(
        kinds, table_map, FIN, weight_slots, moment1_slots, moment2_slots, SM, small_weight, small_moment1,
        small_moment2, EM, emb_weight, emb_moment1, emb_moment2, GI, masks, out,
    )
    grad_inputs = grad_inputs.transpose(0, 2, 3, 1)
    return (
        out.reshape(out_grad.shape), grad_inputs, g_slots, m_slots, v_slots, w_slots, w_copy,
        e_grad, e_m, e_v, e_w, e_copy, s_grad, s_m, s_v, s_w,
    )


def solution(mesh):
    rows3 = P("rows", None, None)
    feat2 = P("feat", None)
    in_specs = (
        P("rows", None, None, "feat"), P(None, "feat"), P("rows"), P(), P("rows", None, "feat", None),
        rows3, rows3, rows3, feat2, feat2, feat2, P(), P(), P(),
    )
    out_specs = (
        P("rows", None, "feat", None), P("rows", None, None, "feat"), rows3, rows3, rows3, rows3, rows3,
        feat2, feat2, feat2, feat2, feat2, P(), P(), P(), P(),
    )
    return jax.shard_map(body, mesh=mesh, in_specs=in_specs, out_specs=out_specs, check_vma=False)
```

```python
import functools
import math

import jax
import jax.numpy as jnp
from jax import lax
from jax.experimental import pallas as pl
from jax.experimental.pallas import tpu as pltpu
from jax.sharding import PartitionSpec as P

MESH = pl.DeviceIdType.MESH
bf16, f32 = jnp.bfloat16, jnp.float32
NN = (((1,), (0,)), ((), ()))
NT = (((1,), (1,)), ((), ()))
TN = (((0,), (0,)), ((), ()))
LOG2E = math.log2(math.e)
HEADS = 4
HEAD_DIM = 128
STEP = 10
LN_EPS = 1e-05
BETA_FIRST = 0.9
BETA_SECOND = 0.999
ADAM_EPS = 1e-08
DECAY = 0.01
RATE_MATRIX = 0.1
RATE_EMBED = 0.3
RATE_SMALL = 0.6
D = 512
HALF = 1024
QUART = 256
PADF = 32
VMEM_BYTES = 60 * 2**20


def dot(a, b, dims=NN):
    return lax.dot_general(a, b, dims, preferred_element_type=f32)


def vmem():
    return pl.BlockSpec(memory_space=pltpu.VMEM)


def anyspace():
    return pl.BlockSpec(memory_space=pl.ANY)


def smem():
    return pl.BlockSpec(memory_space=pltpu.SMEM)


def remote(src, dst, send, recv, dev):
    return pltpu.make_async_remote_copy(
        src_ref=src, dst_ref=dst, send_sem=send, recv_sem=recv, device_id=dev, device_id_type=MESH
    )


def greet(peers):
    bar = pltpu.get_barrier_semaphore()
    for d in peers:
        pl.semaphore_signal(bar, inc=1, device_id=d, device_id_type=MESH)
    return bar


def mask_column(masks, table):
    T, nf = masks.shape
    which = lax.broadcasted_iota(jnp.int32, (T, nf), 0) == table
    line = jnp.sum(jnp.where(which, masks[...], 0), axis=0, keepdims=True)
    eye = lax.broadcasted_iota(jnp.int32, (nf, nf), 0) == lax.broadcasted_iota(jnp.int32, (nf, nf), 1)
    return jnp.sum(jnp.where(eye, jnp.broadcast_to(line, (nf, nf)), 0), axis=1, keepdims=True).astype(f32)


GROUPS = (True, False)


def gather_kernel(
    R, slots_ref, feat_ref, mask_ref, tmap_ref, own_ref, emb_ref, small_ref,
    su_ref, kind_ref, XT_ref, h0_ref, a1s_ref, a1q_ref, n1s_ref, n1q_ref, rs_ref, rq_ref, linv,
    Wo, qo, kTo, vo, ET, OT, Oo,
    pos, G0, G1, own, XTo, XTa, tmpq, W, q_s, k_s, kT_s, v_s, vT_s, ET_s, OT_s, O_s,
    lsem, osem, esem, fs, fr, hs, hr, xs, xr, cs, cr, c2s, c2r,
):
    f = lax.axis_index("feat")
    r = lax.axis_index("rows")
    x = f // 2
    c = f % 2
    n = R.bit_length() - 1
    S, BR = slots_ref.shape[:2]
    U = own_ref.shape[0]
    BH = BR // 2
    Gs = (G0, G1)
    core_id = (f ^ 1, r)
    x_id = (f ^ 2, r)
    row_id = [(f, r ^ (1 << (n - 1 - j))) for j in range(n)]
    peers = [core_id, x_id] + row_id
    bar = greet(peers)
    for k in range(4):
        own[k // 2, k % 2] = slots_ref[:, :, k * 128:(k + 1) * 128].astype(bf16)
    pl.semaphore_wait(bar, len(peers))

    def keep_own(p):
        return pltpu.make_async_copy(own.at[p], Gs[p].at[:, 0], lsem.at[p])

    subs = [(j, g) for j in range(n) for g in range(-1, j)]
    index = {jg: i for i, jg in enumerate(subs)}
    rows_c = pl.ds(pl.multiple_of(c * BH, BH), BH)

    def part(p, s, half, start, size):
        if GROUPS[s]:
            return Gs[p].at[half, pl.ds(start, size), pl.ds(1, 3), rows_c]
        return Gs[p].at[:, pl.ds(start, size), 0, rows_c]

    def hyper(p, s, j, g):
        k = index[(j, g)]
        if g < 0:
            if GROUPS[s]:
                src, dst = own.at[p, x, pl.ds(1, 3), rows_c], Gs[p].at[x, 1 << j, pl.ds(1, 3), rows_c]
            else:
                src, dst = own.at[p, :, 0, rows_c], Gs[p].at[:, 1 << j, 0, rows_c]
        else:
            src, dst = part(p, s, x, 1 << g, 1 << g), part(p, s, x, (1 << j) + (1 << g), 1 << g)
        return remote(src, dst, hs.at[p, s, k], hr.at[p, s, k], row_id[j])

    def forward(p, s, j, g, half, sems, semr, dev):
        start, size = (0, 1) if g < 0 else (1 << g, 1 << g)
        k = index[(j, g)]
        ref = part(p, s, half, (1 << j) + start, size)
        return remote(ref, ref, sems.at[p, s, k], semr.at[p, s, k], dev)

    def to_x(p, s, j, g):
        return forward(p, s, j, g, x, xs, xr, x_id)

    def to_core(p, s, j, g):
        return forward(p, s, j, g, x, cs, cr, core_id)

    def to_core_x(p, s, j, g):
        return forward(p, s, j, g, 1 - x, c2s, c2r, core_id)

    order = range(len(GROUPS))

    def send_own(p):
        for s in order:
            for j in range(n):
                hyper(p, s, j, -1).start()
        keep_own(p).start()

    def x_arrive(p, j):
        for s in order:
            if GROUPS[s]:
                for g in range(-1, j):
                    to_x(p, s, j, g).wait_recv()
                    to_core_x(p, s, j, g).start()

    def hyper_arrive(p, j):
        for s in order:
            for g in range(-1, j):
                hyper(p, s, j, g).wait_recv()
                if GROUPS[s]:
                    to_x(p, s, j, g).start()
                to_core(p, s, j, g).start()
            for j2 in range(j + 1, n):
                hyper(p, s, j2, j).start()

    def all_here(p):
        keep_own(p).wait()
        for s in order:
            for j, g in subs:
                to_core(p, s, j, g).wait_recv()
                if GROUPS[s]:
                    to_core_x(p, s, j, g).wait_recv()

    def all_sent(p):
        for s in order:
            for j, g in subs:
                hyper(p, s, j, g).wait_send()
                to_core(p, s, j, g).wait_send()
                if GROUPS[s]:
                    to_x(p, s, j, g).wait_send()
                    to_core_x(p, s, j, g).wait_send()

    send_own(0)

    nf = feat_ref.shape[1]
    XTo[...] = jnp.zeros_like(XTo)
    for t in range(2):
        keep = mask_column(mask_ref, tmap_ref[t])
        XTo[pl.ds(0, nf), pl.ds(t * HALF, HALF)] = (feat_ref[t, :, 0, :].astype(f32) * keep).astype(bf16)
        query = (feat_ref[t, :, 1, :].astype(f32) * keep).astype(bf16)
        for k in range(4):
            XTo[pl.ds(0, nf), pl.ds(2 * HALF + D + k * 512 + t * QUART, QUART)] = query[:, k * QUART:(k + 1) * QUART]
    XTo[pl.ds(0, nf), pl.ds(2 * HALF, D)] = emb_ref[...].astype(bf16)
    wide = 2 * HALF + D
    shared = pl.ds(0, wide)
    tail = pl.ds(wide, 512)

    def rows_of(dev):
        return pl.ds(pl.multiple_of(dev * PADF, PADF), PADF)

    def chunk_of(dev):
        return pl.ds(pl.multiple_of(wide + dev * 512, 512), 512)

    feats = [
        remote(XTo.at[:, shared], XTa.at[rows_of(f), shared], fs.at[0], fr.at[0], core_id),
        remote(XTo.at[:, chunk_of(f ^ 1)], XTa.at[rows_of(f), tail], fs.at[1], fr.at[1], core_id),
        remote(XTo.at[:, shared], XTa.at[rows_of(f), shared], fs.at[2], fr.at[2], x_id),
        remote(XTo.at[:, chunk_of(f ^ 2)], XTa.at[rows_of(f), tail], fs.at[3], fr.at[3], x_id),
        remote(XTo.at[:, chunk_of(f ^ 3)], tmpq, fs.at[4], fr.at[4], x_id),
        remote(XTa.at[rows_of(f ^ 2), shared], XTa.at[rows_of(f ^ 2), shared], fs.at[5], fr.at[5], core_id),
        remote(tmpq, XTa.at[rows_of(f ^ 2), tail], fs.at[6], fr.at[6], core_id),
    ]
    for copy in feats[:5]:
        copy.start()
    XTa[rows_of(f), shared] = XTo[:, shared]
    XTa[rows_of(f), tail] = XTo[:, chunk_of(f)]

    for k in range(2 * S):
        su_ref[k] = 0
    for k in range(7 * S):
        kind_ref[k] = 0

    @pl.loop(0, U)
    def _(u):
        owner = own_ref[u]
        rank = lax.fori_loop(0, u, lambda j, total: total + jnp.where(own_ref[j] == owner, 1, 0), 0)
        distance = owner ^ r
        place = 0
        for bit in range(n):
            place = place + (((distance >> bit) & 1) << (n - 1 - bit))
        pos[u] = place * S + jnp.minimum(rank, S - 1)
        for k in range(2 * S):
            hit = jnp.where(owner == r ^ (k // S), 1, 0) * jnp.where(rank == k % S, 1, 0)
            su_ref[k] = su_ref[k] + hit * u
            here = hit * jnp.where((u % R) // (R // 2) == r % 2, 1, 0)
            late = here * jnp.where(u < R, 1, 0)
            if k < S:
                kind_ref[k] = kind_ref[k] + hit
            kind_ref[S + k] = kind_ref[S + k] + here
            kind_ref[3 * S + k] = kind_ref[3 * S + k] + here - late
            kind_ref[5 * S + k] = kind_ref[5 * S + k] + late

    hyper_arrive(0, 0)
    feats[2].wait_recv()
    feats[4].wait_recv()
    feats[5].start()
    feats[6].start()
    for j in range(1, n - 1):
        hyper_arrive(0, j)
        x_arrive(0, j - 1)
    send_own(1)
    for k in (0, 1, 3, 5, 6):
        feats[k].wait_recv()

    shift0 = small_ref[0:1]
    gain = small_ref[1:2]
    shift = small_ref[2:3]

    def norm(cols):
        h = dot(XTa[:, cols], XTa[:, pl.ds(2 * HALF, D)], TN) + shift0
        mean = jnp.mean(h, axis=-1, keepdims=True)
        cen = h - mean
        rstd = lax.rsqrt(jnp.mean(cen * cen, axis=-1, keepdims=True) + LN_EPS)
        nrm = cen * rstd
        return h, nrm, rstd, (nrm * gain + shift).astype(bf16)

    @pl.loop(0, 8)
    def _(i):
        rows = pl.ds(pl.multiple_of(i * QUART, QUART), QUART)
        h, nrm, rstd, act = norm(rows)
        n1s_ref[rows] = nrm.astype(bf16)
        a1s_ref[rows] = act
        rs_ref[rows] = jnp.broadcast_to(rstd, (QUART, 128))

        @pl.when(i % 4 == f)
        def _():
            h0_ref[pl.ds(pl.multiple_of((i // 4) * 512, 512), QUART)] = h

    hyper_arrive(0, n - 1)
    if n > 1:
        x_arrive(0, n - 2)

    @pl.loop(0, 2)
    def _(t):
        rows = pl.ds(pl.multiple_of(t * QUART, QUART), QUART)
        h, nrm, rstd, act = norm(pl.ds(pl.multiple_of(wide + t * QUART, QUART), QUART))
        n1q_ref[rows] = nrm.astype(bf16)
        a1q_ref[rows] = act
        rq_ref[rows] = jnp.broadcast_to(rstd, (QUART, 128))
        h0_ref[pl.ds(pl.multiple_of(t * 512 + QUART, QUART), QUART)] = h

    XT_ref[...] = XTa[...]
    hyper_arrive(1, 0)
    x_arrive(0, n - 1)
    scale = (HEAD_DIM**-0.5) * LOG2E

    def assemble(p):
        for u in range(U):
            place, rank = pos[u] // S, pos[u] % S
            for k in range(2):
                W[pl.ds(u * BR, BR), pl.ds(p * 256 + k * 128, 128)] = Gs[p][k, place, rank]

    def project(p):
        cols = pl.ds(p * 256, 256)
        for t in range(2):
            sup = pl.multiple_of(t * HALF + f * QUART, QUART)
            wq = W[pl.ds(0, D), cols]
            q_s[pl.ds(t * 512, QUART), cols] = (dot(a1s_ref[pl.ds(sup, QUART)], wq) * scale).astype(bf16)
            q_s[pl.ds(t * 512 + QUART, QUART), cols] = (dot(a1q_ref[pl.ds(t * QUART, QUART)], wq) * scale).astype(bf16)

        @pl.loop(0, 4)
        def _(i):
            rows = pl.ds(pl.multiple_of(i * 512, 512), 512)
            a = a1s_ref[rows]
            k = dot(a, W[pl.ds(D, D), cols]).astype(bf16)
            k_s[rows, cols] = k
            kT_s[cols, rows] = k.T
            v = dot(a, W[pl.ds(2 * D, D), cols]).astype(bf16)
            v_s[rows, cols] = v
            vT_s[cols, rows] = v.T

    def ecopy(i):
        return pltpu.make_async_copy(ET_s.at[i], ET.at[i], esem.at[i])

    def head(h):
        hs = pl.ds(h * HEAD_DIM, HEAD_DIM)
        for t in range(2):
            i = t * HEADS + h
            ks = pl.ds(t * HALF, HALF)
            qs = pl.ds(t * 512, 512)
            st = dot(k_s[ks, hs], q_s[qs, hs], NT)
            top = jnp.max(st, axis=0, keepdims=True)
            e = jnp.exp2(st - top)
            inv = 1.0 / jnp.sum(e, axis=0, keepdims=True)
            eb = e.astype(bf16)
            ET_s[i] = eb
            ecopy(i).start()
            linv[pl.ds(i, 1)] = inv
            ot = (dot(vT_s[hs, ks], eb) * inv).astype(bf16)
            OT_s[hs, qs] = ot
            O_s[qs, hs] = ot.T

    outs = []

    def ship(src, dst):
        copy = pltpu.make_async_copy(src, dst, osem.at[len(outs)])
        copy.start()
        outs.append(copy)

    all_here(0)
    assemble(0)
    for j in range(1, n - 1):
        hyper_arrive(1, j)
        x_arrive(1, j - 1)
    project(0)
    hyper_arrive(1, n - 1)
    if n > 1:
        x_arrive(1, n - 2)
    head(0)
    x_arrive(1, n - 1)
    head(1)
    all_here(1)
    assemble(1)
    ship(W, Wo)
    project(1)
    ship(q_s, qo)
    ship(kT_s, kTo)
    ship(v_s, vo)
    head(2)
    head(3)
    ship(O_s, Oo)
    ship(OT_s, OT)
    for copy in feats:
        copy.wait_send()
    all_sent(0)
    all_sent(1)
    for i in range(8):
        ecopy(i).wait()
    for copy in outs:
        copy.wait()


def gather_call(R, slots, features, masks, tmap, owners, emb, small):
    S, BR, W = slots.shape
    n = R.bit_length() - 1
    M = n * (n + 1) // 2
    dma = pltpu.SemaphoreType.DMA
    sem = dma((2, len(GROUPS), M))
    sd = jax.ShapeDtypeStruct
    V = pltpu.VMEM
    cols = 2 * HALF + D + 512
    half = V((2, R, S, BR, 128), bf16)
    return pl.pallas_call(
        functools.partial(gather_kernel, R),
        out_shape=(
            sd((2 * S,), jnp.int32), sd((7 * S,), jnp.int32), sd((4 * PADF, cols), bf16), sd((1024, D), f32),
            sd((2048, D), bf16), sd((512, D), bf16), sd((2048, D), bf16), sd((512, D), bf16),
            sd((2048, 128), f32), sd((512, 128), f32), sd((8, 512), f32),
            sd((12 * D, D), bf16), sd((1024, D), bf16), sd((D, 2048), bf16), sd((2048, D), bf16),
            sd((8, HALF, 512), bf16), sd((D, 1024), bf16), sd((1024, D), bf16),
        ),
        in_specs=[vmem(), vmem(), vmem(), smem(), smem(), vmem(), vmem()],
        out_specs=(smem(), smem()) + (vmem(),) * 9 + (anyspace(),) * 7,
        scratch_shapes=[
            pltpu.SMEM(owners.shape, jnp.int32), half, half, V((2, 2, S, BR, 128), bf16),
            V((PADF, 2 * HALF + D + 2048), bf16), V((4 * PADF, cols), bf16), V((PADF, 512), bf16),
            V((12 * D, D), bf16), V((1024, D), bf16), V((2048, D), bf16), V((D, 2048), bf16), V((2048, D), bf16),
            V((D, 2048), bf16), V((8, HALF, 512), bf16), V((D, 1024), bf16), V((1024, D), bf16),
            dma((2,)), dma((6,)), dma((8,)), dma((7,)), dma((7,)),
        ] + [sem] * 8,
        compiler_params=pltpu.CompilerParams(collective_id=0, has_side_effects=True, vmem_limit_bytes=VMEM_BYTES),
        name="gather",
    )(slots, features, masks, tmap, owners, emb, small)


def gelu_pair(u):
    den = 1.0 + (0.3275911 * math.sqrt(0.5)) * jnp.abs(u)
    t = pl.reciprocal(den, approx=True)
    t = t * (2.0 - den * t)
    ex = jnp.exp2((-0.5 * LOG2E) * (u * u))
    poly = t * (0.127414796 + t * (-0.142248368 + t * (0.7107068705 + t * (-0.7265760135 + t * 0.5307027145))))
    e = poly * ex
    phi = jnp.where(u >= 0, 1.0 - e, e)
    return u * phi, phi + u * ex * (1.0 / math.sqrt(2 * math.pi))


AFTER = {
    "fb0": (2, 3), "up": (2,), "mix": (3, 0, 1), "h01": (2,), "h10": (3,), "w0": (2, 0, 3), "h20": (4,),
    "h30": (1, 2, 0, 3), "b0": (4, 2, 1, 0), "b1": (5,), "b2": (3,), "b3": (2,), "b5": (4, 1), "b7": (0, 3), "b9": (4, 5, 1, 0),
}


def main_kernel(
    R, su, occ, linv, small, Wh, Oh, h0h, dYh, ETh, OTh, qh, kTh, vh, a1sh, a1qh, n1sh, n1qh, rsh, rqh, XTh,
    out, FIN, SM, EM, GI,
    W, O_s, y_s, dY, ETb, OT, qs, kT, a1q, n1s, n1q, rs, rq, XT,
    a2_s, G_s, dU_s, Dp, sg, eg, GT, S, RC, RX, RH, AG0, AG1, AGL, SY, RY, SEL, PK, RK, GC, XS, XR,
    lsem, esem, osem, ss, sr, ys, yr, fs, fr, ps, pr, gs, gr,
):
    f = lax.axis_index("feat")
    r = lax.axis_index("rows")
    x = f // 2
    c = f % 2
    n = R.bit_length() - 1
    BH = S.shape[4]
    per = D // (2 * BH)
    core_id = (f ^ 1, r)
    x_id = (f ^ 2, r)
    row_id = [(f, r ^ (1 << j)) for j in range(n)]
    peers = [core_id, x_id] + row_id
    bar = greet(peers)

    loads = {}

    def load(name, src, dst):
        loads[name] = pltpu.make_async_copy(src, dst, lsem.at[len(loads)])
        loads[name].start()

    def rows_w(i):
        return pl.ds(i * D, D)

    load("O", Oh, O_s)
    load("h0", h0h, y_s)
    for i in (3, 4, 8, 5, 9, 6, 10, 7, 11):
        load(i, Wh.at[rows_w(i)], W.at[rows_w(i)])
    load("dY", dYh, dY)
    load("OT", OTh, OT)
    load("q", qh, qs)
    load("kT", kTh, kT)

    def ecopy(h, t):
        k = (h % 2) * 2 + t
        return pltpu.make_async_copy(ETh.at[t * HEADS + h], ETb.at[k], esem.at[k])

    for h in range(2):
        for t in range(2):
            ecopy(h, t).start()
    load("a1q", a1qh, a1q)
    load("n1s", n1sh, n1s)
    load("n1q", n1qh, n1q)
    load("rs", rsh, rs)
    load("rq", rqh, rq)
    load("XT", XTh, XT)
    for i in range(3):
        load(i, Wh.at[rows_w(i)], W.at[rows_w(i)])
    pl.semaphore_wait(bar, len(peers))

    bits = [(r >> j) & 1 for j in range(n)]
    base = [0]
    for j in range(n):
        base.append(base[j] + bits[j] * (R >> (j + 1)))

    def core_copy(g):
        return remote(S.at[1 - c, :, g], RC.at[:, g], ss.at[g, 0], sr.at[g, 0], core_id)

    def x_copy(g):
        return remote(S.at[c, 1 - x, g], RX.at[g], ss.at[g, 1], sr.at[g, 1], x_id)

    def rs_copy(g, j):
        half = R >> (j + 1)
        away = base[j] + (1 - bits[j]) * half
        off = R - (R >> j)
        return remote(
            S.at[c, x, g, pl.ds(away, half)], RH.at[g, pl.ds(off, half)],
            ss.at[g, 2 + j], sr.at[g, 2 + j], row_id[j],
        )

    def swap_copy(g):
        span = pl.ds(base[n - 1], 2)
        return remote(S.at[c, x, g, span], RH.at[g, pl.ds(R - 2, 2)], ss.at[g, 1 + n], sr.at[g, 1 + n], row_id[n - 1])

    def total_of(g):
        return AGL if g == 5 else AG1.at[g // 2] if g % 2 else AG0.at[(g // 2 + 1) % 3]

    def ag_copy(g, j):
        ref = total_of(g).at[pl.ds(base[j + 1] - base[1], R >> (j + 1))]
        return remote(ref, ref, ss.at[g, 2 + n + j], sr.at[g, 2 + n + j], row_id[j])

    def add(a, b):
        return (a.astype(f32) + b.astype(f32)).astype(bf16)

    def step(g, stage):
        if stage == 0:
            core_copy(g).wait_recv()
            S[c, 1 - x, g] = add(S[c, 1 - x, g], RC[1 - x, g])
            x_copy(g).start()
            S[c, x, g] = add(S[c, x, g], RC[x, g])
        elif stage == 1:
            x_copy(g).wait_recv()
            S[c, x, g] = add(S[c, x, g], RX[g])
            rs_copy(g, 0).start()
        elif stage < 1 + n:
            j = stage - 2
            half = R >> (j + 1)
            off = R - (R >> j)
            rs_copy(g, j).wait_recv()
            keep = pl.ds(base[j + 1], half)
            S[c, x, g, keep] = add(S[c, x, g, keep], RH[g, pl.ds(off, half)])
            if j < n - 2:
                rs_copy(g, j + 1).start()
            else:
                swap_copy(g).start()
        elif stage == 1 + n:
            swap_copy(g).wait_recv()
            total_of(g)[pl.ds(base[n - 1] - base[1], 2)] = add(S[c, x, g, pl.ds(base[n - 1], 2)], RH[g, pl.ds(R - 2, 2)])
            if n > 2:
                ag_copy(g, n - 2).start()
        else:
            j = 2 * n - stage
            ag_copy(g, j).wait_recv()
            if j > 1:
                ag_copy(g, j - 1).start()

    def select(m, who):
        picked = []
        for s in range(4):
            u = su[who * 4 + s]
            p = lax.rem(u, R // 2)
            q = lax.div(u, R)
            k = who * 4 + s
            if m == 0:
                picked.append(AG0[q, p].astype(f32) * occ[4 + k].astype(f32))
            else:
                picked.append(AG1[lax.max(q - 1, 0), p].astype(f32) * occ[12 + k].astype(f32) + AGL[p].astype(f32) * occ[20 + k].astype(f32))
        return picked

    def y_copy(m):
        return remote(SY.at[m], RY.at[m], ys.at[m], yr.at[m], row_id[0])

    def fin(m, k):
        if k == 3:
            return pltpu.make_async_copy(SEL.at[m], FIN.at[m, f], osem.at[1 + m])
        src, at = (FIN.at[m, f ^ 2], f ^ 2) if k == 2 else (SEL.at[m], f)
        return remote(src, FIN.at[m, at], fs.at[m, k], fr.at[m, k], x_id if k == 1 else core_id)

    def fin_step(m, stage):
        if stage == 0:
            for s, value in enumerate(select(m, 1)):
                SY[m, s] = value.astype(bf16)
            y_copy(m).start()
            for s, value in enumerate(select(m, 0)):
                SEL[m, s] = value.astype(bf16)
        elif stage == 1:
            y_copy(m).wait_recv()
            SEL[m] = add(SEL[m], RY[m])
            for k in (1, 0, 3):
                fin(m, k).start()
        else:
            fin(m, 1).wait_recv()
            fin(m, 2).start()

    last = 2 * n
    done = [0] * 6
    ended = [0, 0]

    def tick(g):
        if done[g] < last:
            step(g, done[g])
            done[g] += 1

    def finish(m):
        if ended[m] < 3 and all(done[g] == last for g in (m, 2 + m, 4 + m)):
            fin_step(m, ended[m])
            ended[m] += 1

    def after(piece):
        for g in AFTER.get(piece, ()):
            tick(g)

    def put(g0, i, val):
        for k in range(val.shape[1] // 128):
            piece = val[:, k * 128:(k + 1) * 128].reshape(per, 2, BH, 128)
            for h in range(2):
                S[k % 2, h, g0 + k // 2, pl.ds(i * per, per)] = piece[:, h]

    gain2 = small[3:4]
    shift2 = small[4:5]
    RB = 256

    def norm2(y1):
        cen = y1 - jnp.mean(y1, axis=-1, keepdims=True)
        rstd = lax.rsqrt(jnp.mean(cen * cen, axis=-1, keepdims=True) + LN_EPS)
        return cen * rstd, rstd

    loads["O"].wait()
    loads["h0"].wait()
    loads[3].wait()

    @pl.loop(0, 1024 // RB)
    def _(i):
        rows = pl.ds(pl.multiple_of(i * RB, RB), RB)
        y1 = y_s[rows] + dot(O_s[rows], W[rows_w(3)])
        y_s[rows] = y1
        n2, _ = norm2(y1)
        a2 = (n2 * gain2 + shift2).astype(bf16)
        a2_s[rows] = a2
        acc = y1 + small[5:6]
        for j in range(4):
            @pl.when(i == 0)
            def _():
                loads[4 + j].wait()
                loads[8 + j].wait()
            gl, gp = gelu_pair(dot(a2, W[rows_w(4 + j)]) + small[6 + j:7 + j])
            gb = gl.astype(bf16)
            G_s[j, rows] = gb
            dU_s[j, rows] = gp.astype(bf16)
            acc = acc + dot(gb, W[rows_w(8 + j)])
        O_s[rows] = acc.astype(bf16)

    ship_out = pltpu.make_async_copy(O_s, out, osem.at[0])
    ship_out.start()
    loads["dY"].wait()
    for j in range(4):
        put(2, j, dot(G_s[j], dY[...], TN).astype(bf16))
    core_copy(2).start()
    core_copy(3).start()

    sg[...] = jnp.zeros_like(sg)

    def backward_rows(i):
        rows = pl.ds(i * RB, RB)
        dy = dY[rows]
        da2 = jnp.zeros((RB, D), f32)
        for j in range(4):
            du = (dot(dy, W[rows_w(8 + j)], NT) * dU_s[j, rows].astype(f32)).astype(bf16)
            dU_s[j, rows] = du
            sg[6 + j:7 + j] += jnp.sum(du.astype(f32), axis=0, keepdims=True)
            da2 = da2 + dot(du, W[rows_w(4 + j)], NT)
        n2, rstd = norm2(y_s[rows])
        dyf = dy.astype(f32)
        sg[3:4] += jnp.sum(da2 * n2, axis=0, keepdims=True)
        sg[4:5] += jnp.sum(da2, axis=0, keepdims=True)
        sg[5:6] += jnp.sum(dyf, axis=0, keepdims=True)
        cc = da2 * gain2
        m1 = jnp.mean(cc, axis=-1, keepdims=True)
        m2 = jnp.mean(cc * n2, axis=-1, keepdims=True)
        y_s[rows] = dyf + rstd * (cc - m1 - n2 * m2)

    for i in range(1024 // RB):
        backward_rows(i)
        after("fb%d" % i)
    vs = W.at[pl.ds(4 * D, 4 * D)]
    a1s = W.at[pl.ds(8 * D, 4 * D)]
    load("v", vh, vs)
    load("a1s", a1sh, a1s)
    for j in range(4):
        put(0, j, dot(a2_s[...], dU_s[j], TN).astype(bf16))
    core_copy(0).start()
    core_copy(1).start()
    after("up")

    scale = HEAD_DIM**-0.5
    for i in range(2):
        dU_s[1, pl.ds(i * 512, 512)] = y_s[pl.ds(i * 512, 512)].astype(bf16)
    for name in ("OT", "v", "q", "kT", "a1s", "a1q"):
        loads[name].wait()
    put(4, 3, dot(OT[...], dU_s[1]).astype(bf16))
    for t in range(2):
        cols = pl.ds(t * 512, 512)
        for h in range(HEADS):
            rows = pl.ds(h * HEAD_DIM, HEAD_DIM)
            d = dot(W[pl.ds(3 * D + h * HEAD_DIM, HEAD_DIM)], dU_s[1, cols], NT) * linv[pl.ds(t * HEADS + h, 1)]
            Dp[pl.ds(t * HEADS + h, 1)] = jnp.sum(d * OT[rows, cols].astype(f32), axis=0, keepdims=True)
            dU_s[2, pl.ds(t * 512 + h * HEAD_DIM, HEAD_DIM)] = d.astype(bf16)
    after("mix")

    def heads(h):
        hs = pl.ds(h * HEAD_DIM, HEAD_DIM)
        for t in range(2):
            ecopy(h, t).wait()
            i = t * HEADS + h
            ksl = pl.ds(t * HALF, HALF)
            qsl = pl.ds(t * 512, 512)
            do = dU_s[2, pl.ds(t * 512 + h * HEAD_DIM, HEAD_DIM)]
            dp = dot(vs[ksl, hs], do)
            e = ETb[(h % 2) * 2 + t]
            ds = (e.astype(f32) * (dp - Dp[pl.ds(i, 1)])).astype(bf16)
            G_s[2 + t, :, hs] = dot(e, do, NT).astype(bf16)
            G_s[t, :, hs] = (dot(ds, qs[qsl, hs]) * (1.0 / LOG2E)).astype(bf16)
            dqT = (dot(kT[hs, ksl], ds) * scale).astype(bf16)
            dU_s[0, qsl, hs] = dqT.T
            if h + 2 < HEADS:
                ecopy(h + 2, t).start()
            after("h%d%d" % (h, t))

    def weight_grads(m):
        cols = pl.ds(m * 256, 256)
        acc = jnp.zeros((D, 256), f32)
        for t in range(2):
            sup = pl.multiple_of(t * HALF + f * QUART, QUART)
            acc += dot(a1s[pl.ds(sup, QUART)], dU_s[0, pl.ds(t * 512, QUART), cols], TN)
            acc += dot(a1q[pl.ds(t * QUART, QUART)], dU_s[0, pl.ds(t * 512 + QUART, QUART), cols], TN)
        put(4 + m, 0, acc.astype(bf16))
        for k in range(2):
            total = dot(a1s[pl.ds(0, HALF)], G_s[2 * k, :, cols], TN) + dot(a1s[pl.ds(HALF, HALF)], G_s[2 * k + 1, :, cols], TN)
            put(4 + m, 1 + k, total.astype(bf16))

    for m in range(2):
        heads(2 * m)
        heads(2 * m + 1)
        weight_grads(m)
        core_copy(4 + m).start()
        after("w%d" % m)

    eg[...] = jnp.zeros_like(eg)
    gain1 = small[1:2]
    emb_cols = pl.ds(2 * HALF, D)
    for name in ("n1s", "n1q", "rs", "rq", "XT", 0, 1, 2):
        loads[name].wait()

    def back(da, nrm, rstd, extra, cols, out_cols):
        sg[1:2] += jnp.sum(da * nrm, axis=0, keepdims=True)
        sg[2:3] += jnp.sum(da, axis=0, keepdims=True)
        cc = da * gain1
        m1 = jnp.mean(cc, axis=-1, keepdims=True)
        m2 = jnp.mean(cc * nrm, axis=-1, keepdims=True)
        wide = jnp.concatenate([rstd] * 4, axis=1)
        dh = wide * (cc - m1 - nrm * m2)
        if extra is not None:
            dh = dh + extra
        sg[0:1] += jnp.sum(dh, axis=0, keepdims=True)
        de = dh.astype(bf16)
        part = dot(XT[:, cols], de)
        back_in = dot(XT[:, emb_cols], de, NT).astype(bf16)
        for k in range(4):
            eg[k] += part[k * PADF:(k + 1) * PADF]
            GT[k % 2, k // 2, :, out_cols] = back_in[k * PADF:(k + 1) * PADF]

    def below(t):
        q0 = t * 512
        wq, wk, wv = W[rows_w(0)], W[rows_w(1)], W[rows_w(2)]
        da = dot(dU_s[0, pl.ds(q0 + QUART, QUART)], wq, NT)
        p0 = pl.ds(t * QUART, QUART)
        back(
            da, n1q[p0].astype(f32), rq[p0], y_s[pl.ds(q0 + QUART, QUART)],
            pl.ds(2 * HALF + D + t * QUART, QUART), pl.ds(2 * HALF + t * QUART, QUART),
        )
        after("b%d" % (5 * t))
        for b in range(4):
            at = pl.ds(pl.multiple_of(((f + b) % 4) * QUART, QUART), QUART)
            rows = pl.ds(pl.multiple_of(t * HALF + ((f + b) % 4) * QUART, QUART), QUART)
            da = dot(G_s[t, at], wk, NT) + dot(G_s[2 + t, at], wv, NT)
            extra = None
            if b == 0:
                da = da + dot(dU_s[0, pl.ds(q0, QUART)], wq, NT)
                extra = y_s[pl.ds(q0, QUART)]
            back(da, n1s[rows].astype(f32), rs[rows], extra, rows, rows)
            if 5 * t + b < 8:
                after("b%d" % (5 * t + b + 1))

    below(0)
    below(1)

    small_rows = pl.ds(0, 16)
    PK[0, small_rows] = sg[...]
    for k in range(2):
        PK[0, pl.ds(16 + k * PADF, PADF)] = eg[2 * k + 1 - c]

    def pk_copy(i):
        rows = pl.ds(0, 80 if i == 0 else 48)
        dev = core_id if i == 0 else x_id if i == 1 else row_id[i - 2]
        return remote(PK.at[i, rows], RK.at[i, rows], ps.at[i], pr.at[i], dev)

    def pk_step(i):
        pk_copy(i).wait_recv()
        if i == 0:
            PK[1, small_rows] = PK[0, small_rows] + RK[0, small_rows]
            own = [eg[2 * k + c] + RK[0, pl.ds(16 + k * PADF, PADF)] for k in range(2)]
            PK[1, pl.ds(16, PADF)] = jnp.where(x == 0, own[1], own[0])
            PK[1, pl.ds(48, PADF)] = jnp.where(x == 0, own[0], own[1])
            pk_copy(1).start()
        else:
            old = PK[1, pl.ds(48, PADF)] if i == 1 else PK[i, pl.ds(16, PADF)]
            a = PK[i, small_rows] + RK[i, small_rows]
            b = old + RK[i, pl.ds(16, PADF)]
            if i < n + 1:
                PK[i + 1, small_rows] = a
                PK[i + 1, pl.ds(16, PADF)] = b
                pk_copy(i + 1).start()
            else:
                SM[...] = a
                EM[...] = b

    pk_copy(0).start()
    gt1 = remote(GT.at[1 - c], GC, gs.at[0], gr.at[0], core_id)
    gt1.start()
    sup = pl.ds(0, 2 * HALF)
    que = pl.ds(2 * HALF, 512)

    def que_of(k):
        return pl.ds(pl.multiple_of(2 * HALF + k * 512, 512), 512)

    gt2 = remote(XS, XR, gs.at[1], gr.at[1], x_id)
    after("b9")
    pk_step(0)
    gt1.wait_recv()
    XS[:, sup] = add(GT[c, 1 - x, :, sup], GC[1 - x, :, sup])
    XS[:, que_of(c)] = GT[c, 1 - x, :, que]
    XS[:, que_of(1 - c)] = GC[1 - x, :, que]
    gt2.start()
    next_pk = 1
    while min(done) < last:
        for g in (4, 5, 2, 3, 1, 0):
            tick(g)
        finish(0)
        if next_pk < n + 2:
            pk_step(next_pk)
            next_pk += 1
    finish(1)
    finish(0)
    for i in range(next_pk, n + 2):
        pk_step(i)
    gt2.wait_recv()
    GI[:, sup] = (
        GT[c, x, :, sup].astype(f32) + GC[x, :, sup].astype(f32) + XR[:, sup].astype(f32)
    ).astype(bf16)
    GI[:, que_of(f)] = GT[c, x, :, que]
    GI[:, que_of(f ^ 1)] = GC[x, :, que]
    for k in range(2):
        GI[:, que_of(2 * (1 - x) + k)] = XR[:, pl.ds(2 * HALF + k * 512, 512)]
    while min(ended) < 3:
        finish(0)
        finish(1)
    for m in range(2):
        y_copy(m).wait_send()
        fin(m, 0).wait()
        fin(m, 1).wait_send()
        fin(m, 2).wait()
        fin(m, 3).wait()
    for g in range(6):
        core_copy(g).wait_send()
        x_copy(g).wait_send()
        swap_copy(g).wait_send()
        for j in range(n - 1):
            rs_copy(g, j).wait_send()
        for j in range(1, n - 1):
            ag_copy(g, j).wait_send()
    for i in range(n + 2):
        pk_copy(i).wait_send()
    gt1.wait_send()
    gt2.wait_send()
    ship_out.wait()


def main_call(R, su, occ, linv, small, W, O, h0, dY, ET, OT, q, kT, v, a1s, a1q, n1s, n1q, rs, rq, XT):
    BH = 12 * D // (3 * R) // 2
    n = R.bit_length() - 1
    sd = jax.ShapeDtypeStruct
    V = pltpu.VMEM
    dma = pltpu.SemaphoreType.DMA
    blk = (R, BH, 128)
    like = lambda a: V(a.shape, a.dtype)
    return pl.pallas_call(
        functools.partial(main_kernel, R),
        out_shape=(sd((1024, D), bf16), sd((2, 4, 4, BH, 128), bf16), sd((16, D), f32), sd((PADF, D), f32), sd((PADF, 4096), bf16)),
        in_specs=[smem(), smem(), vmem(), vmem()] + [anyspace()] * 16,
        out_specs=(anyspace(), anyspace(), vmem(), vmem(), vmem()),
        scratch_shapes=[
            like(W), like(O), like(h0), like(dY), V((4, HALF, 512), bf16), like(OT), like(q), like(kT),
            like(a1q), like(n1s), like(n1q), like(rs), like(rq), like(XT),
            V((1024, D), bf16), V((4, 1024, 512), bf16), V((4, 1024, 512), bf16), V((8, 512), f32), V((16, D), f32),
            V((4, PADF, D), f32), V((2, 2, PADF, 2560), bf16),
            V((2, 2, 6) + blk, bf16), V((2, 6) + blk, bf16), V((6,) + blk, bf16), V((6,) + blk, bf16), V((3, R // 2, BH, 128), bf16), V((2, R // 2, BH, 128), bf16), V((R // 2, BH, 128), bf16),
            V((2, 4, BH, 128), bf16), V((2, 4, BH, 128), bf16), V((2, 4, BH, 128), bf16), V((n + 2, 80, D), f32), V((n + 2, 80, D), f32),
            V((2, PADF, 2560), bf16), V((PADF, 3072), bf16), V((PADF, 3072), bf16),
            dma((26,)), dma((4,)), dma((3,)), dma((6, 2 + 2 * n)), dma((6, 2 + 2 * n)), dma((2,)), dma((2,)), dma((2, 3)), dma((2, 3)),
            dma((n + 2,)), dma((n + 2,)), dma((2,)), dma((2,)),
        ],
        compiler_params=pltpu.CompilerParams(collective_id=1, has_side_effects=True, vmem_limit_bytes=VMEM_BYTES),
        name="main",
    )(su, occ, linv, small, W, O, h0, dY, ET, OT, q, kT, v, a1s, a1q, n1s, n1q, rs, rq, XT)


def adamw(weight, grad, first, second, rate):
    first_new = BETA_FIRST * first + (1.0 - BETA_FIRST) * grad
    second_new = BETA_SECOND * second + (1.0 - BETA_SECOND) * grad * grad
    first_hat = first_new / (1.0 - BETA_FIRST**STEP)
    second_hat = second_new / (1.0 - BETA_SECOND**STEP)
    weight_new = weight - rate * (first_hat / (jnp.sqrt(second_hat) + ADAM_EPS) + DECAY * weight)
    return (first_new, second_new, weight_new)


def update_kernel(
    occ, tmap, FIN, w, m, v, SM, sw, sm, sv, EM, ew, em, ev, GI, masks, lo,
    g_o, m_o, v_o, w_o, wc_o, eg_o, em_o, ev_o, ew_o, ec_o, sg_o, sm_o, sv_o, sw_o, gi_o, lo_o,
):
    s = pl.program_id(0)
    keep = occ[s].astype(f32)
    BH = FIN.shape[3]
    for f in range(4):
        rows = pl.ds((f // 2) * BH, BH)
        for k in range(2):
            cols = pl.ds(k * 256 + (f % 2) * 128, 128)
            g = FIN[k, f, 0].astype(f32)
            a, b, d = adamw(w[0, rows, cols], g, m[0, rows, cols], v[0, rows, cols], RATE_MATRIX)
            g_o[0, rows, cols] = g * keep
            m_o[0, rows, cols] = a * keep
            v_o[0, rows, cols] = b * keep
            d = d * keep
            w_o[0, rows, cols] = d
            wc_o[0, rows, cols] = d.astype(bf16)

    @pl.when(s == 0)
    def _():
        g = SM[0:10]
        a, b, d = adamw(sw[...], g, sm[...], sv[...], RATE_SMALL)
        sg_o[...] = g
        sm_o[...] = a
        sv_o[...] = b
        sw_o[...] = d
        nf = ew.shape[0]
        g = EM[pl.ds(0, nf)]
        a, b, d = adamw(ew[...], g, em[...], ev[...], RATE_EMBED)
        eg_o[...] = g
        em_o[...] = a
        ev_o[...] = b
        ew_o[...] = d
        ec_o[...] = d.astype(bf16)

    nf = gi_o.shape[1]
    t = s // 2
    keep_in = mask_column(masks, tmap[t])

    @pl.when(s % 2 == 0)
    def _():
        cols = pl.ds(pl.multiple_of(t * HALF, HALF), HALF)
        gi_o[t, :, 0, :] = (GI[pl.ds(0, nf), cols].astype(f32) * keep_in).astype(bf16)

    @pl.when(s % 2 == 1)
    def _():
        for k in range(4):
            cols = pl.ds(pl.multiple_of(2 * HALF + k * 512 + t * QUART, QUART), QUART)
            gi_o[t, :, 1, pl.ds(k * QUART, QUART)] = (GI[pl.ds(0, nf), cols].astype(f32) * keep_in).astype(bf16)

    lo_o[...] = lo[...]


def update_call(occ, tmap, FIN, w, m, v, SM, sw, sm, sv, EM, ew, em, ev, GI, masks, lo):
    S, BR, W = w.shape
    nf = ew.shape[0]
    sd = jax.ShapeDtypeStruct
    blk = pl.BlockSpec((1, BR, W), lambda s: (s, 0, 0))
    whole = lambda a: pl.BlockSpec(a.shape, lambda s: (0,) * len(a.shape))
    ins = [smem(), smem(), pl.BlockSpec((2, 4, 1, BR // 2, 128), lambda s: (0, 0, s, 0, 0)), blk, blk, blk]
    ins += [whole(a) for a in (SM, sw, sm, sv, EM, ew, em, ev, GI, masks)] + [pl.BlockSpec((1024 // S, D), lambda s: (s, 0))]
    big = sd((S, BR, W), f32)
    small = sd((10, D), f32)
    e = sd((nf, D), f32)
    outs = [big, big, big, big, sd((S, BR, W), bf16), e, e, e, e, sd((nf, D), bf16), small, small, small, small, sd((2, nf, 2, HALF), bf16), sd(lo.shape, lo.dtype)]
    specs = [blk] * 5 + [whole(a) for a in outs[5:14]] + [whole(outs[14]), pl.BlockSpec((1024 // S, D), lambda s: (s, 0))]
    return pl.pallas_call(
        update_kernel, out_shape=tuple(outs), grid=(S,), in_specs=ins, out_specs=tuple(specs),
        compiler_params=pltpu.CompilerParams(vmem_limit_bytes=VMEM_BYTES), name="update",
    )(occ, tmap, FIN, w, m, v, SM, sw, sm, sv, EM, ew, em, ev, GI, masks, lo)


def body(
    features, feature_masks, table_map, owners, out_grad, weight_slots, moment1_slots, moment2_slots,
    emb_weight, emb_moment1, emb_moment2, small_weight, small_moment1, small_moment2,
):
    width = weight_slots.shape[2]
    R = lax.axis_size("rows")
    slot_unit, kinds, XT, h0o, a1s, a1q, n1s, n1q, rs, rq, linv, W, q, kT, v, ET, OT, O = gather_call(
        R, weight_slots, features.transpose(0, 3, 1, 2), feature_masks, table_map, owners, emb_weight, small_weight
    )
    dY = out_grad.reshape(1024, width)
    out, FIN, SM, EM, GI = main_call(
        R, slot_unit, kinds, linv, small_weight, W, O, h0o, dY, ET, OT, q, kT, v, a1s, a1q, n1s, n1q, rs, rq, XT
    )
    (
        g_slots, m_slots, v_slots, w_slots, w_copy, e_grad, e_m, e_v, e_w, e_copy, s_grad, s_m, s_v, s_w, grad_inputs, out,
    ) = update_call(
        kinds, table_map, FIN, weight_slots, moment1_slots, moment2_slots, SM, small_weight, small_moment1,
        small_moment2, EM, emb_weight, emb_moment1, emb_moment2, GI, feature_masks, out,
    )
    grad_inputs = grad_inputs.transpose(0, 2, 3, 1)
    return (
        out.reshape(out_grad.shape), grad_inputs, g_slots, m_slots, v_slots, w_slots, w_copy,
        e_grad, e_m, e_v, e_w, e_copy, s_grad, s_m, s_v, s_w,
    )


def solution(mesh):
    rows3 = P("rows", None, None)
    feat2 = P("feat", None)
    in_specs = (
        P("rows", None, None, "feat"), P(None, "feat"), P("rows"), P(), P("rows", None, "feat", None),
        rows3, rows3, rows3, feat2, feat2, feat2, P(), P(), P(),
    )
    out_specs = (
        P("rows", None, "feat", None), P("rows", None, None, "feat"), rows3, rows3, rows3, rows3, rows3,
        feat2, feat2, feat2, feat2, feat2, P(), P(), P(), P(),
    )
    return jax.shard_map(body, mesh=mesh, in_specs=in_specs, out_specs=out_specs, check_vma=False)
```

```python
import functools
import math

import jax
import jax.numpy as jnp
from jax import lax
from jax.experimental import pallas as pl
from jax.experimental.pallas import tpu as pltpu
from jax.sharding import PartitionSpec as P

MESH = pl.DeviceIdType.MESH
bf16, f32 = jnp.bfloat16, jnp.float32
NN = (((1,), (0,)), ((), ()))
NT = (((1,), (1,)), ((), ()))
TN = (((0,), (0,)), ((), ()))
LOG2E = math.log2(math.e)
HEADS = 4
HEAD_DIM = 128
STEP = 10
LN_EPS = 1e-05
BETA_FIRST = 0.9
BETA_SECOND = 0.999
ADAM_EPS = 1e-08
DECAY = 0.01
RATE_MATRIX = 0.1
RATE_EMBED = 0.3
RATE_SMALL = 0.6
D = 512
HALF = 1024
QUART = 256
PADF = 32
VMEM_BYTES = 60 * 2**20


def dot(a, b, dims=NN):
    return lax.dot_general(a, b, dims, preferred_element_type=f32)


def vmem():
    return pl.BlockSpec(memory_space=pltpu.VMEM)


def anyspace():
    return pl.BlockSpec(memory_space=pl.ANY)


def smem():
    return pl.BlockSpec(memory_space=pltpu.SMEM)


def remote(src, dst, send, recv, dev):
    return pltpu.make_async_remote_copy(
        src_ref=src, dst_ref=dst, send_sem=send, recv_sem=recv, device_id=dev, device_id_type=MESH
    )


def greet(peers):
    bar = pltpu.get_barrier_semaphore()
    for d in peers:
        pl.semaphore_signal(bar, inc=1, device_id=d, device_id_type=MESH)
    return bar


def mask_column(masks, table):
    T, nf = masks.shape
    which = lax.broadcasted_iota(jnp.int32, (T, nf), 0) == table
    line = jnp.sum(jnp.where(which, masks[...], 0), axis=0, keepdims=True)
    eye = lax.broadcasted_iota(jnp.int32, (nf, nf), 0) == lax.broadcasted_iota(jnp.int32, (nf, nf), 1)
    return jnp.sum(jnp.where(eye, jnp.broadcast_to(line, (nf, nf)), 0), axis=1, keepdims=True).astype(f32)


GROUPS = (True, False)


def gather_kernel(
    R, slots_ref, feat_ref, mask_ref, tmap_ref, own_ref, emb_ref, small_ref,
    su_ref, kind_ref, XT_ref, h0_ref, a1s_ref, a1q_ref, n1s_ref, n1q_ref, rs_ref, rq_ref, linv,
    Wo, qo, kTo, vo, ET, OT, Oo,
    pos, G0, G1, own, XTo, XTa, tmpq, W, q_s, k_s, kT_s, v_s, vT_s, ET_s, OT_s, O_s,
    lsem, osem, esem, fs, fr, hs, hr, xs, xr, cs, cr, c2s, c2r,
):
    f = lax.axis_index("feat")
    r = lax.axis_index("rows")
    x = f // 2
    c = f % 2
    n = R.bit_length() - 1
    S, BR = slots_ref.shape[:2]
    U = own_ref.shape[0]
    BH = BR // 2
    Gs = (G0, G1)
    core_id = (f ^ 1, r)
    x_id = (f ^ 2, r)
    row_id = [(f, r ^ (1 << (n - 1 - j))) for j in range(n)]
    peers = [core_id, x_id] + row_id
    bar = greet(peers)
    for k in range(4):
        own[k // 2, k % 2] = slots_ref[:, :, k * 128:(k + 1) * 128].astype(bf16)
    pl.semaphore_wait(bar, len(peers))

    def keep_own(p):
        return pltpu.make_async_copy(own.at[p], Gs[p].at[:, 0], lsem.at[p])

    subs = [(j, g) for j in range(n) for g in range(-1, j)]
    index = {jg: i for i, jg in enumerate(subs)}
    rows_c = pl.ds(pl.multiple_of(c * BH, BH), BH)

    def part(p, s, half, start, size):
        if GROUPS[s]:
            return Gs[p].at[half, pl.ds(start, size), pl.ds(1, 3), rows_c]
        return Gs[p].at[:, pl.ds(start, size), 0, rows_c]

    def hyper(p, s, j, g):
        k = index[(j, g)]
        if g < 0:
            if GROUPS[s]:
                src, dst = own.at[p, x, pl.ds(1, 3), rows_c], Gs[p].at[x, 1 << j, pl.ds(1, 3), rows_c]
            else:
                src, dst = own.at[p, :, 0, rows_c], Gs[p].at[:, 1 << j, 0, rows_c]
        else:
            src, dst = part(p, s, x, 1 << g, 1 << g), part(p, s, x, (1 << j) + (1 << g), 1 << g)
        return remote(src, dst, hs.at[p, s, k], hr.at[p, s, k], row_id[j])

    def forward(p, s, j, g, half, sems, semr, dev):
        start, size = (0, 1) if g < 0 else (1 << g, 1 << g)
        k = index[(j, g)]
        ref = part(p, s, half, (1 << j) + start, size)
        return remote(ref, ref, sems.at[p, s, k], semr.at[p, s, k], dev)

    def to_x(p, s, j, g):
        return forward(p, s, j, g, x, xs, xr, x_id)

    def to_core(p, s, j, g):
        return forward(p, s, j, g, x, cs, cr, core_id)

    def to_core_x(p, s, j, g):
        return forward(p, s, j, g, 1 - x, c2s, c2r, core_id)

    order = range(len(GROUPS))

    def send_own(p):
        for s in order:
            for j in range(n):
                hyper(p, s, j, -1).start()
        keep_own(p).start()

    def x_arrive(p, j):
        for s in order:
            if GROUPS[s]:
                for g in range(-1, j):
                    to_x(p, s, j, g).wait_recv()
                    to_core_x(p, s, j, g).start()

    def hyper_arrive(p, j):
        for s in order:
            for g in range(-1, j):
                hyper(p, s, j, g).wait_recv()
                if GROUPS[s]:
                    to_x(p, s, j, g).start()
                to_core(p, s, j, g).start()
            for j2 in range(j + 1, n):
                hyper(p, s, j2, j).start()

    def all_here(p):
        keep_own(p).wait()
        for s in order:
            for j, g in subs:
                to_core(p, s, j, g).wait_recv()
                if GROUPS[s]:
                    to_core_x(p, s, j, g).wait_recv()

    def all_sent(p):
        for s in order:
            for j, g in subs:
                hyper(p, s, j, g).wait_send()
                to_core(p, s, j, g).wait_send()
                if GROUPS[s]:
                    to_x(p, s, j, g).wait_send()
                    to_core_x(p, s, j, g).wait_send()

    send_own(0)

    nf = feat_ref.shape[1]
    XTo[...] = jnp.zeros_like(XTo)
    for t in range(2):
        keep = mask_column(mask_ref, tmap_ref[t])
        XTo[pl.ds(0, nf), pl.ds(t * HALF, HALF)] = (feat_ref[t, :, 0, :].astype(f32) * keep).astype(bf16)
        query = (feat_ref[t, :, 1, :].astype(f32) * keep).astype(bf16)
        for k in range(4):
            XTo[pl.ds(0, nf), pl.ds(2 * HALF + D + k * 512 + t * QUART, QUART)] = query[:, k * QUART:(k + 1) * QUART]
    XTo[pl.ds(0, nf), pl.ds(2 * HALF, D)] = emb_ref[...].astype(bf16)
    wide = 2 * HALF + D
    shared = pl.ds(0, wide)
    tail = pl.ds(wide, 512)

    def rows_of(dev):
        return pl.ds(pl.multiple_of(dev * PADF, PADF), PADF)

    def chunk_of(dev):
        return pl.ds(pl.multiple_of(wide + dev * 512, 512), 512)

    feats = [
        remote(XTo.at[:, shared], XTa.at[rows_of(f), shared], fs.at[0], fr.at[0], core_id),
        remote(XTo.at[:, chunk_of(f ^ 1)], XTa.at[rows_of(f), tail], fs.at[1], fr.at[1], core_id),
        remote(XTo.at[:, shared], XTa.at[rows_of(f), shared], fs.at[2], fr.at[2], x_id),
        remote(XTo.at[:, chunk_of(f ^ 2)], XTa.at[rows_of(f), tail], fs.at[3], fr.at[3], x_id),
        remote(XTo.at[:, chunk_of(f ^ 3)], tmpq, fs.at[4], fr.at[4], x_id),
        remote(XTa.at[rows_of(f ^ 2), shared], XTa.at[rows_of(f ^ 2), shared], fs.at[5], fr.at[5], core_id),
        remote(tmpq, XTa.at[rows_of(f ^ 2), tail], fs.at[6], fr.at[6], core_id),
    ]
    for copy in feats[:5]:
        copy.start()
    XTa[rows_of(f), shared] = XTo[:, shared]
    XTa[rows_of(f), tail] = XTo[:, chunk_of(f)]

    for k in range(2 * S):
        su_ref[k] = 0
    for k in range(7 * S):
        kind_ref[k] = 0

    @pl.loop(0, U)
    def _(u):
        owner = own_ref[u]
        rank = lax.fori_loop(0, u, lambda j, total: total + jnp.where(own_ref[j] == owner, 1, 0), 0)
        distance = owner ^ r
        place = 0
        for bit in range(n):
            place = place + (((distance >> bit) & 1) << (n - 1 - bit))
        pos[u] = place * S + jnp.minimum(rank, S - 1)
        for k in range(2 * S):
            hit = jnp.where(owner == r ^ (k // S), 1, 0) * jnp.where(rank == k % S, 1, 0)
            su_ref[k] = su_ref[k] + hit * u
            here = hit * jnp.where((u % R) // (R // 2) == r % 2, 1, 0)
            late = here * jnp.where(u < R, 1, 0)
            if k < S:
                kind_ref[k] = kind_ref[k] + hit
            kind_ref[S + k] = kind_ref[S + k] + here
            kind_ref[3 * S + k] = kind_ref[3 * S + k] + here - late
            kind_ref[5 * S + k] = kind_ref[5 * S + k] + late

    hyper_arrive(0, 0)
    feats[2].wait_recv()
    feats[4].wait_recv()
    feats[5].start()
    feats[6].start()
    for j in range(1, n - 1):
        hyper_arrive(0, j)
        x_arrive(0, j - 1)
    send_own(1)
    for k in (0, 1, 3, 5, 6):
        feats[k].wait_recv()

    shift0 = small_ref[0:1]
    gain = small_ref[1:2]
    shift = small_ref[2:3]

    def norm(cols):
        h = dot(XTa[:, cols], XTa[:, pl.ds(2 * HALF, D)], TN) + shift0
        mean = jnp.mean(h, axis=-1, keepdims=True)
        cen = h - mean
        rstd = lax.rsqrt(jnp.mean(cen * cen, axis=-1, keepdims=True) + LN_EPS)
        nrm = cen * rstd
        return h, nrm, rstd, (nrm * gain + shift).astype(bf16)

    @pl.loop(0, 8)
    def _(i):
        rows = pl.ds(pl.multiple_of(i * QUART, QUART), QUART)
        h, nrm, rstd, act = norm(rows)
        n1s_ref[rows] = nrm.astype(bf16)
        a1s_ref[rows] = act
        rs_ref[rows] = jnp.broadcast_to(rstd, (QUART, 128))

        @pl.when(i % 4 == f)
        def _():
            h0_ref[pl.ds(pl.multiple_of((i // 4) * 512, 512), QUART)] = h

    hyper_arrive(0, n - 1)
    if n > 1:
        x_arrive(0, n - 2)

    @pl.loop(0, 2)
    def _(t):
        rows = pl.ds(pl.multiple_of(t * QUART, QUART), QUART)
        h, nrm, rstd, act = norm(pl.ds(pl.multiple_of(wide + t * QUART, QUART), QUART))
        n1q_ref[rows] = nrm.astype(bf16)
        a1q_ref[rows] = act
        rq_ref[rows] = jnp.broadcast_to(rstd, (QUART, 128))
        h0_ref[pl.ds(pl.multiple_of(t * 512 + QUART, QUART), QUART)] = h

    XT_ref[...] = XTa[...]
    hyper_arrive(1, 0)
    x_arrive(0, n - 1)
    scale = (HEAD_DIM**-0.5) * LOG2E

    def assemble(p):
        for u in range(U):
            place, rank = pos[u] // S, pos[u] % S
            for k in range(2):
                W[pl.ds(u * BR, BR), pl.ds(p * 256 + k * 128, 128)] = Gs[p][k, place, rank]

    def project(p):
        cols = pl.ds(p * 256, 256)
        for t in range(2):
            sup = pl.multiple_of(t * HALF + f * QUART, QUART)
            wq = W[pl.ds(0, D), cols]
            q_s[pl.ds(t * 512, QUART), cols] = (dot(a1s_ref[pl.ds(sup, QUART)], wq) * scale).astype(bf16)
            q_s[pl.ds(t * 512 + QUART, QUART), cols] = (dot(a1q_ref[pl.ds(t * QUART, QUART)], wq) * scale).astype(bf16)

        @pl.loop(0, 4)
        def _(i):
            rows = pl.ds(pl.multiple_of(i * 512, 512), 512)
            a = a1s_ref[rows]
            k = dot(a, W[pl.ds(D, D), cols]).astype(bf16)
            k_s[rows, cols] = k
            kT_s[cols, rows] = k.T
            v = dot(a, W[pl.ds(2 * D, D), cols]).astype(bf16)
            v_s[rows, cols] = v
            vT_s[cols, rows] = v.T

    def ecopy(i):
        return pltpu.make_async_copy(ET_s.at[i], ET.at[i], esem.at[i])

    def head(h):
        hs = pl.ds(h * HEAD_DIM, HEAD_DIM)

        @pl.loop(0, 2)
        def _(t):
            i = t * HEADS + h
            ks = pl.ds(pl.multiple_of(t * HALF, HALF), HALF)
            qs = pl.ds(pl.multiple_of(t * 512, 512), 512)
            st = dot(k_s[ks, hs], q_s[qs, hs], NT)
            top = jnp.max(st, axis=0, keepdims=True)
            e = jnp.exp2(st - top)
            inv = 1.0 / jnp.sum(e, axis=0, keepdims=True)
            eb = e.astype(bf16)
            ET_s[i] = eb
            ecopy(i).start()
            linv[pl.ds(i, 1)] = inv
            ot = (dot(vT_s[hs, ks], eb) * inv).astype(bf16)
            OT_s[hs, qs] = ot
            O_s[qs, hs] = ot.T

    outs = []

    def ship(src, dst):
        copy = pltpu.make_async_copy(src, dst, osem.at[len(outs)])
        copy.start()
        outs.append(copy)

    all_here(0)
    assemble(0)
    for j in range(1, n - 1):
        hyper_arrive(1, j)
        x_arrive(1, j - 1)
    project(0)
    hyper_arrive(1, n - 1)
    if n > 1:
        x_arrive(1, n - 2)
    head(0)
    x_arrive(1, n - 1)
    head(1)
    all_here(1)
    assemble(1)
    ship(W, Wo)
    project(1)
    ship(q_s, qo)
    ship(kT_s, kTo)
    ship(v_s, vo)
    head(2)
    head(3)
    ship(O_s, Oo)
    ship(OT_s, OT)
    for copy in feats:
        copy.wait_send()
    all_sent(0)
    all_sent(1)
    for i in range(8):
        ecopy(i).wait()
    for copy in outs:
        copy.wait()


def gather_call(R, slots, features, masks, tmap, owners, emb, small):
    S, BR, W = slots.shape
    n = R.bit_length() - 1
    M = n * (n + 1) // 2
    dma = pltpu.SemaphoreType.DMA
    sem = dma((2, len(GROUPS), M))
    sd = jax.ShapeDtypeStruct
    V = pltpu.VMEM
    cols = 2 * HALF + D + 512
    half = V((2, R, S, BR, 128), bf16)
    return pl.pallas_call(
        functools.partial(gather_kernel, R),
        out_shape=(
            sd((2 * S,), jnp.int32), sd((7 * S,), jnp.int32), sd((4 * PADF, cols), bf16), sd((1024, D), f32),
            sd((2048, D), bf16), sd((512, D), bf16), sd((2048, D), bf16), sd((512, D), bf16),
            sd((2048, 128), f32), sd((512, 128), f32), sd((8, 512), f32),
            sd((12 * D, D), bf16), sd((1024, D), bf16), sd((D, 2048), bf16), sd((2048, D), bf16),
            sd((8, HALF, 512), bf16), sd((D, 1024), bf16), sd((1024, D), bf16),
        ),
        in_specs=[vmem(), vmem(), vmem(), smem(), smem(), vmem(), vmem()],
        out_specs=(smem(), smem()) + (vmem(),) * 9 + (anyspace(),) * 7,
        scratch_shapes=[
            pltpu.SMEM(owners.shape, jnp.int32), half, half, V((2, 2, S, BR, 128), bf16),
            V((PADF, 2 * HALF + D + 2048), bf16), V((4 * PADF, cols), bf16), V((PADF, 512), bf16),
            V((12 * D, D), bf16), V((1024, D), bf16), V((2048, D), bf16), V((D, 2048), bf16), V((2048, D), bf16),
            V((D, 2048), bf16), V((8, HALF, 512), bf16), V((D, 1024), bf16), V((1024, D), bf16),
            dma((2,)), dma((6,)), dma((8,)), dma((7,)), dma((7,)),
        ] + [sem] * 8,
        compiler_params=pltpu.CompilerParams(collective_id=0, has_side_effects=True, vmem_limit_bytes=VMEM_BYTES),
        name="gather",
    )(slots, features, masks, tmap, owners, emb, small)


def gelu_pair(u):
    den = 1.0 + (0.3275911 * math.sqrt(0.5)) * jnp.abs(u)
    t = pl.reciprocal(den, approx=True)
    t = t * (2.0 - den * t)
    ex = jnp.exp2((-0.5 * LOG2E) * (u * u))
    poly = t * (0.127414796 + t * (-0.142248368 + t * (0.7107068705 + t * (-0.7265760135 + t * 0.5307027145))))
    e = poly * ex
    phi = jnp.where(u >= 0, 1.0 - e, e)
    return u * phi, phi + u * ex * (1.0 / math.sqrt(2 * math.pi))


AFTER = {
    "fb0": (2, 3), "up": (2,), "mix": (3, 0, 1), "h01": (2,), "h10": (3,), "w0": (2, 0, 3), "h20": (4,),
    "h30": (1, 2, 0, 3), "b0": (4, 2, 1, 0), "b1": (5,), "b2": (3,), "b3": (2,), "b5": (4, 1), "b7": (0, 3), "b9": (4, 5, 1, 0),
}


def main_kernel(
    R, su, occ, linv, small, Wh, Oh, h0h, dYh, ETh, OTh, qh, kTh, vh, a1sh, a1qh, n1sh, n1qh, rsh, rqh, XTh,
    out, FIN, SM, EM, GI,
    W, O_s, y_s, dY, ETb, OT, qs, kT, a1q, n1s, n1q, rs, rq, XT,
    a2_s, G_s, dU_s, Dp, sg, eg, GT, S, RC, RX, RH, AG0, AG1, AGL, SY, RY, SEL, PK, RK, GC, XS, XR,
    lsem, esem, osem, ss, sr, ys, yr, fs, fr, ps, pr, gs, gr,
):
    f = lax.axis_index("feat")
    r = lax.axis_index("rows")
    x = f // 2
    c = f % 2
    n = R.bit_length() - 1
    BH = S.shape[4]
    per = D // (2 * BH)
    core_id = (f ^ 1, r)
    x_id = (f ^ 2, r)
    row_id = [(f, r ^ (1 << j)) for j in range(n)]
    peers = [core_id, x_id] + row_id
    bar = greet(peers)

    loads = {}

    def load(name, src, dst):
        loads[name] = pltpu.make_async_copy(src, dst, lsem.at[len(loads)])
        loads[name].start()

    def rows_w(i):
        return pl.ds(i * D, D)

    load("O", Oh, O_s)
    load("h0", h0h, y_s)
    for i in (3, 4, 8, 5, 9, 6, 10, 7, 11):
        load(i, Wh.at[rows_w(i)], W.at[rows_w(i)])
    load("dY", dYh, dY)
    load("OT", OTh, OT)
    load("q", qh, qs)
    load("kT", kTh, kT)

    def ecopy(h, t):
        k = (h % 2) * 2 + t
        return pltpu.make_async_copy(ETh.at[t * HEADS + h], ETb.at[k], esem.at[k])

    for h in range(2):
        for t in range(2):
            ecopy(h, t).start()
    load("a1q", a1qh, a1q)
    load("n1s", n1sh, n1s)
    load("n1q", n1qh, n1q)
    load("rs", rsh, rs)
    load("rq", rqh, rq)
    load("XT", XTh, XT)
    for i in range(3):
        load(i, Wh.at[rows_w(i)], W.at[rows_w(i)])
    pl.semaphore_wait(bar, len(peers))

    bits = [(r >> j) & 1 for j in range(n)]
    base = [0]
    for j in range(n):
        base.append(base[j] + bits[j] * (R >> (j + 1)))

    def core_copy(g):
        return remote(S.at[1 - c, :, g], RC.at[:, g], ss.at[g, 0], sr.at[g, 0], core_id)

    def x_copy(g):
        return remote(S.at[c, 1 - x, g], RX.at[g], ss.at[g, 1], sr.at[g, 1], x_id)

    def rs_copy(g, j):
        half = R >> (j + 1)
        away = base[j] + (1 - bits[j]) * half
        off = R - (R >> j)
        return remote(
            S.at[c, x, g, pl.ds(away, half)], RH.at[g, pl.ds(off, half)],
            ss.at[g, 2 + j], sr.at[g, 2 + j], row_id[j],
        )

    def swap_copy(g):
        span = pl.ds(base[n - 1], 2)
        return remote(S.at[c, x, g, span], RH.at[g, pl.ds(R - 2, 2)], ss.at[g, 1 + n], sr.at[g, 1 + n], row_id[n - 1])

    def total_of(g):
        return AGL if g == 5 else AG1.at[g // 2] if g % 2 else AG0.at[(g // 2 + 1) % 3]

    def ag_copy(g, j):
        ref = total_of(g).at[pl.ds(base[j + 1] - base[1], R >> (j + 1))]
        return remote(ref, ref, ss.at[g, 2 + n + j], sr.at[g, 2 + n + j], row_id[j])

    def add(a, b):
        return (a.astype(f32) + b.astype(f32)).astype(bf16)

    def step(g, stage):
        if stage == 0:
            core_copy(g).wait_recv()
            S[c, 1 - x, g] = add(S[c, 1 - x, g], RC[1 - x, g])
            x_copy(g).start()
            S[c, x, g] = add(S[c, x, g], RC[x, g])
        elif stage == 1:
            x_copy(g).wait_recv()
            S[c, x, g] = add(S[c, x, g], RX[g])
            rs_copy(g, 0).start()
        elif stage < 1 + n:
            j = stage - 2
            half = R >> (j + 1)
            off = R - (R >> j)
            rs_copy(g, j).wait_recv()
            keep = pl.ds(base[j + 1], half)
            S[c, x, g, keep] = add(S[c, x, g, keep], RH[g, pl.ds(off, half)])
            if j < n - 2:
                rs_copy(g, j + 1).start()
            else:
                swap_copy(g).start()
        elif stage == 1 + n:
            swap_copy(g).wait_recv()
            total_of(g)[pl.ds(base[n - 1] - base[1], 2)] = add(S[c, x, g, pl.ds(base[n - 1], 2)], RH[g, pl.ds(R - 2, 2)])
            if n > 2:
                ag_copy(g, n - 2).start()
        else:
            j = 2 * n - stage
            ag_copy(g, j).wait_recv()
            if j > 1:
                ag_copy(g, j - 1).start()

    def select(m, who):
        picked = []
        for s in range(4):
            u = su[who * 4 + s]
            p = lax.rem(u, R // 2)
            q = lax.div(u, R)
            k = who * 4 + s
            if m == 0:
                picked.append(AG0[q, p].astype(f32) * occ[4 + k].astype(f32))
            else:
                picked.append(AG1[lax.max(q - 1, 0), p].astype(f32) * occ[12 + k].astype(f32) + AGL[p].astype(f32) * occ[20 + k].astype(f32))
        return picked

    def y_copy(m):
        return remote(SY.at[m], RY.at[m], ys.at[m], yr.at[m], row_id[0])

    def fin(m, k):
        if k == 3:
            return pltpu.make_async_copy(SEL.at[m], FIN.at[m, f], osem.at[1 + m])
        src, at = (FIN.at[m, f ^ 2], f ^ 2) if k == 2 else (SEL.at[m], f)
        return remote(src, FIN.at[m, at], fs.at[m, k], fr.at[m, k], x_id if k == 1 else core_id)

    def fin_step(m, stage):
        if stage == 0:
            for s, value in enumerate(select(m, 1)):
                SY[m, s] = value.astype(bf16)
            y_copy(m).start()
            for s, value in enumerate(select(m, 0)):
                SEL[m, s] = value.astype(bf16)
        elif stage == 1:
            y_copy(m).wait_recv()
            SEL[m] = add(SEL[m], RY[m])
            for k in (1, 0, 3):
                fin(m, k).start()
        else:
            fin(m, 1).wait_recv()
            fin(m, 2).start()

    last = 2 * n
    done = [0] * 6
    ended = [0, 0]

    def tick(g):
        if done[g] < last:
            step(g, done[g])
            done[g] += 1

    def finish(m):
        if ended[m] < 3 and all(done[g] == last for g in (m, 2 + m, 4 + m)):
            fin_step(m, ended[m])
            ended[m] += 1

    def after(piece):
        for g in AFTER.get(piece, ()):
            tick(g)

    def put(g0, i, val):
        for k in range(val.shape[1] // 128):
            piece = val[:, k * 128:(k + 1) * 128].reshape(per, 2, BH, 128)
            for h in range(2):
                S[k % 2, h, g0 + k // 2, pl.ds(i * per, per)] = piece[:, h]

    gain2 = small[3:4]
    shift2 = small[4:5]
    RB = 256

    def norm2(y1):
        cen = y1 - jnp.mean(y1, axis=-1, keepdims=True)
        rstd = lax.rsqrt(jnp.mean(cen * cen, axis=-1, keepdims=True) + LN_EPS)
        return cen * rstd, rstd

    loads["O"].wait()
    loads["h0"].wait()
    loads[3].wait()

    @pl.loop(0, 1024 // RB)
    def _(i):
        rows = pl.ds(pl.multiple_of(i * RB, RB), RB)
        y1 = y_s[rows] + dot(O_s[rows], W[rows_w(3)])
        y_s[rows] = y1
        n2, _ = norm2(y1)
        a2 = (n2 * gain2 + shift2).astype(bf16)
        a2_s[rows] = a2
        acc = y1 + small[5:6]
        for j in range(4):
            @pl.when(i == 0)
            def _():
                loads[4 + j].wait()
                loads[8 + j].wait()
            gl, gp = gelu_pair(dot(a2, W[rows_w(4 + j)]) + small[6 + j:7 + j])
            gb = gl.astype(bf16)
            G_s[j, rows] = gb
            dU_s[j, rows] = gp.astype(bf16)
            acc = acc + dot(gb, W[rows_w(8 + j)])
        O_s[rows] = acc.astype(bf16)

    ship_out = pltpu.make_async_copy(O_s, out, osem.at[0])
    ship_out.start()
    loads["dY"].wait()

    @pl.loop(0, 4)
    def _(j):
        put(2, j, dot(G_s[j], dY[...], TN).astype(bf16))

    core_copy(2).start()
    core_copy(3).start()

    sg[...] = jnp.zeros_like(sg)

    def backward_rows(i):
        rows = pl.ds(i * RB, RB)
        dy = dY[rows]
        da2 = jnp.zeros((RB, D), f32)
        for j in range(4):
            du = (dot(dy, W[rows_w(8 + j)], NT) * dU_s[j, rows].astype(f32)).astype(bf16)
            dU_s[j, rows] = du
            sg[6 + j:7 + j] += jnp.sum(du.astype(f32), axis=0, keepdims=True)
            da2 = da2 + dot(du, W[rows_w(4 + j)], NT)
        n2, rstd = norm2(y_s[rows])
        dyf = dy.astype(f32)
        sg[3:4] += jnp.sum(da2 * n2, axis=0, keepdims=True)
        sg[4:5] += jnp.sum(da2, axis=0, keepdims=True)
        sg[5:6] += jnp.sum(dyf, axis=0, keepdims=True)
        cc = da2 * gain2
        m1 = jnp.mean(cc, axis=-1, keepdims=True)
        m2 = jnp.mean(cc * n2, axis=-1, keepdims=True)
        y_s[rows] = dyf + rstd * (cc - m1 - n2 * m2)

    for i in range(1024 // RB):
        backward_rows(i)
        after("fb%d" % i)
    vs = W.at[pl.ds(4 * D, 4 * D)]
    a1s = W.at[pl.ds(8 * D, 4 * D)]
    load("v", vh, vs)
    load("a1s", a1sh, a1s)

    @pl.loop(0, 4)
    def _(j):
        put(0, j, dot(a2_s[...], dU_s[j], TN).astype(bf16))

    core_copy(0).start()
    core_copy(1).start()
    after("up")

    scale = HEAD_DIM**-0.5
    for i in range(2):
        dU_s[1, pl.ds(i * 512, 512)] = y_s[pl.ds(i * 512, 512)].astype(bf16)
    for name in ("OT", "v", "q", "kT", "a1s", "a1q"):
        loads[name].wait()
    put(4, 3, dot(OT[...], dU_s[1]).astype(bf16))

    @pl.loop(0, 2)
    def _(t):
        cols = pl.ds(pl.multiple_of(t * 512, 512), 512)
        whole = dot(W[rows_w(3)], dU_s[1, cols], NT)
        for h in range(HEADS):
            rows = pl.ds(h * HEAD_DIM, HEAD_DIM)
            d = whole[h * HEAD_DIM:(h + 1) * HEAD_DIM] * linv[pl.ds(t * HEADS + h, 1)]
            Dp[pl.ds(t * HEADS + h, 1)] = jnp.sum(d * OT[rows, cols].astype(f32), axis=0, keepdims=True)
            dU_s[2, pl.ds(pl.multiple_of(t * 512 + h * HEAD_DIM, HEAD_DIM), HEAD_DIM)] = d.astype(bf16)

    after("mix")

    def heads(h):
        hs = pl.ds(h * HEAD_DIM, HEAD_DIM)
        for t in range(2):
            ecopy(h, t).wait()

        @pl.loop(0, 2)
        def _(t):
            i = t * HEADS + h
            ksl = pl.ds(pl.multiple_of(t * HALF, HALF), HALF)
            qsl = pl.ds(pl.multiple_of(t * 512, 512), 512)
            do = dU_s[2, pl.ds(pl.multiple_of(t * 512 + h * HEAD_DIM, HEAD_DIM), HEAD_DIM)]
            dp = dot(vs[ksl, hs], do)
            e = ETb[(h % 2) * 2 + t]
            ds = (e.astype(f32) * (dp - Dp[pl.ds(i, 1)])).astype(bf16)
            G_s[2 + t, :, hs] = dot(e, do, NT).astype(bf16)
            G_s[t, :, hs] = (dot(ds, qs[qsl, hs]) * (1.0 / LOG2E)).astype(bf16)
            dqT = (dot(kT[hs, ksl], ds) * scale).astype(bf16)
            dU_s[0, qsl, hs] = dqT.T

        for t in range(2):
            if h + 2 < HEADS:
                ecopy(h + 2, t).start()
            after("h%d%d" % (h, t))

    def weight_grads(m):
        cols = pl.ds(m * 256, 256)
        acc = jnp.zeros((D, 256), f32)
        for t in range(2):
            sup = pl.multiple_of(t * HALF + f * QUART, QUART)
            acc += dot(a1s[pl.ds(sup, QUART)], dU_s[0, pl.ds(t * 512, QUART), cols], TN)
            acc += dot(a1q[pl.ds(t * QUART, QUART)], dU_s[0, pl.ds(t * 512 + QUART, QUART), cols], TN)
        put(4 + m, 0, acc.astype(bf16))
        for k in range(2):
            total = dot(a1s[pl.ds(0, HALF)], G_s[2 * k, :, cols], TN) + dot(a1s[pl.ds(HALF, HALF)], G_s[2 * k + 1, :, cols], TN)
            put(4 + m, 1 + k, total.astype(bf16))

    for m in range(2):
        heads(2 * m)
        heads(2 * m + 1)
        weight_grads(m)
        core_copy(4 + m).start()
        after("w%d" % m)

    eg[...] = jnp.zeros_like(eg)
    gain1 = small[1:2]
    emb_cols = pl.ds(2 * HALF, D)
    for name in ("n1s", "n1q", "rs", "rq", "XT", 0, 1, 2):
        loads[name].wait()

    def back(da, nrm, rstd, extra, cols, out_cols):
        sg[1:2] += jnp.sum(da * nrm, axis=0, keepdims=True)
        sg[2:3] += jnp.sum(da, axis=0, keepdims=True)
        cc = da * gain1
        m1 = jnp.mean(cc, axis=-1, keepdims=True)
        m2 = jnp.mean(cc * nrm, axis=-1, keepdims=True)
        wide = jnp.concatenate([rstd] * 4, axis=1)
        dh = wide * (cc - m1 - nrm * m2)
        if extra is not None:
            dh = dh + extra
        sg[0:1] += jnp.sum(dh, axis=0, keepdims=True)
        de = dh.astype(bf16)
        part = dot(XT[:, cols], de)
        back_in = dot(XT[:, emb_cols], de, NT).astype(bf16)
        for k in range(4):
            eg[k] += part[k * PADF:(k + 1) * PADF]
            GT[k % 2, k // 2, :, out_cols] = back_in[k * PADF:(k + 1) * PADF]

    def below(t):
        q0 = t * 512
        wq, wk, wv = W[rows_w(0)], W[rows_w(1)], W[rows_w(2)]
        da = dot(dU_s[0, pl.ds(q0 + QUART, QUART)], wq, NT)
        p0 = pl.ds(t * QUART, QUART)
        back(
            da, n1q[p0].astype(f32), rq[p0], y_s[pl.ds(q0 + QUART, QUART)],
            pl.ds(2 * HALF + D + t * QUART, QUART), pl.ds(2 * HALF + t * QUART, QUART),
        )
        after("b%d" % (5 * t))
        for b in range(4):
            at = pl.ds(pl.multiple_of(((f + b) % 4) * QUART, QUART), QUART)
            rows = pl.ds(pl.multiple_of(t * HALF + ((f + b) % 4) * QUART, QUART), QUART)
            da = dot(G_s[t, at], wk, NT) + dot(G_s[2 + t, at], wv, NT)
            extra = None
            if b == 0:
                da = da + dot(dU_s[0, pl.ds(q0, QUART)], wq, NT)
                extra = y_s[pl.ds(q0, QUART)]
            back(da, n1s[rows].astype(f32), rs[rows], extra, rows, rows)
            if 5 * t + b < 8:
                after("b%d" % (5 * t + b + 1))

    below(0)
    below(1)

    small_rows = pl.ds(0, 16)
    PK[0, small_rows] = sg[...]
    for k in range(2):
        PK[0, pl.ds(16 + k * PADF, PADF)] = eg[2 * k + 1 - c]

    def pk_copy(i):
        rows = pl.ds(0, 80 if i == 0 else 48)
        dev = core_id if i == 0 else x_id if i == 1 else row_id[i - 2]
        return remote(PK.at[i, rows], RK.at[i, rows], ps.at[i], pr.at[i], dev)

    def pk_step(i):
        pk_copy(i).wait_recv()
        if i == 0:
            PK[1, small_rows] = PK[0, small_rows] + RK[0, small_rows]
            own = [eg[2 * k + c] + RK[0, pl.ds(16 + k * PADF, PADF)] for k in range(2)]
            PK[1, pl.ds(16, PADF)] = jnp.where(x == 0, own[1], own[0])
            PK[1, pl.ds(48, PADF)] = jnp.where(x == 0, own[0], own[1])
            pk_copy(1).start()
        else:
            old = PK[1, pl.ds(48, PADF)] if i == 1 else PK[i, pl.ds(16, PADF)]
            a = PK[i, small_rows] + RK[i, small_rows]
            b = old + RK[i, pl.ds(16, PADF)]
            if i < n + 1:
                PK[i + 1, small_rows] = a
                PK[i + 1, pl.ds(16, PADF)] = b
                pk_copy(i + 1).start()
            else:
                SM[...] = a
                EM[...] = b

    pk_copy(0).start()
    gt1 = remote(GT.at[1 - c], GC, gs.at[0], gr.at[0], core_id)
    gt1.start()
    sup = pl.ds(0, 2 * HALF)
    que = pl.ds(2 * HALF, 512)

    def que_of(k):
        return pl.ds(pl.multiple_of(2 * HALF + k * 512, 512), 512)

    gt2 = remote(XS, XR, gs.at[1], gr.at[1], x_id)
    after("b9")
    pk_step(0)
    gt1.wait_recv()
    XS[:, sup] = add(GT[c, 1 - x, :, sup], GC[1 - x, :, sup])
    XS[:, que_of(c)] = GT[c, 1 - x, :, que]
    XS[:, que_of(1 - c)] = GC[1 - x, :, que]
    gt2.start()
    next_pk = 1
    while min(done) < last:
        for g in (4, 5, 2, 3, 1, 0):
            tick(g)
        finish(0)
        if next_pk < n + 2:
            pk_step(next_pk)
            next_pk += 1
    finish(1)
    finish(0)
    for i in range(next_pk, n + 2):
        pk_step(i)
    gt2.wait_recv()
    GI[:, sup] = (
        GT[c, x, :, sup].astype(f32) + GC[x, :, sup].astype(f32) + XR[:, sup].astype(f32)
    ).astype(bf16)
    GI[:, que_of(f)] = GT[c, x, :, que]
    GI[:, que_of(f ^ 1)] = GC[x, :, que]
    for k in range(2):
        GI[:, que_of(2 * (1 - x) + k)] = XR[:, pl.ds(2 * HALF + k * 512, 512)]
    while min(ended) < 3:
        finish(0)
        finish(1)
    for m in range(2):
        y_copy(m).wait_send()
        fin(m, 0).wait()
        fin(m, 1).wait_send()
        fin(m, 2).wait()
        fin(m, 3).wait()
    for g in range(6):
        core_copy(g).wait_send()
        x_copy(g).wait_send()
        swap_copy(g).wait_send()
        for j in range(n - 1):
            rs_copy(g, j).wait_send()
        for j in range(1, n - 1):
            ag_copy(g, j).wait_send()
    for i in range(n + 2):
        pk_copy(i).wait_send()
    gt1.wait_send()
    gt2.wait_send()
    ship_out.wait()


def main_call(R, su, occ, linv, small, W, O, h0, dY, ET, OT, q, kT, v, a1s, a1q, n1s, n1q, rs, rq, XT):
    BH = 12 * D // (3 * R) // 2
    n = R.bit_length() - 1
    sd = jax.ShapeDtypeStruct
    V = pltpu.VMEM
    dma = pltpu.SemaphoreType.DMA
    blk = (R, BH, 128)
    like = lambda a: V(a.shape, a.dtype)
    return pl.pallas_call(
        functools.partial(main_kernel, R),
        out_shape=(sd((1024, D), bf16), sd((2, 4, 4, BH, 128), bf16), sd((16, D), f32), sd((PADF, D), f32), sd((PADF, 4096), bf16)),
        in_specs=[smem(), smem(), vmem(), vmem()] + [anyspace()] * 16,
        out_specs=(anyspace(), anyspace(), vmem(), vmem(), vmem()),
        scratch_shapes=[
            like(W), like(O), like(h0), like(dY), V((4, HALF, 512), bf16), like(OT), like(q), like(kT),
            like(a1q), like(n1s), like(n1q), like(rs), like(rq), like(XT),
            V((1024, D), bf16), V((4, 1024, 512), bf16), V((4, 1024, 512), bf16), V((8, 512), f32), V((16, D), f32),
            V((4, PADF, D), f32), V((2, 2, PADF, 2560), bf16),
            V((2, 2, 6) + blk, bf16), V((2, 6) + blk, bf16), V((6,) + blk, bf16), V((6,) + blk, bf16), V((3, R // 2, BH, 128), bf16), V((2, R // 2, BH, 128), bf16), V((R // 2, BH, 128), bf16),
            V((2, 4, BH, 128), bf16), V((2, 4, BH, 128), bf16), V((2, 4, BH, 128), bf16), V((n + 2, 80, D), f32), V((n + 2, 80, D), f32),
            V((2, PADF, 2560), bf16), V((PADF, 3072), bf16), V((PADF, 3072), bf16),
            dma((26,)), dma((4,)), dma((3,)), dma((6, 2 + 2 * n)), dma((6, 2 + 2 * n)), dma((2,)), dma((2,)), dma((2, 3)), dma((2, 3)),
            dma((n + 2,)), dma((n + 2,)), dma((2,)), dma((2,)),
        ],
        compiler_params=pltpu.CompilerParams(collective_id=1, has_side_effects=True, vmem_limit_bytes=VMEM_BYTES),
        name="main",
    )(su, occ, linv, small, W, O, h0, dY, ET, OT, q, kT, v, a1s, a1q, n1s, n1q, rs, rq, XT)


def adamw(weight, grad, first, second, rate):
    first_new = BETA_FIRST * first + (1.0 - BETA_FIRST) * grad
    second_new = BETA_SECOND * second + (1.0 - BETA_SECOND) * grad * grad
    first_hat = first_new / (1.0 - BETA_FIRST**STEP)
    second_hat = second_new / (1.0 - BETA_SECOND**STEP)
    weight_new = weight - rate * (first_hat / (jnp.sqrt(second_hat) + ADAM_EPS) + DECAY * weight)
    return (first_new, second_new, weight_new)


def update_kernel(
    occ, tmap, FIN, w, m, v, SM, sw, sm, sv, EM, ew, em, ev, GI, masks, lo,
    g_o, m_o, v_o, w_o, wc_o, eg_o, em_o, ev_o, ew_o, ec_o, sg_o, sm_o, sv_o, sw_o, gi_o, lo_o,
):
    s = pl.program_id(0)
    keep = occ[s].astype(f32)
    BH = FIN.shape[3]
    for f in range(4):
        rows = pl.ds((f // 2) * BH, BH)
        for k in range(2):
            cols = pl.ds(k * 256 + (f % 2) * 128, 128)
            g = FIN[k, f, 0].astype(f32)
            a, b, d = adamw(w[0, rows, cols], g, m[0, rows, cols], v[0, rows, cols], RATE_MATRIX)
            g_o[0, rows, cols] = g * keep
            m_o[0, rows, cols] = a * keep
            v_o[0, rows, cols] = b * keep
            d = d * keep
            w_o[0, rows, cols] = d
            wc_o[0, rows, cols] = d.astype(bf16)

    @pl.when(s == 0)
    def _():
        g = SM[0:10]
        a, b, d = adamw(sw[...], g, sm[...], sv[...], RATE_SMALL)
        sg_o[...] = g
        sm_o[...] = a
        sv_o[...] = b
        sw_o[...] = d
        nf = ew.shape[0]
        g = EM[pl.ds(0, nf)]
        a, b, d = adamw(ew[...], g, em[...], ev[...], RATE_EMBED)
        eg_o[...] = g
        em_o[...] = a
        ev_o[...] = b
        ew_o[...] = d
        ec_o[...] = d.astype(bf16)

    nf = gi_o.shape[1]
    t = s // 2
    keep_in = mask_column(masks, tmap[t])

    @pl.when(s % 2 == 0)
    def _():
        cols = pl.ds(pl.multiple_of(t * HALF, HALF), HALF)
        gi_o[t, :, 0, :] = (GI[pl.ds(0, nf), cols].astype(f32) * keep_in).astype(bf16)

    @pl.when(s % 2 == 1)
    def _():
        for k in range(4):
            cols = pl.ds(pl.multiple_of(2 * HALF + k * 512 + t * QUART, QUART), QUART)
            gi_o[t, :, 1, pl.ds(k * QUART, QUART)] = (GI[pl.ds(0, nf), cols].astype(f32) * keep_in).astype(bf16)

    lo_o[...] = lo[...]


def update_call(occ, tmap, FIN, w, m, v, SM, sw, sm, sv, EM, ew, em, ev, GI, masks, lo):
    S, BR, W = w.shape
    nf = ew.shape[0]
    sd = jax.ShapeDtypeStruct
    blk = pl.BlockSpec((1, BR, W), lambda s: (s, 0, 0))
    whole = lambda a: pl.BlockSpec(a.shape, lambda s: (0,) * len(a.shape))
    ins = [smem(), smem(), pl.BlockSpec((2, 4, 1, BR // 2, 128), lambda s: (0, 0, s, 0, 0)), blk, blk, blk]
    ins += [whole(a) for a in (SM, sw, sm, sv, EM, ew, em, ev, GI, masks)] + [pl.BlockSpec((1024 // S, D), lambda s: (s, 0))]
    big = sd((S, BR, W), f32)
    small = sd((10, D), f32)
    e = sd((nf, D), f32)
    outs = [big, big, big, big, sd((S, BR, W), bf16), e, e, e, e, sd((nf, D), bf16), small, small, small, small, sd((2, nf, 2, HALF), bf16), sd(lo.shape, lo.dtype)]
    specs = [blk] * 5 + [whole(a) for a in outs[5:14]] + [whole(outs[14]), pl.BlockSpec((1024 // S, D), lambda s: (s, 0))]
    return pl.pallas_call(
        update_kernel, out_shape=tuple(outs), grid=(S,), in_specs=ins, out_specs=tuple(specs),
        compiler_params=pltpu.CompilerParams(vmem_limit_bytes=VMEM_BYTES), name="update",
    )(occ, tmap, FIN, w, m, v, SM, sw, sm, sv, EM, ew, em, ev, GI, masks, lo)


def body(
    features, feature_masks, table_map, owners, out_grad, weight_slots, moment1_slots, moment2_slots,
    emb_weight, emb_moment1, emb_moment2, small_weight, small_moment1, small_moment2,
):
    width = weight_slots.shape[2]
    R = lax.axis_size("rows")
    slot_unit, kinds, XT, h0o, a1s, a1q, n1s, n1q, rs, rq, linv, W, q, kT, v, ET, OT, O = gather_call(
        R, weight_slots, features.transpose(0, 3, 1, 2), feature_masks, table_map, owners, emb_weight, small_weight
    )
    dY = out_grad.reshape(1024, width)
    out, FIN, SM, EM, GI = main_call(
        R, slot_unit, kinds, linv, small_weight, W, O, h0o, dY, ET, OT, q, kT, v, a1s, a1q, n1s, n1q, rs, rq, XT
    )
    (
        g_slots, m_slots, v_slots, w_slots, w_copy, e_grad, e_m, e_v, e_w, e_copy, s_grad, s_m, s_v, s_w, grad_inputs, out,
    ) = update_call(
        kinds, table_map, FIN, weight_slots, moment1_slots, moment2_slots, SM, small_weight, small_moment1,
        small_moment2, EM, emb_weight, emb_moment1, emb_moment2, GI, feature_masks, out,
    )
    grad_inputs = grad_inputs.transpose(0, 2, 3, 1)
    return (
        out.reshape(out_grad.shape), grad_inputs, g_slots, m_slots, v_slots, w_slots, w_copy,
        e_grad, e_m, e_v, e_w, e_copy, s_grad, s_m, s_v, s_w,
    )


def solution(mesh):
    rows3 = P("rows", None, None)
    feat2 = P("feat", None)
    in_specs = (
        P("rows", None, None, "feat"), P(None, "feat"), P("rows"), P(), P("rows", None, "feat", None),
        rows3, rows3, rows3, feat2, feat2, feat2, P(), P(), P(),
    )
    out_specs = (
        P("rows", None, "feat", None), P("rows", None, None, "feat"), rows3, rows3, rows3, rows3, rows3,
        feat2, feat2, feat2, feat2, feat2, P(), P(), P(), P(),
    )
    return jax.shard_map(body, mesh=mesh, in_specs=in_specs, out_specs=out_specs, check_vma=False)
```

```python
import functools
import math

import jax
import jax.numpy as jnp
from jax import lax
from jax.experimental import pallas as pl
from jax.experimental.pallas import tpu as pltpu
from jax.sharding import PartitionSpec as P

MESH = pl.DeviceIdType.MESH
bf16, f32 = jnp.bfloat16, jnp.float32
NN = (((1,), (0,)), ((), ()))
NT = (((1,), (1,)), ((), ()))
TN = (((0,), (0,)), ((), ()))
LOG2E = math.log2(math.e)
HEADS = 4
HEAD_DIM = 128
STEP = 10
LN_EPS = 1e-05
BETA_FIRST = 0.9
BETA_SECOND = 0.999
ADAM_EPS = 1e-08
DECAY = 0.01
RATE_MATRIX = 0.1
RATE_EMBED = 0.3
RATE_SMALL = 0.6
D = 512
HALF = 1024
QUART = 256
PADF = 32
VMEM_BYTES = 60 * 2**20


def dot(a, b, dims=NN):
    return lax.dot_general(a, b, dims, preferred_element_type=f32)


def vmem():
    return pl.BlockSpec(memory_space=pltpu.VMEM)


def anyspace():
    return pl.BlockSpec(memory_space=pl.ANY)


def smem():
    return pl.BlockSpec(memory_space=pltpu.SMEM)


def remote(src, dst, send, recv, dev):
    return pltpu.make_async_remote_copy(
        src_ref=src, dst_ref=dst, send_sem=send, recv_sem=recv, device_id=dev, device_id_type=MESH
    )


def greet(peers):
    bar = pltpu.get_barrier_semaphore()
    for d in peers:
        pl.semaphore_signal(bar, inc=1, device_id=d, device_id_type=MESH)
    return bar


def mask_column(masks, table):
    T, nf = masks.shape
    which = lax.broadcasted_iota(jnp.int32, (T, nf), 0) == table
    line = jnp.sum(jnp.where(which, masks[...], 0), axis=0, keepdims=True)
    eye = lax.broadcasted_iota(jnp.int32, (nf, nf), 0) == lax.broadcasted_iota(jnp.int32, (nf, nf), 1)
    return jnp.sum(jnp.where(eye, jnp.broadcast_to(line, (nf, nf)), 0), axis=1, keepdims=True).astype(f32)


GROUPS = (True, False)


def gather_kernel(
    R, slots_ref, feat_ref, mask_ref, tmap_ref, own_ref, emb_ref, small_ref,
    su_ref, kind_ref, XT_ref, h0_ref, a1s_ref, a1q_ref, n1s_ref, n1q_ref, rs_ref, rq_ref, linv,
    Wo, qo, kTo, vo, ET, OT, Oo,
    pos, G0, G1, own, XTo, XTa, tmpq, W, q_s, k_s, kT_s, v_s, vT_s, ET_s, OT_s, O_s,
    lsem, osem, esem, fs, fr, hs, hr, xs, xr, cs, cr, c2s, c2r,
):
    f = lax.axis_index("feat")
    r = lax.axis_index("rows")
    x = f // 2
    c = f % 2
    n = R.bit_length() - 1
    S, BR = slots_ref.shape[:2]
    U = own_ref.shape[0]
    BH = BR // 2
    Gs = (G0, G1)
    core_id = (f ^ 1, r)
    x_id = (f ^ 2, r)
    row_id = [(f, r ^ (1 << (n - 1 - j))) for j in range(n)]
    peers = [core_id, x_id] + row_id
    bar = greet(peers)
    for k in range(4):
        own[k // 2, k % 2] = slots_ref[:, :, k * 128:(k + 1) * 128].astype(bf16)
    pl.semaphore_wait(bar, len(peers))

    def keep_own(p):
        return pltpu.make_async_copy(own.at[p], Gs[p].at[:, 0], lsem.at[p])

    subs = [(j, g) for j in range(n) for g in range(-1, j)]
    index = {jg: i for i, jg in enumerate(subs)}
    rows_c = pl.ds(pl.multiple_of(c * BH, BH), BH)

    def part(p, s, half, start, size):
        if GROUPS[s]:
            return Gs[p].at[half, pl.ds(start, size), pl.ds(1, 3), rows_c]
        return Gs[p].at[:, pl.ds(start, size), 0, rows_c]

    def hyper(p, s, j, g):
        k = index[(j, g)]
        if g < 0:
            if GROUPS[s]:
                src, dst = own.at[p, x, pl.ds(1, 3), rows_c], Gs[p].at[x, 1 << j, pl.ds(1, 3), rows_c]
            else:
                src, dst = own.at[p, :, 0, rows_c], Gs[p].at[:, 1 << j, 0, rows_c]
        else:
            src, dst = part(p, s, x, 1 << g, 1 << g), part(p, s, x, (1 << j) + (1 << g), 1 << g)
        return remote(src, dst, hs.at[p, s, k], hr.at[p, s, k], row_id[j])

    def forward(p, s, j, g, half, sems, semr, dev):
        start, size = (0, 1) if g < 0 else (1 << g, 1 << g)
        k = index[(j, g)]
        ref = part(p, s, half, (1 << j) + start, size)
        return remote(ref, ref, sems.at[p, s, k], semr.at[p, s, k], dev)

    def to_x(p, s, j, g):
        return forward(p, s, j, g, x, xs, xr, x_id)

    def to_core(p, s, j, g):
        return forward(p, s, j, g, x, cs, cr, core_id)

    def to_core_x(p, s, j, g):
        return forward(p, s, j, g, 1 - x, c2s, c2r, core_id)

    order = range(len(GROUPS))

    def send_own(p):
        for s in order:
            for j in range(n):
                hyper(p, s, j, -1).start()
        keep_own(p).start()

    def x_arrive(p, j):
        for s in order:
            if GROUPS[s]:
                for g in range(-1, j):
                    to_x(p, s, j, g).wait_recv()
                    to_core_x(p, s, j, g).start()

    def hyper_arrive(p, j):
        for s in order:
            for g in range(-1, j):
                hyper(p, s, j, g).wait_recv()
                if GROUPS[s]:
                    to_x(p, s, j, g).start()
                to_core(p, s, j, g).start()
            for j2 in range(j + 1, n):
                hyper(p, s, j2, j).start()

    def all_here(p):
        keep_own(p).wait()
        for s in order:
            for j, g in subs:
                to_core(p, s, j, g).wait_recv()
                if GROUPS[s]:
                    to_core_x(p, s, j, g).wait_recv()

    def all_sent(p):
        for s in order:
            for j, g in subs:
                hyper(p, s, j, g).wait_send()
                to_core(p, s, j, g).wait_send()
                if GROUPS[s]:
                    to_x(p, s, j, g).wait_send()
                    to_core_x(p, s, j, g).wait_send()

    send_own(0)

    nf = feat_ref.shape[1]
    XTo[...] = jnp.zeros_like(XTo)
    for t in range(2):
        keep = mask_column(mask_ref, tmap_ref[t])
        XTo[pl.ds(0, nf), pl.ds(t * HALF, HALF)] = (feat_ref[t, :, 0, :].astype(f32) * keep).astype(bf16)
        query = (feat_ref[t, :, 1, :].astype(f32) * keep).astype(bf16)
        for k in range(4):
            XTo[pl.ds(0, nf), pl.ds(2 * HALF + D + k * 512 + t * QUART, QUART)] = query[:, k * QUART:(k + 1) * QUART]
    XTo[pl.ds(0, nf), pl.ds(2 * HALF, D)] = emb_ref[...].astype(bf16)
    wide = 2 * HALF + D
    shared = pl.ds(0, wide)
    tail = pl.ds(wide, 512)

    def rows_of(dev):
        return pl.ds(pl.multiple_of(dev * PADF, PADF), PADF)

    def chunk_of(dev):
        return pl.ds(pl.multiple_of(wide + dev * 512, 512), 512)

    feats = [
        remote(XTo.at[:, shared], XTa.at[rows_of(f), shared], fs.at[0], fr.at[0], core_id),
        remote(XTo.at[:, chunk_of(f ^ 1)], XTa.at[rows_of(f), tail], fs.at[1], fr.at[1], core_id),
        remote(XTo.at[:, shared], XTa.at[rows_of(f), shared], fs.at[2], fr.at[2], x_id),
        remote(XTo.at[:, chunk_of(f ^ 2)], XTa.at[rows_of(f), tail], fs.at[3], fr.at[3], x_id),
        remote(XTo.at[:, chunk_of(f ^ 3)], tmpq, fs.at[4], fr.at[4], x_id),
        remote(XTa.at[rows_of(f ^ 2), shared], XTa.at[rows_of(f ^ 2), shared], fs.at[5], fr.at[5], core_id),
        remote(tmpq, XTa.at[rows_of(f ^ 2), tail], fs.at[6], fr.at[6], core_id),
    ]
    for copy in feats[:5]:
        copy.start()
    XTa[rows_of(f), shared] = XTo[:, shared]
    XTa[rows_of(f), tail] = XTo[:, chunk_of(f)]

    for k in range(2 * S):
        su_ref[k] = 0
    for k in range(7 * S):
        kind_ref[k] = 0

    @pl.loop(0, U)
    def _(u):
        owner = own_ref[u]
        rank = lax.fori_loop(0, u, lambda j, total: total + jnp.where(own_ref[j] == owner, 1, 0), 0)
        distance = owner ^ r
        place = 0
        for bit in range(n):
            place = place + (((distance >> bit) & 1) << (n - 1 - bit))
        pos[u] = place * S + jnp.minimum(rank, S - 1)
        for k in range(2 * S):
            hit = jnp.where(owner == r ^ (k // S), 1, 0) * jnp.where(rank == k % S, 1, 0)
            su_ref[k] = su_ref[k] + hit * u
            here = hit * jnp.where((u % R) // (R // 2) == r % 2, 1, 0)
            late = here * jnp.where(u < R, 1, 0)
            if k < S:
                kind_ref[k] = kind_ref[k] + hit
            kind_ref[S + k] = kind_ref[S + k] + here
            kind_ref[3 * S + k] = kind_ref[3 * S + k] + here - late
            kind_ref[5 * S + k] = kind_ref[5 * S + k] + late

    hyper_arrive(0, 0)
    feats[2].wait_recv()
    feats[4].wait_recv()
    feats[5].start()
    feats[6].start()
    for j in range(1, n - 1):
        hyper_arrive(0, j)
        x_arrive(0, j - 1)
    send_own(1)
    for k in (0, 1, 3, 5, 6):
        feats[k].wait_recv()

    shift0 = small_ref[0:1]
    gain = small_ref[1:2]
    shift = small_ref[2:3]

    def norm(cols):
        h = dot(XTa[:, cols], XTa[:, pl.ds(2 * HALF, D)], TN) + shift0
        mean = jnp.mean(h, axis=-1, keepdims=True)
        cen = h - mean
        rstd = lax.rsqrt(jnp.mean(cen * cen, axis=-1, keepdims=True) + LN_EPS)
        nrm = cen * rstd
        return h, nrm, rstd, (nrm * gain + shift).astype(bf16)

    @pl.loop(0, 8)
    def _(i):
        rows = pl.ds(pl.multiple_of(i * QUART, QUART), QUART)
        h, nrm, rstd, act = norm(rows)
        n1s_ref[rows] = nrm.astype(bf16)
        a1s_ref[rows] = act
        rs_ref[rows] = jnp.broadcast_to(rstd, (QUART, 128))

        @pl.when(i % 4 == f)
        def _():
            h0_ref[pl.ds(pl.multiple_of((i // 4) * 512, 512), QUART)] = h

    hyper_arrive(0, n - 1)
    if n > 1:
        x_arrive(0, n - 2)

    @pl.loop(0, 2)
    def _(t):
        rows = pl.ds(pl.multiple_of(t * QUART, QUART), QUART)
        h, nrm, rstd, act = norm(pl.ds(pl.multiple_of(wide + t * QUART, QUART), QUART))
        n1q_ref[rows] = nrm.astype(bf16)
        a1q_ref[rows] = act
        rq_ref[rows] = jnp.broadcast_to(rstd, (QUART, 128))
        h0_ref[pl.ds(pl.multiple_of(t * 512 + QUART, QUART), QUART)] = h

    XT_ref[...] = XTa[...]
    hyper_arrive(1, 0)
    x_arrive(0, n - 1)
    scale = (HEAD_DIM**-0.5) * LOG2E

    def assemble(p):
        for u in range(U):
            place, rank = pos[u] // S, pos[u] % S
            for k in range(2):
                W[pl.ds(u * BR, BR), pl.ds(p * 256 + k * 128, 128)] = Gs[p][k, place, rank]

    def project(p):
        cols = pl.ds(p * 256, 256)
        for t in range(2):
            sup = pl.multiple_of(t * HALF + f * QUART, QUART)
            wq = W[pl.ds(0, D), cols]
            q_s[pl.ds(t * 512, QUART), cols] = (dot(a1s_ref[pl.ds(sup, QUART)], wq) * scale).astype(bf16)
            q_s[pl.ds(t * 512 + QUART, QUART), cols] = (dot(a1q_ref[pl.ds(t * QUART, QUART)], wq) * scale).astype(bf16)

        @pl.loop(0, 4)
        def _(i):
            rows = pl.ds(pl.multiple_of(i * 512, 512), 512)
            a = a1s_ref[rows]
            k = dot(a, W[pl.ds(D, D), cols]).astype(bf16)
            k_s[rows, cols] = k
            kT_s[cols, rows] = k.T
            v = dot(a, W[pl.ds(2 * D, D), cols]).astype(bf16)
            v_s[rows, cols] = v
            vT_s[cols, rows] = v.T

    def ecopy(i):
        return pltpu.make_async_copy(ET_s.at[i], ET.at[i], esem.at[i])

    def head(h):
        hs = pl.ds(h * HEAD_DIM, HEAD_DIM)

        @pl.loop(0, 2)
        def _(t):
            i = t * HEADS + h
            ks = pl.ds(pl.multiple_of(t * HALF, HALF), HALF)
            qs = pl.ds(pl.multiple_of(t * 512, 512), 512)
            st = dot(k_s[ks, hs], q_s[qs, hs], NT)
            top = jnp.max(st, axis=0, keepdims=True)
            e = jnp.exp2(st - top)
            inv = 1.0 / jnp.sum(e, axis=0, keepdims=True)
            eb = e.astype(bf16)
            ET_s[i] = eb
            ecopy(i).start()
            linv[pl.ds(i, 1)] = inv
            ot = (dot(vT_s[hs, ks], eb) * inv).astype(bf16)
            OT_s[hs, qs] = ot
            O_s[qs, hs] = ot.T

    outs = []

    def ship(src, dst):
        copy = pltpu.make_async_copy(src, dst, osem.at[len(outs)])
        copy.start()
        outs.append(copy)

    all_here(0)
    assemble(0)
    for j in range(1, n - 1):
        hyper_arrive(1, j)
        x_arrive(1, j - 1)
    project(0)
    hyper_arrive(1, n - 1)
    if n > 1:
        x_arrive(1, n - 2)
    head(0)
    x_arrive(1, n - 1)
    head(1)
    all_here(1)
    assemble(1)
    ship(W, Wo)
    project(1)
    ship(q_s, qo)
    ship(kT_s, kTo)
    ship(v_s, vo)
    head(2)
    head(3)
    ship(O_s, Oo)
    ship(OT_s, OT)
    for copy in feats:
        copy.wait_send()
    all_sent(0)
    all_sent(1)
    for i in range(8):
        ecopy(i).wait()
    for copy in outs:
        copy.wait()


def gather_call(R, slots, features, masks, tmap, owners, emb, small):
    S, BR, W = slots.shape
    n = R.bit_length() - 1
    M = n * (n + 1) // 2
    dma = pltpu.SemaphoreType.DMA
    sem = dma((2, len(GROUPS), M))
    sd = jax.ShapeDtypeStruct
    V = pltpu.VMEM
    cols = 2 * HALF + D + 512
    half = V((2, R, S, BR, 128), bf16)
    return pl.pallas_call(
        functools.partial(gather_kernel, R),
        out_shape=(
            sd((2 * S,), jnp.int32), sd((7 * S,), jnp.int32), sd((4 * PADF, cols), bf16), sd((1024, D), f32),
            sd((2048, D), bf16), sd((512, D), bf16), sd((2048, D), bf16), sd((512, D), bf16),
            sd((2048, 128), f32), sd((512, 128), f32), sd((8, 512), f32),
            sd((12 * D, D), bf16), sd((1024, D), bf16), sd((D, 2048), bf16), sd((2048, D), bf16),
            sd((8, HALF, 512), bf16), sd((D, 1024), bf16), sd((1024, D), bf16),
        ),
        in_specs=[vmem(), vmem(), vmem(), smem(), smem(), vmem(), vmem()],
        out_specs=(smem(), smem()) + (vmem(),) * 9 + (anyspace(),) * 7,
        scratch_shapes=[
            pltpu.SMEM(owners.shape, jnp.int32), half, half, V((2, 2, S, BR, 128), bf16),
            V((PADF, 2 * HALF + D + 2048), bf16), V((4 * PADF, cols), bf16), V((PADF, 512), bf16),
            V((12 * D, D), bf16), V((1024, D), bf16), V((2048, D), bf16), V((D, 2048), bf16), V((2048, D), bf16),
            V((D, 2048), bf16), V((8, HALF, 512), bf16), V((D, 1024), bf16), V((1024, D), bf16),
            dma((2,)), dma((6,)), dma((8,)), dma((7,)), dma((7,)),
        ] + [sem] * 8,
        compiler_params=pltpu.CompilerParams(collective_id=0, has_side_effects=True, vmem_limit_bytes=VMEM_BYTES),
        name="gather",
    )(slots, features, masks, tmap, owners, emb, small)


def gelu_pair(u):
    den = 1.0 + (0.3275911 * math.sqrt(0.5)) * jnp.abs(u)
    t = pl.reciprocal(den, approx=True)
    t = t * (2.0 - den * t)
    ex = jnp.exp2((-0.5 * LOG2E) * (u * u))
    poly = t * (0.127414796 + t * (-0.142248368 + t * (0.7107068705 + t * (-0.7265760135 + t * 0.5307027145))))
    e = poly * ex
    phi = jnp.where(u >= 0, 1.0 - e, e)
    return u * phi, phi + u * ex * (1.0 / math.sqrt(2 * math.pi))


AFTER = {
    "fb0": (2, 3), "up": (2,), "mix": (3, 0, 1), "h01": (2,), "h10": (3,), "w0": (2, 0, 3), "h20": (4,),
    "h30": (1, 2, 0, 3), "b0": (4, 2, 1, 0), "b1": (5,), "b2": (3,), "b3": (2,), "b5": (4, 1), "b7": (0, 3), "b9": (4, 5, 1, 0),
}


def main_kernel(
    R, su, occ, linv, small, Wh, Oh, h0h, dYh, ETh, OTh, qh, kTh, vh, a1sh, a1qh, n1sh, n1qh, rsh, rqh, XTh,
    out, FIN, SM, EM, GI,
    W, O_s, y_s, dY, ETb, OT, qs, kT, a1q, n1s, n1q, rs, rq, XT,
    a2_s, G_s, dU_s, Dp, sg, eg, GT, S, RC, RX, RH, AG0, AG1, AGL, SY, RY, SEL, PK, RK, GC, XS, XR,
    lsem, esem, osem, ss, sr, ys, yr, fs, fr, ps, pr, gs, gr,
):
    f = lax.axis_index("feat")
    r = lax.axis_index("rows")
    x = f // 2
    c = f % 2
    n = R.bit_length() - 1
    BH = S.shape[4]
    per = D // (2 * BH)
    core_id = (f ^ 1, r)
    x_id = (f ^ 2, r)
    row_id = [(f, r ^ (1 << j)) for j in range(n)]
    peers = [core_id, x_id] + row_id
    bar = greet(peers)

    loads = {}

    def load(name, src, dst):
        loads[name] = pltpu.make_async_copy(src, dst, lsem.at[len(loads)])
        loads[name].start()

    def rows_w(i):
        return pl.ds(i * D, D)

    load("O", Oh, O_s)
    load("h0", h0h, y_s)
    for i in (3, 4, 8, 5, 9, 6, 10, 7, 11):
        load(i, Wh.at[rows_w(i)], W.at[rows_w(i)])
    load("dY", dYh, dY)
    load("OT", OTh, OT)
    load("q", qh, qs)
    load("kT", kTh, kT)

    def ecopy(h, t):
        k = (h % 2) * 2 + t
        return pltpu.make_async_copy(ETh.at[t * HEADS + h], ETb.at[k], esem.at[k])

    for h in range(2):
        for t in range(2):
            ecopy(h, t).start()
    load("a1q", a1qh, a1q)
    load("n1s", n1sh, n1s)
    load("n1q", n1qh, n1q)
    load("rs", rsh, rs)
    load("rq", rqh, rq)
    load("XT", XTh, XT)
    for i in range(3):
        load(i, Wh.at[rows_w(i)], W.at[rows_w(i)])
    pl.semaphore_wait(bar, len(peers))

    bits = [(r >> j) & 1 for j in range(n)]
    base = [0]
    for j in range(n):
        base.append(base[j] + bits[j] * (R >> (j + 1)))

    def core_copy(g):
        return remote(S.at[1 - c, :, g], RC.at[:, g], ss.at[g, 0], sr.at[g, 0], core_id)

    def x_copy(g):
        return remote(S.at[c, 1 - x, g], RX.at[g], ss.at[g, 1], sr.at[g, 1], x_id)

    def rs_copy(g, j):
        half = R >> (j + 1)
        away = base[j] + (1 - bits[j]) * half
        off = R - (R >> j)
        return remote(
            S.at[c, x, g, pl.ds(away, half)], RH.at[g, pl.ds(off, half)],
            ss.at[g, 2 + j], sr.at[g, 2 + j], row_id[j],
        )

    def swap_copy(g):
        span = pl.ds(base[n - 1], 2)
        return remote(S.at[c, x, g, span], RH.at[g, pl.ds(R - 2, 2)], ss.at[g, 1 + n], sr.at[g, 1 + n], row_id[n - 1])

    def total_of(g):
        return AGL if g == 5 else AG1.at[g // 2] if g % 2 else AG0.at[(g // 2 + 1) % 3]

    def ag_copy(g, j):
        ref = total_of(g).at[pl.ds(base[j + 1] - base[1], R >> (j + 1))]
        return remote(ref, ref, ss.at[g, 2 + n + j], sr.at[g, 2 + n + j], row_id[j])

    def add(a, b):
        return (a.astype(f32) + b.astype(f32)).astype(bf16)

    def step(g, stage):
        if stage == 0:
            core_copy(g).wait_recv()
            S[c, 1 - x, g] = add(S[c, 1 - x, g], RC[1 - x, g])
            x_copy(g).start()
            S[c, x, g] = add(S[c, x, g], RC[x, g])
        elif stage == 1:
            x_copy(g).wait_recv()
            S[c, x, g] = add(S[c, x, g], RX[g])
            rs_copy(g, 0).start()
        elif stage < 1 + n:
            j = stage - 2
            half = R >> (j + 1)
            off = R - (R >> j)
            rs_copy(g, j).wait_recv()
            keep = pl.ds(base[j + 1], half)
            S[c, x, g, keep] = add(S[c, x, g, keep], RH[g, pl.ds(off, half)])
            if j < n - 2:
                rs_copy(g, j + 1).start()
            else:
                swap_copy(g).start()
        elif stage == 1 + n:
            swap_copy(g).wait_recv()
            total_of(g)[pl.ds(base[n - 1] - base[1], 2)] = add(S[c, x, g, pl.ds(base[n - 1], 2)], RH[g, pl.ds(R - 2, 2)])
            if n > 2:
                ag_copy(g, n - 2).start()
        else:
            j = 2 * n - stage
            ag_copy(g, j).wait_recv()
            if j > 1:
                ag_copy(g, j - 1).start()

    def select(m, who):
        picked = []
        for s in range(4):
            u = su[who * 4 + s]
            p = lax.rem(u, R // 2)
            q = lax.div(u, R)
            k = who * 4 + s
            if m == 0:
                picked.append(AG0[q, p].astype(f32) * occ[4 + k].astype(f32))
            else:
                picked.append(AG1[lax.max(q - 1, 0), p].astype(f32) * occ[12 + k].astype(f32) + AGL[p].astype(f32) * occ[20 + k].astype(f32))
        return picked

    def y_copy(m):
        return remote(SY.at[m], RY.at[m], ys.at[m], yr.at[m], row_id[0])

    def fin(m, k):
        if k == 3:
            return pltpu.make_async_copy(SEL.at[m], FIN.at[m, f], osem.at[1 + m])
        src, at = (FIN.at[m, f ^ 2], f ^ 2) if k == 2 else (SEL.at[m], f)
        return remote(src, FIN.at[m, at], fs.at[m, k], fr.at[m, k], x_id if k == 1 else core_id)

    def fin_step(m, stage):
        if stage == 0:
            for s, value in enumerate(select(m, 1)):
                SY[m, s] = value.astype(bf16)
            y_copy(m).start()
            for s, value in enumerate(select(m, 0)):
                SEL[m, s] = value.astype(bf16)
        elif stage == 1:
            y_copy(m).wait_recv()
            SEL[m] = add(SEL[m], RY[m])
            for k in (1, 0, 3):
                fin(m, k).start()
        else:
            fin(m, 1).wait_recv()
            fin(m, 2).start()

    last = 2 * n
    done = [0] * 6
    ended = [0, 0]

    def tick(g):
        if done[g] < last:
            step(g, done[g])
            done[g] += 1

    def finish(m):
        if ended[m] < 3 and all(done[g] == last for g in (m, 2 + m, 4 + m)):
            fin_step(m, ended[m])
            ended[m] += 1

    def after(piece):
        for g in AFTER.get(piece, ()):
            tick(g)

    def put(g0, i, val):
        for k in range(val.shape[1] // 128):
            piece = val[:, k * 128:(k + 1) * 128].reshape(per, 2, BH, 128)
            for h in range(2):
                S[k % 2, h, g0 + k // 2, pl.ds(i * per, per)] = piece[:, h]

    gain2 = small[3:4]
    shift2 = small[4:5]
    RB = 256

    def norm2(y1):
        cen = y1 - jnp.mean(y1, axis=-1, keepdims=True)
        rstd = lax.rsqrt(jnp.mean(cen * cen, axis=-1, keepdims=True) + LN_EPS)
        return cen * rstd, rstd

    loads["O"].wait()
    loads["h0"].wait()
    loads[3].wait()

    @pl.loop(0, 1024 // RB)
    def _(i):
        rows = pl.ds(pl.multiple_of(i * RB, RB), RB)
        y1 = y_s[rows] + dot(O_s[rows], W[rows_w(3)])
        y_s[rows] = y1
        n2, _ = norm2(y1)
        a2 = (n2 * gain2 + shift2).astype(bf16)
        a2_s[rows] = a2
        acc = y1 + small[5:6]
        for j in range(4):
            @pl.when(i == 0)
            def _():
                loads[4 + j].wait()
                loads[8 + j].wait()
            gl, gp = gelu_pair(dot(a2, W[rows_w(4 + j)]) + small[6 + j:7 + j])
            gb = gl.astype(bf16)
            G_s[j, rows] = gb
            dU_s[j, rows] = gp.astype(bf16)
            acc = acc + dot(gb, W[rows_w(8 + j)])
        O_s[rows] = acc.astype(bf16)

    ship_out = pltpu.make_async_copy(O_s, out, osem.at[0])
    ship_out.start()
    loads["dY"].wait()

    @pl.loop(0, 4)
    def _(j):
        put(2, j, dot(G_s[j], dY[...], TN).astype(bf16))

    core_copy(2).start()
    core_copy(3).start()

    sg[...] = jnp.zeros_like(sg)

    def backward_rows(i):
        rows = pl.ds(i * RB, RB)
        dy = dY[rows]
        da2 = jnp.zeros((RB, D), f32)
        for j in range(4):
            du = (dot(dy, W[rows_w(8 + j)], NT) * dU_s[j, rows].astype(f32)).astype(bf16)
            dU_s[j, rows] = du
            sg[6 + j:7 + j] += jnp.sum(du.astype(f32), axis=0, keepdims=True)
            da2 = da2 + dot(du, W[rows_w(4 + j)], NT)
        n2, rstd = norm2(y_s[rows])
        dyf = dy.astype(f32)
        sg[3:4] += jnp.sum(da2 * n2, axis=0, keepdims=True)
        sg[4:5] += jnp.sum(da2, axis=0, keepdims=True)
        sg[5:6] += jnp.sum(dyf, axis=0, keepdims=True)
        cc = da2 * gain2
        m1 = jnp.mean(cc, axis=-1, keepdims=True)
        m2 = jnp.mean(cc * n2, axis=-1, keepdims=True)
        y_s[rows] = dyf + rstd * (cc - m1 - n2 * m2)

    for i in range(1024 // RB):
        backward_rows(i)
        after("fb%d" % i)
    vs = W.at[pl.ds(4 * D, 4 * D)]
    a1s = W.at[pl.ds(8 * D, 4 * D)]
    load("v", vh, vs)
    load("a1s", a1sh, a1s)

    @pl.loop(0, 4)
    def _(j):
        put(0, j, dot(a2_s[...], dU_s[j], TN).astype(bf16))

    core_copy(0).start()
    core_copy(1).start()
    after("up")

    scale = HEAD_DIM**-0.5
    for i in range(2):
        dU_s[1, pl.ds(i * 512, 512)] = y_s[pl.ds(i * 512, 512)].astype(bf16)
    for name in ("OT", "v", "q", "kT", "a1s", "a1q"):
        loads[name].wait()
    put(4, 3, dot(OT[...], dU_s[1]).astype(bf16))

    @pl.loop(0, 2)
    def _(t):
        cols = pl.ds(pl.multiple_of(t * 512, 512), 512)
        whole = dot(W[rows_w(3)], dU_s[1, cols], NT)
        for h in range(HEADS):
            rows = pl.ds(h * HEAD_DIM, HEAD_DIM)
            d = whole[h * HEAD_DIM:(h + 1) * HEAD_DIM] * linv[pl.ds(t * HEADS + h, 1)]
            Dp[pl.ds(t * HEADS + h, 1)] = jnp.sum(d * OT[rows, cols].astype(f32), axis=0, keepdims=True)
            dU_s[2, pl.ds(pl.multiple_of(t * 512 + h * HEAD_DIM, HEAD_DIM), HEAD_DIM)] = d.astype(bf16)

    after("mix")

    def heads(h):
        hs = pl.ds(h * HEAD_DIM, HEAD_DIM)
        for t in range(2):
            ecopy(h, t).wait()

        @pl.loop(0, 2)
        def _(t):
            i = t * HEADS + h
            ksl = pl.ds(pl.multiple_of(t * HALF, HALF), HALF)
            qsl = pl.ds(pl.multiple_of(t * 512, 512), 512)
            do = dU_s[2, pl.ds(pl.multiple_of(t * 512 + h * HEAD_DIM, HEAD_DIM), HEAD_DIM)]
            dp = dot(vs[ksl, hs], do)
            e = ETb[(h % 2) * 2 + t]
            ds = (e.astype(f32) * (dp - Dp[pl.ds(i, 1)])).astype(bf16)
            G_s[2 + t, :, hs] = dot(e, do, NT).astype(bf16)
            G_s[t, :, hs] = (dot(ds, qs[qsl, hs]) * (1.0 / LOG2E)).astype(bf16)
            dqT = (dot(kT[hs, ksl], ds) * scale).astype(bf16)
            dU_s[0, qsl, hs] = dqT.T

        for t in range(2):
            if h + 2 < HEADS:
                ecopy(h + 2, t).start()
            after("h%d%d" % (h, t))

    def weight_grads(m):
        cols = pl.ds(m * 256, 256)
        acc = jnp.zeros((D, 256), f32)
        for t in range(2):
            sup = pl.multiple_of(t * HALF + f * QUART, QUART)
            acc += dot(a1s[pl.ds(sup, QUART)], dU_s[0, pl.ds(t * 512, QUART), cols], TN)
            acc += dot(a1q[pl.ds(t * QUART, QUART)], dU_s[0, pl.ds(t * 512 + QUART, QUART), cols], TN)
        put(4 + m, 0, acc.astype(bf16))
        for k in range(2):
            total = dot(a1s[pl.ds(0, HALF)], G_s[2 * k, :, cols], TN) + dot(a1s[pl.ds(HALF, HALF)], G_s[2 * k + 1, :, cols], TN)
            put(4 + m, 1 + k, total.astype(bf16))

    for m in range(2):
        heads(2 * m)
        heads(2 * m + 1)
        weight_grads(m)
        core_copy(4 + m).start()
        after("w%d" % m)

    eg[...] = jnp.zeros_like(eg)
    gain1 = small[1:2]
    emb_cols = pl.ds(2 * HALF, D)
    for name in ("n1s", "n1q", "rs", "rq", "XT", 0, 1, 2):
        loads[name].wait()

    def back(da, nrm, rstd, extra, cols, out_cols):
        sg[1:2] += jnp.sum(da * nrm, axis=0, keepdims=True)
        sg[2:3] += jnp.sum(da, axis=0, keepdims=True)
        cc = da * gain1
        m1 = jnp.mean(cc, axis=-1, keepdims=True)
        m2 = jnp.mean(cc * nrm, axis=-1, keepdims=True)
        wide = jnp.concatenate([rstd] * 4, axis=1)
        dh = wide * (cc - m1 - nrm * m2)
        if extra is not None:
            dh = dh + extra
        sg[0:1] += jnp.sum(dh, axis=0, keepdims=True)
        de = dh.astype(bf16)
        part = dot(XT[:, cols], de)
        back_in = dot(XT[:, emb_cols], de, NT).astype(bf16)
        for k in range(4):
            eg[k] += part[k * PADF:(k + 1) * PADF]
            GT[k % 2, k // 2, :, out_cols] = back_in[k * PADF:(k + 1) * PADF]

    def below(t):
        q0 = t * 512
        wq, wk, wv = W[rows_w(0)], W[rows_w(1)], W[rows_w(2)]
        da = dot(dU_s[0, pl.ds(q0 + QUART, QUART)], wq, NT)
        p0 = pl.ds(t * QUART, QUART)
        back(
            da, n1q[p0].astype(f32), rq[p0], y_s[pl.ds(q0 + QUART, QUART)],
            pl.ds(2 * HALF + D + t * QUART, QUART), pl.ds(2 * HALF + t * QUART, QUART),
        )
        after("b%d" % (5 * t))
        for b in range(4):
            at = pl.ds(pl.multiple_of(((f + b) % 4) * QUART, QUART), QUART)
            rows = pl.ds(pl.multiple_of(t * HALF + ((f + b) % 4) * QUART, QUART), QUART)
            da = dot(G_s[t, at], wk, NT) + dot(G_s[2 + t, at], wv, NT)
            extra = None
            if b == 0:
                da = da + dot(dU_s[0, pl.ds(q0, QUART)], wq, NT)
                extra = y_s[pl.ds(q0, QUART)]
            back(da, n1s[rows].astype(f32), rs[rows], extra, rows, rows)
            if 5 * t + b < 8:
                after("b%d" % (5 * t + b + 1))

    below(0)
    below(1)

    small_rows = pl.ds(0, 16)
    PK[0, small_rows] = sg[...]
    for k in range(2):
        PK[0, pl.ds(16 + k * PADF, PADF)] = eg[2 * k + 1 - c]

    def pk_copy(i):
        rows = pl.ds(0, 80 if i == 0 else 48)
        dev = core_id if i == 0 else x_id if i == 1 else row_id[i - 2]
        return remote(PK.at[i, rows], RK.at[i, rows], ps.at[i], pr.at[i], dev)

    def pk_step(i):
        pk_copy(i).wait_recv()
        if i == 0:
            PK[1, small_rows] = PK[0, small_rows] + RK[0, small_rows]
            own = [eg[2 * k + c] + RK[0, pl.ds(16 + k * PADF, PADF)] for k in range(2)]
            PK[1, pl.ds(16, PADF)] = jnp.where(x == 0, own[1], own[0])
            PK[1, pl.ds(48, PADF)] = jnp.where(x == 0, own[0], own[1])
            pk_copy(1).start()
        else:
            old = PK[1, pl.ds(48, PADF)] if i == 1 else PK[i, pl.ds(16, PADF)]
            a = PK[i, small_rows] + RK[i, small_rows]
            b = old + RK[i, pl.ds(16, PADF)]
            if i < n + 1:
                PK[i + 1, small_rows] = a
                PK[i + 1, pl.ds(16, PADF)] = b
                pk_copy(i + 1).start()
            else:
                SM[...] = a
                EM[...] = b

    pk_copy(0).start()
    gt1 = remote(GT.at[1 - c], GC, gs.at[0], gr.at[0], core_id)
    gt1.start()
    sup = pl.ds(0, 2 * HALF)
    que = pl.ds(2 * HALF, 512)

    def que_of(k):
        return pl.ds(pl.multiple_of(2 * HALF + k * 512, 512), 512)

    gt2 = remote(XS, XR, gs.at[1], gr.at[1], x_id)
    after("b9")
    pk_step(0)
    gt1.wait_recv()
    XS[:, sup] = add(GT[c, 1 - x, :, sup], GC[1 - x, :, sup])
    XS[:, que_of(c)] = GT[c, 1 - x, :, que]
    XS[:, que_of(1 - c)] = GC[1 - x, :, que]
    gt2.start()
    next_pk = 1
    while min(done) < last:
        for g in (4, 5, 2, 3, 1, 0):
            tick(g)
        finish(0)
        if next_pk < n + 2:
            pk_step(next_pk)
            next_pk += 1
    finish(1)
    finish(0)
    for i in range(next_pk, n + 2):
        pk_step(i)
    gt2.wait_recv()
    GI[:, sup] = (
        GT[c, x, :, sup].astype(f32) + GC[x, :, sup].astype(f32) + XR[:, sup].astype(f32)
    ).astype(bf16)
    GI[:, que_of(f)] = GT[c, x, :, que]
    GI[:, que_of(f ^ 1)] = GC[x, :, que]
    for k in range(2):
        GI[:, que_of(2 * (1 - x) + k)] = XR[:, pl.ds(2 * HALF + k * 512, 512)]
    while min(ended) < 3:
        finish(0)
        finish(1)
    for m in range(2):
        y_copy(m).wait_send()
        fin(m, 0).wait()
        fin(m, 1).wait_send()
        fin(m, 2).wait()
        fin(m, 3).wait()
    for g in range(6):
        core_copy(g).wait_send()
        x_copy(g).wait_send()
        swap_copy(g).wait_send()
        for j in range(n - 1):
            rs_copy(g, j).wait_send()
        for j in range(1, n - 1):
            ag_copy(g, j).wait_send()
    for i in range(n + 2):
        pk_copy(i).wait_send()
    gt1.wait_send()
    gt2.wait_send()
    ship_out.wait()


def main_call(R, su, occ, linv, small, W, O, h0, dY, ET, OT, q, kT, v, a1s, a1q, n1s, n1q, rs, rq, XT):
    BH = 12 * D // (3 * R) // 2
    n = R.bit_length() - 1
    sd = jax.ShapeDtypeStruct
    V = pltpu.VMEM
    dma = pltpu.SemaphoreType.DMA
    blk = (R, BH, 128)
    like = lambda a: V(a.shape, a.dtype)
    return pl.pallas_call(
        functools.partial(main_kernel, R),
        out_shape=(sd((1024, D), bf16), sd((2, 4, 4, BH, 128), bf16), sd((16, D), f32), sd((PADF, D), f32), sd((PADF, 4096), bf16)),
        in_specs=[smem(), smem(), vmem(), vmem()] + [anyspace()] * 16,
        out_specs=(anyspace(), anyspace(), vmem(), vmem(), vmem()),
        scratch_shapes=[
            like(W), like(O), like(h0), like(dY), V((4, HALF, 512), bf16), like(OT), like(q), like(kT),
            like(a1q), like(n1s), like(n1q), like(rs), like(rq), like(XT),
            V((1024, D), bf16), V((4, 1024, 512), bf16), V((4, 1024, 512), bf16), V((8, 512), f32), V((16, D), f32),
            V((4, PADF, D), f32), V((2, 2, PADF, 2560), bf16),
            V((2, 2, 6) + blk, bf16), V((2, 6) + blk, bf16), V((6,) + blk, bf16), V((6,) + blk, bf16), V((3, R // 2, BH, 128), bf16), V((2, R // 2, BH, 128), bf16), V((R // 2, BH, 128), bf16),
            V((2, 4, BH, 128), bf16), V((2, 4, BH, 128), bf16), V((2, 4, BH, 128), bf16), V((n + 2, 80, D), f32), V((n + 2, 80, D), f32),
            V((2, PADF, 2560), bf16), V((PADF, 3072), bf16), V((PADF, 3072), bf16),
            dma((26,)), dma((4,)), dma((3,)), dma((6, 2 + 2 * n)), dma((6, 2 + 2 * n)), dma((2,)), dma((2,)), dma((2, 3)), dma((2, 3)),
            dma((n + 2,)), dma((n + 2,)), dma((2,)), dma((2,)),
        ],
        compiler_params=pltpu.CompilerParams(collective_id=1, has_side_effects=True, vmem_limit_bytes=VMEM_BYTES),
        name="main",
    )(su, occ, linv, small, W, O, h0, dY, ET, OT, q, kT, v, a1s, a1q, n1s, n1q, rs, rq, XT)


def adamw(weight, grad, first, second, rate):
    first_new = BETA_FIRST * first + (1.0 - BETA_FIRST) * grad
    second_new = BETA_SECOND * second + (1.0 - BETA_SECOND) * grad * grad
    first_hat = first_new * (1.0 / (1.0 - BETA_FIRST**STEP))
    second_hat = second_new * (1.0 / (1.0 - BETA_SECOND**STEP))
    weight_new = weight - rate * (first_hat / (jnp.sqrt(second_hat) + ADAM_EPS) + DECAY * weight)
    return (first_new, second_new, weight_new)


def update_kernel(
    occ, tmap, FIN, w, m, v, SM, sw, sm, sv, EM, ew, em, ev, GI, masks, lo,
    g_o, m_o, v_o, w_o, wc_o, eg_o, em_o, ev_o, ew_o, ec_o, sg_o, sm_o, sv_o, sw_o, gi_o, lo_o,
):
    s = pl.program_id(0)
    BH = FIN.shape[3]
    for slot in range(2):
        keep = occ[2 * s + slot].astype(f32)
        for f in range(4):
            rows = pl.ds((f // 2) * BH, BH)
            for k in range(2):
                cols = pl.ds(k * 256 + (f % 2) * 128, 128)
                g = FIN[k, f, slot].astype(f32)
                a, b, d = adamw(w[slot, rows, cols], g, m[slot, rows, cols], v[slot, rows, cols], RATE_MATRIX)
                g_o[slot, rows, cols] = g * keep
                m_o[slot, rows, cols] = a * keep
                v_o[slot, rows, cols] = b * keep
                d = d * keep
                w_o[slot, rows, cols] = d
                wc_o[slot, rows, cols] = d.astype(bf16)

    @pl.when(s == 0)
    def _():
        g = SM[0:10]
        a, b, d = adamw(sw[...], g, sm[...], sv[...], RATE_SMALL)
        sg_o[...] = g
        sm_o[...] = a
        sv_o[...] = b
        sw_o[...] = d
        nf = ew.shape[0]
        g = EM[pl.ds(0, nf)]
        a, b, d = adamw(ew[...], g, em[...], ev[...], RATE_EMBED)
        eg_o[...] = g
        em_o[...] = a
        ev_o[...] = b
        ew_o[...] = d
        ec_o[...] = d.astype(bf16)

    nf = gi_o.shape[1]
    t = s
    keep_in = mask_column(masks, tmap[t])
    cols = pl.ds(pl.multiple_of(t * HALF, HALF), HALF)
    gi_o[t, :, 0, :] = (GI[pl.ds(0, nf), cols].astype(f32) * keep_in).astype(bf16)
    for k in range(4):
        cols = pl.ds(pl.multiple_of(2 * HALF + k * 512 + t * QUART, QUART), QUART)
        gi_o[t, :, 1, pl.ds(k * QUART, QUART)] = (GI[pl.ds(0, nf), cols].astype(f32) * keep_in).astype(bf16)

    lo_o[...] = lo[...]


def update_call(occ, tmap, FIN, w, m, v, SM, sw, sm, sv, EM, ew, em, ev, GI, masks, lo):
    S, BR, W = w.shape
    nf = ew.shape[0]
    sd = jax.ShapeDtypeStruct
    blk = pl.BlockSpec((2, BR, W), lambda s: (s, 0, 0))
    whole = lambda a: pl.BlockSpec(a.shape, lambda s: (0,) * len(a.shape))
    ins = [smem(), smem(), pl.BlockSpec((2, 4, 2, BR // 2, 128), lambda s: (0, 0, s, 0, 0)), blk, blk, blk]
    ins += [whole(a) for a in (SM, sw, sm, sv, EM, ew, em, ev, GI, masks)] + [pl.BlockSpec((2048 // S, D), lambda s: (s, 0))]
    big = sd((S, BR, W), f32)
    small = sd((10, D), f32)
    e = sd((nf, D), f32)
    outs = [big, big, big, big, sd((S, BR, W), bf16), e, e, e, e, sd((nf, D), bf16), small, small, small, small, sd((2, nf, 2, HALF), bf16), sd(lo.shape, lo.dtype)]
    specs = [blk] * 5 + [whole(a) for a in outs[5:14]] + [whole(outs[14]), pl.BlockSpec((2048 // S, D), lambda s: (s, 0))]
    return pl.pallas_call(
        update_kernel, out_shape=tuple(outs), grid=(S // 2,), in_specs=ins, out_specs=tuple(specs),
        compiler_params=pltpu.CompilerParams(vmem_limit_bytes=VMEM_BYTES), name="update",
    )(occ, tmap, FIN, w, m, v, SM, sw, sm, sv, EM, ew, em, ev, GI, masks, lo)


def body(
    features, feature_masks, table_map, owners, out_grad, weight_slots, moment1_slots, moment2_slots,
    emb_weight, emb_moment1, emb_moment2, small_weight, small_moment1, small_moment2,
):
    width = weight_slots.shape[2]
    R = lax.axis_size("rows")
    slot_unit, kinds, XT, h0o, a1s, a1q, n1s, n1q, rs, rq, linv, W, q, kT, v, ET, OT, O = gather_call(
        R, weight_slots, features.transpose(0, 3, 1, 2), feature_masks, table_map, owners, emb_weight, small_weight
    )
    dY = out_grad.reshape(1024, width)
    out, FIN, SM, EM, GI = main_call(
        R, slot_unit, kinds, linv, small_weight, W, O, h0o, dY, ET, OT, q, kT, v, a1s, a1q, n1s, n1q, rs, rq, XT
    )
    (
        g_slots, m_slots, v_slots, w_slots, w_copy, e_grad, e_m, e_v, e_w, e_copy, s_grad, s_m, s_v, s_w, grad_inputs, out,
    ) = update_call(
        kinds, table_map, FIN, weight_slots, moment1_slots, moment2_slots, SM, small_weight, small_moment1,
        small_moment2, EM, emb_weight, emb_moment1, emb_moment2, GI, feature_masks, out,
    )
    grad_inputs = grad_inputs.transpose(0, 2, 3, 1)
    return (
        out.reshape(out_grad.shape), grad_inputs, g_slots, m_slots, v_slots, w_slots, w_copy,
        e_grad, e_m, e_v, e_w, e_copy, s_grad, s_m, s_v, s_w,
    )


def solution(mesh):
    rows3 = P("rows", None, None)
    feat2 = P("feat", None)
    in_specs = (
        P("rows", None, None, "feat"), P(None, "feat"), P("rows"), P(), P("rows", None, "feat", None),
        rows3, rows3, rows3, feat2, feat2, feat2, P(), P(), P(),
    )
    out_specs = (
        P("rows", None, "feat", None), P("rows", None, None, "feat"), rows3, rows3, rows3, rows3, rows3,
        feat2, feat2, feat2, feat2, feat2, P(), P(), P(), P(),
    )
    return jax.shard_map(body, mesh=mesh, in_specs=in_specs, out_specs=out_specs, check_vma=False)
```

```python
import functools
import math

import jax
import jax.numpy as jnp
from jax import lax
from jax.experimental import pallas as pl
from jax.experimental.pallas import tpu as pltpu
from jax.sharding import PartitionSpec as P

MESH = pl.DeviceIdType.MESH
bf16, f32 = jnp.bfloat16, jnp.float32
NN = (((1,), (0,)), ((), ()))
NT = (((1,), (1,)), ((), ()))
TN = (((0,), (0,)), ((), ()))
LOG2E = math.log2(math.e)
HEADS = 4
HEAD_DIM = 128
STEP = 10
LN_EPS = 1e-05
BETA_FIRST = 0.9
BETA_SECOND = 0.999
ADAM_EPS = 1e-08
DECAY = 0.01
RATE_MATRIX = 0.1
RATE_EMBED = 0.3
RATE_SMALL = 0.6
D = 512
HALF = 1024
QUART = 256
PADF = 32
VMEM_BYTES = 60 * 2**20


def dot(a, b, dims=NN):
    return lax.dot_general(a, b, dims, preferred_element_type=f32)


def vmem():
    return pl.BlockSpec(memory_space=pltpu.VMEM)


def anyspace():
    return pl.BlockSpec(memory_space=pl.ANY)


def smem():
    return pl.BlockSpec(memory_space=pltpu.SMEM)


def remote(src, dst, send, recv, dev):
    return pltpu.make_async_remote_copy(
        src_ref=src, dst_ref=dst, send_sem=send, recv_sem=recv, device_id=dev, device_id_type=MESH
    )


def greet(peers):
    bar = pltpu.get_barrier_semaphore()
    for d in peers:
        pl.semaphore_signal(bar, inc=1, device_id=d, device_id_type=MESH)
    return bar


def mask_column(masks, table):
    T, nf = masks.shape
    which = lax.broadcasted_iota(jnp.int32, (T, nf), 0) == table
    line = jnp.sum(jnp.where(which, masks[...], 0), axis=0, keepdims=True)
    eye = lax.broadcasted_iota(jnp.int32, (nf, nf), 0) == lax.broadcasted_iota(jnp.int32, (nf, nf), 1)
    return jnp.sum(jnp.where(eye, jnp.broadcast_to(line, (nf, nf)), 0), axis=1, keepdims=True).astype(f32)


GROUPS = (True, False)


def gather_kernel(
    R, slots_ref, feat_ref, mask_ref, tmap_ref, own_ref, emb_ref, small_ref,
    su_ref, kind_ref, XT_ref, h0_ref, a1s_ref, a1q_ref, n1s_ref, n1q_ref, rs_ref, rq_ref, linv,
    Wo, qo, kTo, vo, ET, OT, Oo,
    pos, G0, G1, own, XTo, XTa, tmpq, W, q_s, k_s, kT_s, v_s, vT_s, ET_s, OT_s, O_s,
    lsem, osem, esem, fs, fr, hs, hr, xs, xr, cs, cr, c2s, c2r,
):
    f = lax.axis_index("feat")
    r = lax.axis_index("rows")
    x = f // 2
    c = f % 2
    n = R.bit_length() - 1
    S, BR = slots_ref.shape[:2]
    U = own_ref.shape[0]
    BH = BR // 2
    Gs = (G0, G1)
    core_id = (f ^ 1, r)
    x_id = (f ^ 2, r)
    row_id = [(f, r ^ (1 << (n - 1 - j))) for j in range(n)]
    peers = [core_id, x_id] + row_id
    bar = greet(peers)
    for k in range(4):
        own[k // 2, k % 2] = slots_ref[:, :, k * 128:(k + 1) * 128].astype(bf16)
    pl.semaphore_wait(bar, len(peers))

    def keep_own(p):
        return pltpu.make_async_copy(own.at[p], Gs[p].at[:, 0], lsem.at[p])

    subs = [(j, g) for j in range(n) for g in range(-1, j)]
    index = {jg: i for i, jg in enumerate(subs)}
    rows_c = pl.ds(pl.multiple_of(c * BH, BH), BH)

    def part(p, s, half, start, size):
        if GROUPS[s]:
            return Gs[p].at[half, pl.ds(start, size), pl.ds(1, 3), rows_c]
        return Gs[p].at[:, pl.ds(start, size), 0, rows_c]

    def hyper(p, s, j, g):
        k = index[(j, g)]
        if g < 0:
            if GROUPS[s]:
                src, dst = own.at[p, x, pl.ds(1, 3), rows_c], Gs[p].at[x, 1 << j, pl.ds(1, 3), rows_c]
            else:
                src, dst = own.at[p, :, 0, rows_c], Gs[p].at[:, 1 << j, 0, rows_c]
        else:
            src, dst = part(p, s, x, 1 << g, 1 << g), part(p, s, x, (1 << j) + (1 << g), 1 << g)
        return remote(src, dst, hs.at[p, s, k], hr.at[p, s, k], row_id[j])

    def forward(p, s, j, g, half, sems, semr, dev):
        start, size = (0, 1) if g < 0 else (1 << g, 1 << g)
        k = index[(j, g)]
        ref = part(p, s, half, (1 << j) + start, size)
        return remote(ref, ref, sems.at[p, s, k], semr.at[p, s, k], dev)

    def to_x(p, s, j, g):
        return forward(p, s, j, g, x, xs, xr, x_id)

    def to_core(p, s, j, g):
        return forward(p, s, j, g, x, cs, cr, core_id)

    def to_core_x(p, s, j, g):
        return forward(p, s, j, g, 1 - x, c2s, c2r, core_id)

    order = range(len(GROUPS))

    def send_own(p):
        for s in order:
            for j in range(n):
                hyper(p, s, j, -1).start()
        keep_own(p).start()

    def x_arrive(p, j):
        for s in order:
            if GROUPS[s]:
                for g in range(-1, j):
                    to_x(p, s, j, g).wait_recv()
                    to_core_x(p, s, j, g).start()

    def hyper_arrive(p, j):
        for s in order:
            for g in range(-1, j):
                hyper(p, s, j, g).wait_recv()
                if GROUPS[s]:
                    to_x(p, s, j, g).start()
                to_core(p, s, j, g).start()
            for j2 in range(j + 1, n):
                hyper(p, s, j2, j).start()

    def all_here(p):
        keep_own(p).wait()
        for s in order:
            for j, g in subs:
                to_core(p, s, j, g).wait_recv()
                if GROUPS[s]:
                    to_core_x(p, s, j, g).wait_recv()

    def all_sent(p):
        for s in order:
            for j, g in subs:
                hyper(p, s, j, g).wait_send()
                to_core(p, s, j, g).wait_send()
                if GROUPS[s]:
                    to_x(p, s, j, g).wait_send()
                    to_core_x(p, s, j, g).wait_send()

    send_own(0)

    nf = feat_ref.shape[1]
    XTo[...] = jnp.zeros_like(XTo)
    for t in range(2):
        keep = mask_column(mask_ref, tmap_ref[t])
        XTo[pl.ds(0, nf), pl.ds(t * HALF, HALF)] = (feat_ref[t, :, 0, :].astype(f32) * keep).astype(bf16)
        query = (feat_ref[t, :, 1, :].astype(f32) * keep).astype(bf16)
        for k in range(4):
            XTo[pl.ds(0, nf), pl.ds(2 * HALF + D + k * 512 + t * QUART, QUART)] = query[:, k * QUART:(k + 1) * QUART]
    XTo[pl.ds(0, nf), pl.ds(2 * HALF, D)] = emb_ref[...].astype(bf16)
    wide = 2 * HALF + D
    shared = pl.ds(0, wide)
    tail = pl.ds(wide, 512)

    def rows_of(dev):
        return pl.ds(pl.multiple_of(dev * PADF, PADF), PADF)

    def chunk_of(dev):
        return pl.ds(pl.multiple_of(wide + dev * 512, 512), 512)

    feats = [
        remote(XTo.at[:, shared], XTa.at[rows_of(f), shared], fs.at[0], fr.at[0], core_id),
        remote(XTo.at[:, chunk_of(f ^ 1)], XTa.at[rows_of(f), tail], fs.at[1], fr.at[1], core_id),
        remote(XTo.at[:, shared], XTa.at[rows_of(f), shared], fs.at[2], fr.at[2], x_id),
        remote(XTo.at[:, chunk_of(f ^ 2)], XTa.at[rows_of(f), tail], fs.at[3], fr.at[3], x_id),
        remote(XTo.at[:, chunk_of(f ^ 3)], tmpq, fs.at[4], fr.at[4], x_id),
        remote(XTa.at[rows_of(f ^ 2), shared], XTa.at[rows_of(f ^ 2), shared], fs.at[5], fr.at[5], core_id),
        remote(tmpq, XTa.at[rows_of(f ^ 2), tail], fs.at[6], fr.at[6], core_id),
    ]
    for copy in feats[:5]:
        copy.start()
    XTa[rows_of(f), shared] = XTo[:, shared]
    XTa[rows_of(f), tail] = XTo[:, chunk_of(f)]

    for k in range(2 * S):
        su_ref[k] = 0
    for k in range(7 * S):
        kind_ref[k] = 0

    @pl.loop(0, U)
    def _(u):
        owner = own_ref[u]
        rank = lax.fori_loop(0, u, lambda j, total: total + jnp.where(own_ref[j] == owner, 1, 0), 0)
        distance = owner ^ r
        place = 0
        for bit in range(n):
            place = place + (((distance >> bit) & 1) << (n - 1 - bit))
        pos[u] = place * S + jnp.minimum(rank, S - 1)
        for k in range(2 * S):
            hit = jnp.where(owner == r ^ (k // S), 1, 0) * jnp.where(rank == k % S, 1, 0)
            su_ref[k] = su_ref[k] + hit * u
            here = hit * jnp.where((u % R) // (R // 2) == r % 2, 1, 0)
            late = here * jnp.where(u < R, 1, 0)
            if k < S:
                kind_ref[k] = kind_ref[k] + hit
            kind_ref[S + k] = kind_ref[S + k] + here
            kind_ref[3 * S + k] = kind_ref[3 * S + k] + here - late
            kind_ref[5 * S + k] = kind_ref[5 * S + k] + late

    hyper_arrive(0, 0)
    feats[2].wait_recv()
    feats[4].wait_recv()
    feats[5].start()
    feats[6].start()
    for j in range(1, n - 1):
        hyper_arrive(0, j)
        x_arrive(0, j - 1)
    for k in (0, 1, 3, 5, 6):
        feats[k].wait_recv()

    shift0 = small_ref[0:1]
    gain = small_ref[1:2]
    shift = small_ref[2:3]

    def norm(cols):
        h = dot(XTa[:, cols], XTa[:, pl.ds(2 * HALF, D)], TN) + shift0
        mean = jnp.mean(h, axis=-1, keepdims=True)
        cen = h - mean
        rstd = lax.rsqrt(jnp.mean(cen * cen, axis=-1, keepdims=True) + LN_EPS)
        nrm = cen * rstd
        return h, nrm, rstd, (nrm * gain + shift).astype(bf16)

    def support_rows(i):
        rows = pl.ds(pl.multiple_of(i * QUART, QUART), QUART)
        h, nrm, rstd, act = norm(rows)
        n1s_ref[rows] = nrm.astype(bf16)
        a1s_ref[rows] = act
        rs_ref[rows] = jnp.broadcast_to(rstd, (QUART, 128))

        @pl.when(i % 4 == f)
        def _():
            h0_ref[pl.ds(pl.multiple_of((i // 4) * 512, 512), QUART)] = h

    pl.loop(0, 4)(support_rows)
    send_own(1)
    pl.loop(4, 8)(support_rows)
    hyper_arrive(0, n - 1)
    if n > 1:
        x_arrive(0, n - 2)

    @pl.loop(0, 2)
    def _(t):
        rows = pl.ds(pl.multiple_of(t * QUART, QUART), QUART)
        h, nrm, rstd, act = norm(pl.ds(pl.multiple_of(wide + t * QUART, QUART), QUART))
        n1q_ref[rows] = nrm.astype(bf16)
        a1q_ref[rows] = act
        rq_ref[rows] = jnp.broadcast_to(rstd, (QUART, 128))
        h0_ref[pl.ds(pl.multiple_of(t * 512 + QUART, QUART), QUART)] = h

    XT_ref[...] = XTa[...]
    hyper_arrive(1, 0)
    x_arrive(0, n - 1)
    scale = (HEAD_DIM**-0.5) * LOG2E

    def assemble(p):
        for u in range(U):
            place, rank = pos[u] // S, pos[u] % S
            for k in range(2):
                W[pl.ds(u * BR, BR), pl.ds(p * 256 + k * 128, 128)] = Gs[p][k, place, rank]

    def project(p):
        cols = pl.ds(p * 256, 256)
        for t in range(2):
            sup = pl.multiple_of(t * HALF + f * QUART, QUART)
            wq = W[pl.ds(0, D), cols]
            q_s[pl.ds(t * 512, QUART), cols] = (dot(a1s_ref[pl.ds(sup, QUART)], wq) * scale).astype(bf16)
            q_s[pl.ds(t * 512 + QUART, QUART), cols] = (dot(a1q_ref[pl.ds(t * QUART, QUART)], wq) * scale).astype(bf16)

        @pl.loop(0, 4)
        def _(i):
            rows = pl.ds(pl.multiple_of(i * 512, 512), 512)
            a = a1s_ref[rows]
            k = dot(a, W[pl.ds(D, D), cols]).astype(bf16)
            k_s[rows, cols] = k
            kT_s[cols, rows] = k.T
            v = dot(a, W[pl.ds(2 * D, D), cols]).astype(bf16)
            v_s[rows, cols] = v
            vT_s[cols, rows] = v.T

    def ecopy(i):
        return pltpu.make_async_copy(ET_s.at[i], ET.at[i], esem.at[i])

    def head(h):
        hs = pl.ds(h * HEAD_DIM, HEAD_DIM)

        @pl.loop(0, 2)
        def _(t):
            i = t * HEADS + h
            ks = pl.ds(pl.multiple_of(t * HALF, HALF), HALF)
            qs = pl.ds(pl.multiple_of(t * 512, 512), 512)
            st = dot(k_s[ks, hs], q_s[qs, hs], NT)
            top = jnp.max(st, axis=0, keepdims=True)
            e = jnp.exp2(st - top)
            inv = 1.0 / jnp.sum(e, axis=0, keepdims=True)
            eb = e.astype(bf16)
            ET_s[i] = eb
            ecopy(i).start()
            linv[pl.ds(i, 1)] = inv
            ot = (dot(vT_s[hs, ks], eb) * inv).astype(bf16)
            OT_s[hs, qs] = ot
            O_s[qs, hs] = ot.T

    outs = []

    def ship(src, dst):
        copy = pltpu.make_async_copy(src, dst, osem.at[len(outs)])
        copy.start()
        outs.append(copy)

    for j in range(1, n - 1):
        hyper_arrive(1, j)
        x_arrive(1, j - 1)
    all_here(0)
    assemble(0)
    project(0)
    hyper_arrive(1, n - 1)
    if n > 1:
        x_arrive(1, n - 2)
    head(0)
    x_arrive(1, n - 1)
    head(1)
    all_here(1)
    assemble(1)
    ship(W, Wo)
    project(1)
    ship(q_s, qo)
    ship(kT_s, kTo)
    ship(v_s, vo)
    head(2)
    head(3)
    ship(O_s, Oo)
    ship(OT_s, OT)
    for copy in feats:
        copy.wait_send()
    all_sent(0)
    all_sent(1)
    for i in range(8):
        ecopy(i).wait()
    for copy in outs:
        copy.wait()


def gather_call(R, slots, features, masks, tmap, owners, emb, small):
    S, BR, W = slots.shape
    n = R.bit_length() - 1
    M = n * (n + 1) // 2
    dma = pltpu.SemaphoreType.DMA
    sem = dma((2, len(GROUPS), M))
    sd = jax.ShapeDtypeStruct
    V = pltpu.VMEM
    cols = 2 * HALF + D + 512
    half = V((2, R, S, BR, 128), bf16)
    return pl.pallas_call(
        functools.partial(gather_kernel, R),
        out_shape=(
            sd((2 * S,), jnp.int32), sd((7 * S,), jnp.int32), sd((4 * PADF, cols), bf16), sd((1024, D), f32),
            sd((2048, D), bf16), sd((512, D), bf16), sd((2048, D), bf16), sd((512, D), bf16),
            sd((2048, 128), f32), sd((512, 128), f32), sd((8, 512), f32),
            sd((12 * D, D), bf16), sd((1024, D), bf16), sd((D, 2048), bf16), sd((2048, D), bf16),
            sd((8, HALF, 512), bf16), sd((D, 1024), bf16), sd((1024, D), bf16),
        ),
        in_specs=[vmem(), vmem(), vmem(), smem(), smem(), vmem(), vmem()],
        out_specs=(smem(), smem()) + (vmem(),) * 9 + (anyspace(),) * 7,
        scratch_shapes=[
            pltpu.SMEM(owners.shape, jnp.int32), half, half, V((2, 2, S, BR, 128), bf16),
            V((PADF, 2 * HALF + D + 2048), bf16), V((4 * PADF, cols), bf16), V((PADF, 512), bf16),
            V((12 * D, D), bf16), V((1024, D), bf16), V((2048, D), bf16), V((D, 2048), bf16), V((2048, D), bf16),
            V((D, 2048), bf16), V((8, HALF, 512), bf16), V((D, 1024), bf16), V((1024, D), bf16),
            dma((2,)), dma((6,)), dma((8,)), dma((7,)), dma((7,)),
        ] + [sem] * 8,
        compiler_params=pltpu.CompilerParams(collective_id=0, has_side_effects=True, vmem_limit_bytes=VMEM_BYTES),
        name="gather",
    )(slots, features, masks, tmap, owners, emb, small)


def gelu_pair(u):
    den = 1.0 + (0.3275911 * math.sqrt(0.5)) * jnp.abs(u)
    t = pl.reciprocal(den, approx=True)
    t = t * (2.0 - den * t)
    ex = jnp.exp2((-0.5 * LOG2E) * (u * u))
    poly = t * (0.127414796 + t * (-0.142248368 + t * (0.7107068705 + t * (-0.7265760135 + t * 0.5307027145))))
    e = poly * ex
    phi = jnp.where(u >= 0, 1.0 - e, e)
    return u * phi, phi + u * ex * (1.0 / math.sqrt(2 * math.pi))


AFTER = {
    "fb0": (2, 3), "up": (2,), "mix": (3, 0, 1), "h01": (2,), "h10": (3,), "w0": (2, 0, 3), "h20": (4,),
    "h30": (1, 2, 0, 3), "b0": (4, 2, 1, 0), "b1": (5,), "b2": (3,), "b3": (2,), "b5": (4, 1), "b7": (0, 3), "b9": (4, 5, 1, 0),
}


def main_kernel(
    R, su, occ, linv, small, Wh, Oh, h0h, dYh, ETh, OTh, qh, kTh, vh, a1sh, a1qh, n1sh, n1qh, rsh, rqh, XTh,
    out, FIN, SM, EM, GI,
    W, O_s, y_s, dY, ETb, OT, qs, kT, a1q, n1s, n1q, rs, rq, XT,
    a2_s, G_s, dU_s, Dp, sg, eg, GT, S, RC, RX, RH, AG0, AG1, AGL, SY, RY, SEL, PK, RK, GC, XS, XR,
    lsem, esem, osem, ss, sr, ys, yr, fs, fr, ps, pr, gs, gr,
):
    f = lax.axis_index("feat")
    r = lax.axis_index("rows")
    x = f // 2
    c = f % 2
    n = R.bit_length() - 1
    BH = S.shape[4]
    per = D // (2 * BH)
    core_id = (f ^ 1, r)
    x_id = (f ^ 2, r)
    row_id = [(f, r ^ (1 << j)) for j in range(n)]
    peers = [core_id, x_id] + row_id
    bar = greet(peers)

    loads = {}

    def load(name, src, dst):
        loads[name] = pltpu.make_async_copy(src, dst, lsem.at[len(loads)])
        loads[name].start()

    def rows_w(i):
        return pl.ds(i * D, D)

    load("O", Oh, O_s)
    load("h0", h0h, y_s)
    for i in (3, 4, 8, 5, 9, 6, 10, 7, 11):
        load(i, Wh.at[rows_w(i)], W.at[rows_w(i)])
    load("dY", dYh, dY)
    load("OT", OTh, OT)
    load("q", qh, qs)
    load("kT", kTh, kT)

    def ecopy(h, t):
        k = (h % 2) * 2 + t
        return pltpu.make_async_copy(ETh.at[t * HEADS + h], ETb.at[k], esem.at[k])

    for h in range(2):
        for t in range(2):
            ecopy(h, t).start()
    load("a1q", a1qh, a1q)
    load("n1s", n1sh, n1s)
    load("n1q", n1qh, n1q)
    load("rs", rsh, rs)
    load("rq", rqh, rq)
    load("XT", XTh, XT)
    for i in range(3):
        load(i, Wh.at[rows_w(i)], W.at[rows_w(i)])
    pl.semaphore_wait(bar, len(peers))

    bits = [(r >> j) & 1 for j in range(n)]
    base = [0]
    for j in range(n):
        base.append(base[j] + bits[j] * (R >> (j + 1)))

    def core_copy(g):
        return remote(S.at[1 - c, :, g], RC.at[:, g], ss.at[g, 0], sr.at[g, 0], core_id)

    def x_copy(g):
        return remote(S.at[c, 1 - x, g], RX.at[g], ss.at[g, 1], sr.at[g, 1], x_id)

    def rs_copy(g, j):
        half = R >> (j + 1)
        away = base[j] + (1 - bits[j]) * half
        off = R - (R >> j)
        return remote(
            S.at[c, x, g, pl.ds(away, half)], RH.at[g, pl.ds(off, half)],
            ss.at[g, 2 + j], sr.at[g, 2 + j], row_id[j],
        )

    def swap_copy(g):
        span = pl.ds(base[n - 1], 2)
        return remote(S.at[c, x, g, span], RH.at[g, pl.ds(R - 2, 2)], ss.at[g, 1 + n], sr.at[g, 1 + n], row_id[n - 1])

    def total_of(g):
        return AGL if g == 5 else AG1.at[g // 2] if g % 2 else AG0.at[(g // 2 + 1) % 3]

    def ag_copy(g, j):
        ref = total_of(g).at[pl.ds(base[j + 1] - base[1], R >> (j + 1))]
        return remote(ref, ref, ss.at[g, 2 + n + j], sr.at[g, 2 + n + j], row_id[j])

    def add(a, b):
        return (a.astype(f32) + b.astype(f32)).astype(bf16)

    def step(g, stage):
        if stage == 0:
            core_copy(g).wait_recv()
            S[c, 1 - x, g] = add(S[c, 1 - x, g], RC[1 - x, g])
            x_copy(g).start()
            S[c, x, g] = add(S[c, x, g], RC[x, g])
        elif stage == 1:
            x_copy(g).wait_recv()
            S[c, x, g] = add(S[c, x, g], RX[g])
            rs_copy(g, 0).start()
        elif stage < 1 + n:
            j = stage - 2
            half = R >> (j + 1)
            off = R - (R >> j)
            rs_copy(g, j).wait_recv()
            keep = pl.ds(base[j + 1], half)
            S[c, x, g, keep] = add(S[c, x, g, keep], RH[g, pl.ds(off, half)])
            if j < n - 2:
                rs_copy(g, j + 1).start()
            else:
                swap_copy(g).start()
        elif stage == 1 + n:
            swap_copy(g).wait_recv()
            total_of(g)[pl.ds(base[n - 1] - base[1], 2)] = add(S[c, x, g, pl.ds(base[n - 1], 2)], RH[g, pl.ds(R - 2, 2)])
            if n > 2:
                ag_copy(g, n - 2).start()
        else:
            j = 2 * n - stage
            ag_copy(g, j).wait_recv()
            if j > 1:
                ag_copy(g, j - 1).start()

    def select(m, who):
        picked = []
        for s in range(4):
            u = su[who * 4 + s]
            p = lax.rem(u, R // 2)
            q = lax.div(u, R)
            k = who * 4 + s
            if m == 0:
                picked.append(AG0[q, p].astype(f32) * occ[4 + k].astype(f32))
            else:
                picked.append(AG1[lax.max(q - 1, 0), p].astype(f32) * occ[12 + k].astype(f32) + AGL[p].astype(f32) * occ[20 + k].astype(f32))
        return picked

    def y_copy(m):
        return remote(SY.at[m], RY.at[m], ys.at[m], yr.at[m], row_id[0])

    def fin(m, k):
        if k == 3:
            return pltpu.make_async_copy(SEL.at[m], FIN.at[m, f], osem.at[1 + m])
        src, at = (FIN.at[m, f ^ 2], f ^ 2) if k == 2 else (SEL.at[m], f)
        return remote(src, FIN.at[m, at], fs.at[m, k], fr.at[m, k], x_id if k == 1 else core_id)

    def fin_step(m, stage):
        if stage == 0:
            for s, value in enumerate(select(m, 1)):
                SY[m, s] = value.astype(bf16)
            y_copy(m).start()
            for s, value in enumerate(select(m, 0)):
                SEL[m, s] = value.astype(bf16)
        elif stage == 1:
            y_copy(m).wait_recv()
            SEL[m] = add(SEL[m], RY[m])
            for k in (1, 0, 3):
                fin(m, k).start()
        else:
            fin(m, 1).wait_recv()
            fin(m, 2).start()

    last = 2 * n
    done = [0] * 6
    ended = [0, 0]

    def tick(g):
        if done[g] < last:
            step(g, done[g])
            done[g] += 1

    def finish(m):
        if ended[m] < 3 and all(done[g] == last for g in (m, 2 + m, 4 + m)):
            fin_step(m, ended[m])
            ended[m] += 1

    def after(piece):
        for g in AFTER.get(piece, ()):
            tick(g)

    def put(g0, i, val):
        for k in range(val.shape[1] // 128):
            piece = val[:, k * 128:(k + 1) * 128].reshape(per, 2, BH, 128)
            for h in range(2):
                S[k % 2, h, g0 + k // 2, pl.ds(i * per, per)] = piece[:, h]

    gain2 = small[3:4]
    shift2 = small[4:5]
    RB = 256

    def norm2(y1):
        cen = y1 - jnp.mean(y1, axis=-1, keepdims=True)
        rstd = lax.rsqrt(jnp.mean(cen * cen, axis=-1, keepdims=True) + LN_EPS)
        return cen * rstd, rstd

    loads["O"].wait()
    loads["h0"].wait()
    loads[3].wait()

    @pl.loop(0, 1024 // RB)
    def _(i):
        rows = pl.ds(pl.multiple_of(i * RB, RB), RB)
        y1 = y_s[rows] + dot(O_s[rows], W[rows_w(3)])
        y_s[rows] = y1
        n2, _ = norm2(y1)
        a2 = (n2 * gain2 + shift2).astype(bf16)
        a2_s[rows] = a2
        acc = y1 + small[5:6]
        for j in range(4):
            @pl.when(i == 0)
            def _():
                loads[4 + j].wait()
                loads[8 + j].wait()
            gl, gp = gelu_pair(dot(a2, W[rows_w(4 + j)]) + small[6 + j:7 + j])
            gb = gl.astype(bf16)
            G_s[j, rows] = gb
            dU_s[j, rows] = gp.astype(bf16)
            acc = acc + dot(gb, W[rows_w(8 + j)])
        O_s[rows] = acc.astype(bf16)

    ship_out = pltpu.make_async_copy(O_s, out, osem.at[0])
    ship_out.start()
    loads["dY"].wait()

    @pl.loop(0, 4)
    def _(j):
        put(2, j, dot(G_s[j], dY[...], TN).astype(bf16))

    core_copy(2).start()
    core_copy(3).start()

    sg[...] = jnp.zeros_like(sg)

    def backward_rows(i):
        rows = pl.ds(i * RB, RB)
        dy = dY[rows]
        da2 = jnp.zeros((RB, D), f32)
        for j in range(4):
            du = (dot(dy, W[rows_w(8 + j)], NT) * dU_s[j, rows].astype(f32)).astype(bf16)
            dU_s[j, rows] = du
            sg[6 + j:7 + j] += jnp.sum(du.astype(f32), axis=0, keepdims=True)
            da2 = da2 + dot(du, W[rows_w(4 + j)], NT)
        n2, rstd = norm2(y_s[rows])
        dyf = dy.astype(f32)
        sg[3:4] += jnp.sum(da2 * n2, axis=0, keepdims=True)
        sg[4:5] += jnp.sum(da2, axis=0, keepdims=True)
        sg[5:6] += jnp.sum(dyf, axis=0, keepdims=True)
        cc = da2 * gain2
        m1 = jnp.mean(cc, axis=-1, keepdims=True)
        m2 = jnp.mean(cc * n2, axis=-1, keepdims=True)
        y_s[rows] = dyf + rstd * (cc - m1 - n2 * m2)

    for i in range(1024 // RB):
        backward_rows(i)
        after("fb%d" % i)
    vs = W.at[pl.ds(4 * D, 4 * D)]
    a1s = W.at[pl.ds(8 * D, 4 * D)]
    load("v", vh, vs)
    load("a1s", a1sh, a1s)

    @pl.loop(0, 4)
    def _(j):
        put(0, j, dot(a2_s[...], dU_s[j], TN).astype(bf16))

    core_copy(0).start()
    core_copy(1).start()
    after("up")

    scale = HEAD_DIM**-0.5
    for i in range(2):
        dU_s[1, pl.ds(i * 512, 512)] = y_s[pl.ds(i * 512, 512)].astype(bf16)
    for name in ("OT", "v", "q", "kT", "a1s", "a1q"):
        loads[name].wait()
    put(4, 3, dot(OT[...], dU_s[1]).astype(bf16))

    @pl.loop(0, 2)
    def _(t):
        cols = pl.ds(pl.multiple_of(t * 512, 512), 512)
        whole = dot(W[rows_w(3)], dU_s[1, cols], NT)
        for h in range(HEADS):
            rows = pl.ds(h * HEAD_DIM, HEAD_DIM)
            d = whole[h * HEAD_DIM:(h + 1) * HEAD_DIM] * linv[pl.ds(t * HEADS + h, 1)]
            Dp[pl.ds(t * HEADS + h, 1)] = jnp.sum(d * OT[rows, cols].astype(f32), axis=0, keepdims=True)
            dU_s[2, pl.ds(pl.multiple_of(t * 512 + h * HEAD_DIM, HEAD_DIM), HEAD_DIM)] = d.astype(bf16)

    after("mix")

    def heads(h):
        hs = pl.ds(h * HEAD_DIM, HEAD_DIM)
        for t in range(2):
            ecopy(h, t).wait()

        @pl.loop(0, 2)
        def _(t):
            i = t * HEADS + h
            ksl = pl.ds(pl.multiple_of(t * HALF, HALF), HALF)
            qsl = pl.ds(pl.multiple_of(t * 512, 512), 512)
            do = dU_s[2, pl.ds(pl.multiple_of(t * 512 + h * HEAD_DIM, HEAD_DIM), HEAD_DIM)]
            dp = dot(vs[ksl, hs], do)
            e = ETb[(h % 2) * 2 + t]
            ds = (e.astype(f32) * (dp - Dp[pl.ds(i, 1)])).astype(bf16)
            G_s[2 + t, :, hs] = dot(e, do, NT).astype(bf16)
            G_s[t, :, hs] = (dot(ds, qs[qsl, hs]) * (1.0 / LOG2E)).astype(bf16)
            dqT = (dot(kT[hs, ksl], ds) * scale).astype(bf16)
            dU_s[0, qsl, hs] = dqT.T

        for t in range(2):
            if h + 2 < HEADS:
                ecopy(h + 2, t).start()
            after("h%d%d" % (h, t))

    def weight_grads(m):
        cols = pl.ds(m * 256, 256)
        acc = jnp.zeros((D, 256), f32)
        for t in range(2):
            sup = pl.multiple_of(t * HALF + f * QUART, QUART)
            acc += dot(a1s[pl.ds(sup, QUART)], dU_s[0, pl.ds(t * 512, QUART), cols], TN)
            acc += dot(a1q[pl.ds(t * QUART, QUART)], dU_s[0, pl.ds(t * 512 + QUART, QUART), cols], TN)
        put(4 + m, 0, acc.astype(bf16))
        for k in range(2):
            total = dot(a1s[pl.ds(0, HALF)], G_s[2 * k, :, cols], TN) + dot(a1s[pl.ds(HALF, HALF)], G_s[2 * k + 1, :, cols], TN)
            put(4 + m, 1 + k, total.astype(bf16))

    for m in range(2):
        heads(2 * m)
        heads(2 * m + 1)
        weight_grads(m)
        core_copy(4 + m).start()
        after("w%d" % m)

    eg[...] = jnp.zeros_like(eg)
    gain1 = small[1:2]
    emb_cols = pl.ds(2 * HALF, D)
    for name in ("n1s", "n1q", "rs", "rq", "XT", 0, 1, 2):
        loads[name].wait()

    def back(da, nrm, rstd, extra, cols, out_cols):
        sg[1:2] += jnp.sum(da * nrm, axis=0, keepdims=True)
        sg[2:3] += jnp.sum(da, axis=0, keepdims=True)
        cc = da * gain1
        m1 = jnp.mean(cc, axis=-1, keepdims=True)
        m2 = jnp.mean(cc * nrm, axis=-1, keepdims=True)
        wide = jnp.concatenate([rstd] * 4, axis=1)
        dh = wide * (cc - m1 - nrm * m2)
        if extra is not None:
            dh = dh + extra
        sg[0:1] += jnp.sum(dh, axis=0, keepdims=True)
        de = dh.astype(bf16)
        part = dot(XT[:, cols], de)
        back_in = dot(XT[:, emb_cols], de, NT).astype(bf16)
        for k in range(4):
            eg[k] += part[k * PADF:(k + 1) * PADF]
            GT[k % 2, k // 2, :, out_cols] = back_in[k * PADF:(k + 1) * PADF]

    def below(t):
        q0 = t * 512
        wq, wk, wv = W[rows_w(0)], W[rows_w(1)], W[rows_w(2)]
        da = dot(dU_s[0, pl.ds(q0 + QUART, QUART)], wq, NT)
        p0 = pl.ds(t * QUART, QUART)
        back(
            da, n1q[p0].astype(f32), rq[p0], y_s[pl.ds(q0 + QUART, QUART)],
            pl.ds(2 * HALF + D + t * QUART, QUART), pl.ds(2 * HALF + t * QUART, QUART),
        )
        after("b%d" % (5 * t))
        for b in range(4):
            at = pl.ds(pl.multiple_of(((f + b) % 4) * QUART, QUART), QUART)
            rows = pl.ds(pl.multiple_of(t * HALF + ((f + b) % 4) * QUART, QUART), QUART)
            da = dot(G_s[t, at], wk, NT) + dot(G_s[2 + t, at], wv, NT)
            extra = None
            if b == 0:
                da = da + dot(dU_s[0, pl.ds(q0, QUART)], wq, NT)
                extra = y_s[pl.ds(q0, QUART)]
            back(da, n1s[rows].astype(f32), rs[rows], extra, rows, rows)
            if 5 * t + b < 8:
                after("b%d" % (5 * t + b + 1))

    below(0)
    below(1)

    small_rows = pl.ds(0, 16)
    PK[0, small_rows] = sg[...]
    for k in range(2):
        PK[0, pl.ds(16 + k * PADF, PADF)] = eg[2 * k + 1 - c]

    def pk_copy(i):
        rows = pl.ds(0, 80 if i == 0 else 48)
        dev = core_id if i == 0 else x_id if i == 1 else row_id[i - 2]
        return remote(PK.at[i, rows], RK.at[i, rows], ps.at[i], pr.at[i], dev)

    def pk_step(i):
        pk_copy(i).wait_recv()
        if i == 0:
            PK[1, small_rows] = PK[0, small_rows] + RK[0, small_rows]
            own = [eg[2 * k + c] + RK[0, pl.ds(16 + k * PADF, PADF)] for k in range(2)]
            PK[1, pl.ds(16, PADF)] = jnp.where(x == 0, own[1], own[0])
            PK[1, pl.ds(48, PADF)] = jnp.where(x == 0, own[0], own[1])
            pk_copy(1).start()
        else:
            old = PK[1, pl.ds(48, PADF)] if i == 1 else PK[i, pl.ds(16, PADF)]
            a = PK[i, small_rows] + RK[i, small_rows]
            b = old + RK[i, pl.ds(16, PADF)]
            if i < n + 1:
                PK[i + 1, small_rows] = a
                PK[i + 1, pl.ds(16, PADF)] = b
                pk_copy(i + 1).start()
            else:
                SM[...] = a
                EM[...] = b

    pk_copy(0).start()
    gt1 = remote(GT.at[1 - c], GC, gs.at[0], gr.at[0], core_id)
    gt1.start()
    sup = pl.ds(0, 2 * HALF)
    que = pl.ds(2 * HALF, 512)

    def que_of(k):
        return pl.ds(pl.multiple_of(2 * HALF + k * 512, 512), 512)

    gt2 = remote(XS, XR, gs.at[1], gr.at[1], x_id)
    after("b9")
    pk_step(0)
    gt1.wait_recv()
    XS[:, sup] = add(GT[c, 1 - x, :, sup], GC[1 - x, :, sup])
    XS[:, que_of(c)] = GT[c, 1 - x, :, que]
    XS[:, que_of(1 - c)] = GC[1 - x, :, que]
    gt2.start()
    next_pk = 1
    while min(done) < last:
        for g in (4, 5, 2, 3, 1, 0):
            tick(g)
        finish(0)
        if next_pk < n + 2:
            pk_step(next_pk)
            next_pk += 1
    finish(1)
    finish(0)
    for i in range(next_pk, n + 2):
        pk_step(i)
    gt2.wait_recv()
    GI[:, sup] = (
        GT[c, x, :, sup].astype(f32) + GC[x, :, sup].astype(f32) + XR[:, sup].astype(f32)
    ).astype(bf16)
    GI[:, que_of(f)] = GT[c, x, :, que]
    GI[:, que_of(f ^ 1)] = GC[x, :, que]
    for k in range(2):
        GI[:, que_of(2 * (1 - x) + k)] = XR[:, pl.ds(2 * HALF + k * 512, 512)]
    while min(ended) < 3:
        finish(0)
        finish(1)
    for m in range(2):
        y_copy(m).wait_send()
        fin(m, 0).wait()
        fin(m, 1).wait_send()
        fin(m, 2).wait()
        fin(m, 3).wait()
    for g in range(6):
        core_copy(g).wait_send()
        x_copy(g).wait_send()
        swap_copy(g).wait_send()
        for j in range(n - 1):
            rs_copy(g, j).wait_send()
        for j in range(1, n - 1):
            ag_copy(g, j).wait_send()
    for i in range(n + 2):
        pk_copy(i).wait_send()
    gt1.wait_send()
    gt2.wait_send()
    ship_out.wait()


def main_call(R, su, occ, linv, small, W, O, h0, dY, ET, OT, q, kT, v, a1s, a1q, n1s, n1q, rs, rq, XT):
    BH = 12 * D // (3 * R) // 2
    n = R.bit_length() - 1
    sd = jax.ShapeDtypeStruct
    V = pltpu.VMEM
    dma = pltpu.SemaphoreType.DMA
    blk = (R, BH, 128)
    like = lambda a: V(a.shape, a.dtype)
    return pl.pallas_call(
        functools.partial(main_kernel, R),
        out_shape=(sd((1024, D), bf16), sd((2, 4, 4, BH, 128), bf16), sd((16, D), f32), sd((PADF, D), f32), sd((PADF, 4096), bf16)),
        in_specs=[smem(), smem(), vmem(), vmem()] + [anyspace()] * 16,
        out_specs=(anyspace(), anyspace(), vmem(), vmem(), vmem()),
        scratch_shapes=[
            like(W), like(O), like(h0), like(dY), V((4, HALF, 512), bf16), like(OT), like(q), like(kT),
            like(a1q), like(n1s), like(n1q), like(rs), like(rq), like(XT),
            V((1024, D), bf16), V((4, 1024, 512), bf16), V((4, 1024, 512), bf16), V((8, 512), f32), V((16, D), f32),
            V((4, PADF, D), f32), V((2, 2, PADF, 2560), bf16),
            V((2, 2, 6) + blk, bf16), V((2, 6) + blk, bf16), V((6,) + blk, bf16), V((6,) + blk, bf16), V((3, R // 2, BH, 128), bf16), V((2, R // 2, BH, 128), bf16), V((R // 2, BH, 128), bf16),
            V((2, 4, BH, 128), bf16), V((2, 4, BH, 128), bf16), V((2, 4, BH, 128), bf16), V((n + 2, 80, D), f32), V((n + 2, 80, D), f32),
            V((2, PADF, 2560), bf16), V((PADF, 3072), bf16), V((PADF, 3072), bf16),
            dma((26,)), dma((4,)), dma((3,)), dma((6, 2 + 2 * n)), dma((6, 2 + 2 * n)), dma((2,)), dma((2,)), dma((2, 3)), dma((2, 3)),
            dma((n + 2,)), dma((n + 2,)), dma((2,)), dma((2,)),
        ],
        compiler_params=pltpu.CompilerParams(collective_id=1, has_side_effects=True, vmem_limit_bytes=VMEM_BYTES),
        name="main",
    )(su, occ, linv, small, W, O, h0, dY, ET, OT, q, kT, v, a1s, a1q, n1s, n1q, rs, rq, XT)


def adamw(weight, grad, first, second, rate):
    first_new = BETA_FIRST * first + (1.0 - BETA_FIRST) * grad
    second_new = BETA_SECOND * second + (1.0 - BETA_SECOND) * grad * grad
    first_hat = first_new * (1.0 / (1.0 - BETA_FIRST**STEP))
    second_hat = second_new * (1.0 / (1.0 - BETA_SECOND**STEP))
    weight_new = weight - rate * (first_hat / (jnp.sqrt(second_hat) + ADAM_EPS) + DECAY * weight)
    return (first_new, second_new, weight_new)


def update_kernel(
    occ, tmap, FIN, w, m, v, SM, sw, sm, sv, EM, ew, em, ev, GI, masks, lo,
    g_o, m_o, v_o, w_o, wc_o, eg_o, em_o, ev_o, ew_o, ec_o, sg_o, sm_o, sv_o, sw_o, gi_o, lo_o,
):
    s = pl.program_id(0)
    BH = FIN.shape[3]
    for slot in range(2):
        keep = occ[2 * s + slot].astype(f32)
        for f in range(4):
            rows = pl.ds((f // 2) * BH, BH)
            for k in range(2):
                cols = pl.ds(k * 256 + (f % 2) * 128, 128)
                g = FIN[k, f, slot].astype(f32)
                a, b, d = adamw(w[slot, rows, cols], g, m[slot, rows, cols], v[slot, rows, cols], RATE_MATRIX)
                g_o[slot, rows, cols] = g * keep
                m_o[slot, rows, cols] = a * keep
                v_o[slot, rows, cols] = b * keep
                d = d * keep
                w_o[slot, rows, cols] = d
                wc_o[slot, rows, cols] = d.astype(bf16)

    @pl.when(s == 0)
    def _():
        g = SM[0:10]
        a, b, d = adamw(sw[...], g, sm[...], sv[...], RATE_SMALL)
        sg_o[...] = g
        sm_o[...] = a
        sv_o[...] = b
        sw_o[...] = d
        nf = ew.shape[0]
        g = EM[pl.ds(0, nf)]
        a, b, d = adamw(ew[...], g, em[...], ev[...], RATE_EMBED)
        eg_o[...] = g
        em_o[...] = a
        ev_o[...] = b
        ew_o[...] = d
        ec_o[...] = d.astype(bf16)

    nf = gi_o.shape[1]
    t = s
    keep_in = mask_column(masks, tmap[t])
    cols = pl.ds(pl.multiple_of(t * HALF, HALF), HALF)
    gi_o[t, :, 0, :] = (GI[pl.ds(0, nf), cols].astype(f32) * keep_in).astype(bf16)
    for k in range(4):
        cols = pl.ds(pl.multiple_of(2 * HALF + k * 512 + t * QUART, QUART), QUART)
        gi_o[t, :, 1, pl.ds(k * QUART, QUART)] = (GI[pl.ds(0, nf), cols].astype(f32) * keep_in).astype(bf16)

    lo_o[...] = lo[...]


def update_call(occ, tmap, FIN, w, m, v, SM, sw, sm, sv, EM, ew, em, ev, GI, masks, lo):
    S, BR, W = w.shape
    nf = ew.shape[0]
    sd = jax.ShapeDtypeStruct
    blk = pl.BlockSpec((2, BR, W), lambda s: (s, 0, 0))
    whole = lambda a: pl.BlockSpec(a.shape, lambda s: (0,) * len(a.shape))
    ins = [smem(), smem(), pl.BlockSpec((2, 4, 2, BR // 2, 128), lambda s: (0, 0, s, 0, 0)), blk, blk, blk]
    ins += [whole(a) for a in (SM, sw, sm, sv, EM, ew, em, ev, GI, masks)] + [pl.BlockSpec((2048 // S, D), lambda s: (s, 0))]
    big = sd((S, BR, W), f32)
    small = sd((10, D), f32)
    e = sd((nf, D), f32)
    outs = [big, big, big, big, sd((S, BR, W), bf16), e, e, e, e, sd((nf, D), bf16), small, small, small, small, sd((2, nf, 2, HALF), bf16), sd(lo.shape, lo.dtype)]
    specs = [blk] * 5 + [whole(a) for a in outs[5:14]] + [whole(outs[14]), pl.BlockSpec((2048 // S, D), lambda s: (s, 0))]
    return pl.pallas_call(
        update_kernel, out_shape=tuple(outs), grid=(S // 2,), in_specs=ins, out_specs=tuple(specs),
        compiler_params=pltpu.CompilerParams(vmem_limit_bytes=VMEM_BYTES), name="update",
    )(occ, tmap, FIN, w, m, v, SM, sw, sm, sv, EM, ew, em, ev, GI, masks, lo)


def body(
    features, feature_masks, table_map, owners, out_grad, weight_slots, moment1_slots, moment2_slots,
    emb_weight, emb_moment1, emb_moment2, small_weight, small_moment1, small_moment2,
):
    width = weight_slots.shape[2]
    R = lax.axis_size("rows")
    slot_unit, kinds, XT, h0o, a1s, a1q, n1s, n1q, rs, rq, linv, W, q, kT, v, ET, OT, O = gather_call(
        R, weight_slots, features.transpose(0, 3, 1, 2), feature_masks, table_map, owners, emb_weight, small_weight
    )
    dY = out_grad.reshape(1024, width)
    out, FIN, SM, EM, GI = main_call(
        R, slot_unit, kinds, linv, small_weight, W, O, h0o, dY, ET, OT, q, kT, v, a1s, a1q, n1s, n1q, rs, rq, XT
    )
    (
        g_slots, m_slots, v_slots, w_slots, w_copy, e_grad, e_m, e_v, e_w, e_copy, s_grad, s_m, s_v, s_w, grad_inputs, out,
    ) = update_call(
        kinds, table_map, FIN, weight_slots, moment1_slots, moment2_slots, SM, small_weight, small_moment1,
        small_moment2, EM, emb_weight, emb_moment1, emb_moment2, GI, feature_masks, out,
    )
    grad_inputs = grad_inputs.transpose(0, 2, 3, 1)
    return (
        out.reshape(out_grad.shape), grad_inputs, g_slots, m_slots, v_slots, w_slots, w_copy,
        e_grad, e_m, e_v, e_w, e_copy, s_grad, s_m, s_v, s_w,
    )


def solution(mesh):
    rows3 = P("rows", None, None)
    feat2 = P("feat", None)
    in_specs = (
        P("rows", None, None, "feat"), P(None, "feat"), P("rows"), P(), P("rows", None, "feat", None),
        rows3, rows3, rows3, feat2, feat2, feat2, P(), P(), P(),
    )
    out_specs = (
        P("rows", None, "feat", None), P("rows", None, None, "feat"), rows3, rows3, rows3, rows3, rows3,
        feat2, feat2, feat2, feat2, feat2, P(), P(), P(), P(),
    )
    return jax.shard_map(body, mesh=mesh, in_specs=in_specs, out_specs=out_specs, check_vma=False)
```
